32 devices in a mesh: fsdp: 8 (over y, x, core), tensor: 4 (over z).
Axes of the slice: x: 2, y: 2, z: 4, core: 2. Of those that a mesh axis runs over, the one named last changes fastest.
Arguments:
- images: bfloat16 [8, 576, 768], P('fsdp'), may hold values from -6 to 6
- cotangent: bfloat16 [8, 576, 768], P('fsdp'), may hold values from -6 to 6
- qkv_weight: float32 [3, 768, 768], P(None, 'fsdp', 'tensor'), may hold values from -0.21875 to 0.21875
- out_weight: float32 [768, 768], P('tensor', 'fsdp'), may hold values from -0.875 to 0.875
- up_weight: float32 [768, 3072], P('fsdp', 'tensor'), may hold values from -0.21875 to 0.21875
- down_weight: float32 [3072, 768], P('tensor', 'fsdp'), may hold values from -0.109375 to 0.109375
- vectors: float32 [8, 768], P(None, ('fsdp', 'tensor')), may hold values from -1.2 to 1.8, as said below
- up_bias: float32 [3072], P(('fsdp', 'tensor')), may hold values from -1.8 to 1.8
- qkv_first: float32 [3, 768, 768], P(None, 'fsdp', 'tensor'), may hold values from -31.3616 to 31.3616
- qkv_second: float32 [3, 768, 768], P(None, 'fsdp', 'tensor'), may hold values from 1.12896 to 18.06336
- out_first: float32 [768, 768], P('tensor', 'fsdp'), may hold values from -8.960457 to 8.960457
- out_second: float32 [768, 768], P('tensor', 'fsdp'), may hold values from 0.09216 to 1.47456
- up_first: float32 [768, 3072], P('fsdp', 'tensor'), may hold values from -13.440685 to 13.440685
- up_second: float32 [768, 3072], P('fsdp', 'tensor'), may hold values from 0.20736 to 3.31776
- down_first: float32 [3072, 768], P('tensor', 'fsdp'), may hold values from -29.121485 to 29.121485
- down_second: float32 [3072, 768], P('tensor', 'fsdp'), may hold values from 0.96768 to 15.48288
- vector_first: float32 [8, 768], P(None, ('fsdp', 'tensor')), may hold values from -44.802284 to 44.802284
- vector_second: float32 [8, 768], P(None, ('fsdp', 'tensor')), may hold values from 2.304 to 36.864
- bias_first: float32 [3072], P(('fsdp', 'tensor')), may hold values from -13.440685 to 13.440685
- bias_second: float32 [3072], P(('fsdp', 'tensor')), may hold values from 0.20736 to 3.31776
Outputs:
- output: bfloat16 [8, 576, 768], P('fsdp', 'tensor')
- input_grad: float32 [8, 576, 768], P('fsdp', 'tensor')
- qkv_new: float32 [3, 768, 768], P(None, 'fsdp', 'tensor')
- qkv_first_new: float32 [3, 768, 768], P(None, 'fsdp', 'tensor')
- qkv_second_new: float32 [3, 768, 768], P(None, 'fsdp', 'tensor')
- out_new: float32 [768, 768], P('tensor', 'fsdp')
- out_first_new: float32 [768, 768], P('tensor', 'fsdp')
- out_second_new: float32 [768, 768], P('tensor', 'fsdp')
- up_new: float32 [768, 3072], P('fsdp', 'tensor')
- up_first_new: float32 [768, 3072], P('fsdp', 'tensor')
- up_second_new: float32 [768, 3072], P('fsdp', 'tensor')
- down_new: float32 [3072, 768], P('tensor', 'fsdp')
- down_first_new: float32 [3072, 768], P('tensor', 'fsdp')
- down_second_new: float32 [3072, 768], P('tensor', 'fsdp')
- vectors_new: float32 [8, 768], P(None, ('fsdp', 'tensor'))
- vector_first_new: float32 [8, 768], P(None, ('fsdp', 'tensor'))
- vector_second_new: float32 [8, 768], P(None, ('fsdp', 'tensor'))
- bias_new: float32 [3072], P(('fsdp', 'tensor'))
- bias_first_new: float32 [3072], P(('fsdp', 'tensor'))
- bias_second_new: float32 [3072], P(('fsdp', 'tensor'))
The draws below stay inside these ranges and needn't reach their ends.
Inputs may be any that keep to these rules, and one draw needn't show every extreme that they name: `vectors`: rows 0 and 2 are gains about 1, the other rows biases about 0.
All inputs are finite; a program needn't handle non-finite values.
Results may differ from the reference program's by a relative error of at most 0.013.
Values may be sent and summed in bfloat16 or wider, within the bound.
No kernel may reach another device: no remote copies, remote signals or barrier semaphores. Data moves between devices by JAX's collectives and lax.ppermute only.
A program may use at most 128 MiB of HBM per device.

```python
import math
import jax
import jax.numpy as jnp
from jax import lax

D = 768
HEADS = 12
HD = 64
FF = 3072
SEQ = 576
STEP = 10
IMAGES = 8


def draw_vectors(key, part):
    key = jax.random.fold_in(key, 11)
    rough_noise = jnp.clip(jax.random.normal(key, (8, D), jnp.float32), -4.0, 4.0)
    row_index = jnp.arange(8)[:, None]
    gain_rows = (row_index == 0) | (row_index == 2)
    return jnp.where(gain_rows, 1.0 + 0.2 * rough_noise, 0.3 * rough_noise)


def steps_of(stream_key, dims, cuts, least, top_value):
    def one(axis_at, parts):
        draws = jax.random.uniform(jax.random.fold_in(jax.random.fold_in(stream_key, 6), axis_at), (parts,), jnp.float32, least / len(cuts), top_value / len(cuts))
        return jnp.repeat(jnp.exp(draws), dims[axis_at] // parts).reshape((-1,) + (1,) * (len(dims) - axis_at - 1))

    gain = one(*cuts[0])
    for cut in cuts[1:]:
        gain = gain * one(*cut)
    return gain


def gaussian(key, extent, deviation, bound, cuts=(), dtype=jnp.bfloat16):
    entries = deviation * jax.random.normal(key, extent, jnp.float32)
    if cuts:
        entries = entries * steps_of(key, extent, cuts, -0.22, 0.18)
    return jnp.clip(entries, -bound, bound).astype(dtype)


def setup_inputs(seed: int = 0) -> dict:
    streams_of = jax.random.split(jax.random.key(seed), 21)
    images = gaussian(streams_of[0], (IMAGES, SEQ, D), 1.0, 6.0, ((0, 8),))
    cotangent = gaussian(streams_of[1], (IMAGES, SEQ, D), 1.0, 6.0, ((0, 8),))
    qkv_weight = gaussian(streams_of[2], (3, D, D), D ** -0.5, 0.21875, ((1, 8), (2, 4)), jnp.float32)
    out_weight = gaussian(streams_of[3], (D, D), (D // 16) ** -0.5, 0.875, ((0, 4), (1, 8)), jnp.float32)
    up_weight = gaussian(streams_of[4], (D, FF), D ** -0.5, 0.21875, ((0, 8), (1, 4)), jnp.float32)
    down_weight = gaussian(streams_of[5], (FF, D), FF ** -0.5, 0.109375, ((0, 4), (1, 8)), jnp.float32)
    vectors = draw_vectors(jax.random.fold_in(streams_of[20], 71), 0)
    up_bias = gaussian(streams_of[7], (FF,), 0.3, 1.8, ((0, 32),), jnp.float32)
    qkv_first = gaussian(streams_of[8], (3, D, D), (0.11 * 0.7 * (IMAGES * SEQ) ** 0.5), 31.3616, ((1, 8), (2, 4)), jnp.float32)
    qkv_second = jnp.clip(jnp.exp(math.log(18.06336) - 2.7725887 * jax.random.uniform(streams_of[9], (3, D, D), jnp.float32) ** steps_of(streams_of[9], (3, D, D), ((1, 8), (2, 4)), -0.2, 0.2)), 1.12896, 18.06336)
    out_first = gaussian(streams_of[10], (D, D), (0.11 * 0.2 * (IMAGES * SEQ) ** 0.5), 8.960457, ((0, 4), (1, 8)), jnp.float32)
    out_second = jnp.clip(jnp.exp(math.log(1.47456) - 2.7725887 * jax.random.uniform(streams_of[11], (D, D), jnp.float32) ** steps_of(streams_of[11], (D, D), ((0, 4), (1, 8)), -0.2, 0.2)), 0.09216, 1.47456)
    up_first = gaussian(streams_of[12], (D, FF), (0.11 * 0.3 * (IMAGES * SEQ) ** 0.5), 13.440685, ((0, 8), (1, 4)), jnp.float32)
    up_second = jnp.clip(jnp.exp(math.log(3.31776) - 2.7725887 * jax.random.uniform(streams_of[13], (D, FF), jnp.float32) ** steps_of(streams_of[13], (D, FF), ((0, 8), (1, 4)), -0.2, 0.2)), 0.20736, 3.31776)
    down_first = gaussian(streams_of[14], (FF, D), (0.11 * 0.65 * (IMAGES * SEQ) ** 0.5), 29.121485, ((0, 4), (1, 8)), jnp.float32)
    down_second = jnp.clip(jnp.exp(math.log(15.48288) - 2.7725887 * jax.random.uniform(streams_of[15], (FF, D), jnp.float32) ** steps_of(streams_of[15], (FF, D), ((0, 4), (1, 8)), -0.2, 0.2)), 0.96768, 15.48288)
    vector_first = gaussian(streams_of[16], (8, D), (0.11 * (IMAGES * SEQ) ** 0.5), 44.802284, ((1, 32),), jnp.float32)
    vector_second = jnp.clip(jnp.exp(math.log(36.864) - 2.7725887 * jax.random.uniform(streams_of[17], (8, D), jnp.float32) ** steps_of(streams_of[17], (8, D), ((1, 32),), -0.2, 0.2)), 2.304, 36.864)
    bias_first = gaussian(streams_of[18], (FF,), (0.11 * 0.3 * (IMAGES * SEQ) ** 0.5), 13.440685, ((0, 32),), jnp.float32)
    bias_second = jnp.clip(jnp.exp(math.log(3.31776) - 2.7725887 * jax.random.uniform(streams_of[19], (FF,), jnp.float32) ** steps_of(streams_of[19], (FF,), ((0, 32),), -0.2, 0.2)), 0.20736, 3.31776)
    return {"images": images, "cotangent": cotangent, "qkv_weight": qkv_weight, "out_weight": out_weight, "up_weight": up_weight, "down_weight": down_weight, "vectors": vectors, "up_bias": up_bias, "qkv_first": qkv_first, "qkv_second": qkv_second, "out_first": out_first, "out_second": out_second, "up_first": up_first, "up_second": up_second, "down_first": down_first, "down_second": down_second, "vector_first": vector_first, "vector_second": vector_second, "bias_first": bias_first, "bias_second": bias_second}


@jax.custom_vjp
def low(v):
    return lax.optimization_barrier(v.astype(jnp.bfloat16)).astype(jnp.float32)

@jax.custom_vjp
def low_back(v):
    return v

def low_keep(v):
    return (low(v), None)

def low_pass(kept, grad):
    return (grad,)

def back_keep(v):
    return (v, None)

def back_low(kept, grad):
    return (low(grad),)
low.defvjp(low_keep, low_pass)
low_back.defvjp(back_keep, back_low)
norm_eps = 1e-06
beta_one = 0.9
beta_two = 0.999
adam_eps = 1e-08
highest = lax.Precision.HIGHEST

def product(left, right):
    return jnp.dot(left, right, precision=highest, preferred_element_type=jnp.float32)

def norm_rows(values, gain_vec, shift_vec):
    row_mean = lax.optimization_barrier(jnp.mean(values, axis=-1, keepdims=True))
    centred = values - row_mean
    row_var = lax.optimization_barrier(jnp.mean(centred * centred, axis=-1, keepdims=True))
    return centred * lax.rsqrt(row_var + norm_eps) * gain_vec + shift_vec

def attend_image(pieces):
    queries, keys_in, values_in = pieces
    query_heads = queries.reshape(SEQ, HEADS, HD)
    key_heads = keys_in.reshape(SEQ, HEADS, HD)
    value_heads = values_in.reshape(SEQ, HEADS, HD)
    scores = jnp.einsum('shd,thd->hst', query_heads, key_heads, precision=highest) * HD ** (-0.5)
    scores = low_back(scores)
    soft_probs = low(jax.nn.softmax(scores, axis=-1))
    attended = jnp.einsum('hst,thd->shd', soft_probs, value_heads, precision=highest)
    return attended.reshape(SEQ, D)

def block_layer(inputs, qkv_weight, out_weight, up_weight, down_weight, vectors, up_bias):
    group_size = inputs.shape[0]
    flat_rows = inputs.reshape(-1, D)
    first_norm = norm_rows(flat_rows, vectors[0], vectors[1])
    first_low = low(first_norm)
    qkv_low = low(qkv_weight)
    queries = low(low_back(product(first_low, qkv_low[0]) + vectors[4]))
    keys_all = low(low_back(product(first_low, qkv_low[1])))
    values_all = low(low_back(product(first_low, qkv_low[2]) + vectors[5]))
    attended = lax.map(jax.checkpoint(attend_image), (queries.reshape(group_size, SEQ, D), keys_all.reshape(group_size, SEQ, D), values_all.reshape(group_size, SEQ, D)))
    attended = low(low_back(attended.reshape(-1, D)))
    hidden_state = flat_rows + low_back(product(attended, low(out_weight))) + vectors[6]
    second_low = low(norm_rows(hidden_state, vectors[2], vectors[3]))
    pre_act = low_back(product(second_low, low(up_weight)) + up_bias)
    activated = low(jax.nn.gelu(pre_act, approximate=True))
    result = hidden_state + product(activated, low(down_weight)) + vectors[7]
    return result.reshape(inputs.shape)

def adamw(weight, gradient, first, second, rate, decay):
    first_new = beta_one * first + (1.0 - beta_one) * gradient
    second_new = beta_two * second + (1.0 - beta_two) * gradient * gradient
    first_hat = first_new / (1.0 - beta_one ** STEP)
    second_hat = second_new / (1.0 - beta_two ** STEP)
    weight_new = weight - rate * (first_hat / (jnp.sqrt(second_hat) + adam_eps) + decay * weight)
    return (weight_new, first_new, second_new)

def reference(images, cotangent, qkv_weight, out_weight, up_weight, down_weight, vectors, up_bias, qkv_first, qkv_second, out_first, out_second, up_first, up_second, down_first, down_second, vector_first, vector_second, bias_first, bias_second):
    params = (qkv_weight, out_weight, up_weight, down_weight, vectors, up_bias)
    group_size = math.gcd(IMAGES, 4)
    blocks = IMAGES // group_size
    inputs = images.astype(jnp.float32).reshape(blocks, group_size, SEQ, D)
    cotans = cotangent.astype(jnp.float32).reshape(blocks, group_size, SEQ, D)

    def block_step(summed, pieces):
        input_block, cotan_block = pieces
        result, pullback = jax.vjp(block_layer, input_block, *params)
        gradients = pullback(cotan_block)
        summed = jax.tree.map(jnp.add, summed, tuple(gradients[1:]))
        return (summed, (result, gradients[0]))
    zeros_init = jax.tree.map(jnp.zeros_like, params)
    gradients, (results, input_grads) = lax.scan(block_step, zeros_init, (inputs, cotans))
    output = results.reshape(IMAGES, SEQ, D).astype(jnp.bfloat16)
    input_grad = input_grads.reshape(IMAGES, SEQ, D)
    qkv_state = adamw(qkv_weight, gradients[0], qkv_first, qkv_second, 0.08, 0.1)
    out_state = adamw(out_weight, gradients[1], out_first, out_second, 0.3, 0.1)
    up_state = adamw(up_weight, gradients[2], up_first, up_second, 0.08, 0.1)
    down_state = adamw(down_weight, gradients[3], down_first, down_second, 0.045, 0.1)
    vec_state = adamw(vectors, gradients[4], vector_first, vector_second, 0.5, 0.0)
    bias_state = adamw(up_bias, gradients[5], bias_first, bias_second, 0.7, 0.0)
    return (output, input_grad, qkv_state[0], qkv_state[1], qkv_state[2], out_state[0], out_state[1], out_state[2], up_state[0], up_state[1], up_state[2], down_state[0], down_state[1], down_state[2], vec_state[0], vec_state[1], vec_state[2], bias_state[0], bias_state[1], bias_state[2])
```

```python
import functools
import math

import jax
import jax.numpy as jnp
from jax import lax
from jax.experimental import pallas as pl
from jax.experimental.pallas import tpu as pltpu
from jax.sharding import PartitionSpec as P

HD = 64
STEP = 10


norm_eps = 1e-06
beta_one = 0.9
beta_two = 0.999
adam_eps = 1e-08
gelu_coef = math.sqrt(2.0 / math.pi)
score_scale = float(HD) ** (-0.5)
low = jnp.bfloat16
wide = jnp.float32
VMEM_LIMIT = 48 * 1024 * 1024

NN = (((1,), (0,)), ((), ()))
NT = (((1,), (1,)), ((), ()))
TN = (((0,), (0,)), ((), ()))


def dot(left, right, dims=NN):
    return lax.dot_general(left, right, dims, preferred_element_type=wide)


def kernel_call(body, outs, args, scratch=(), flops=0, moved=0):
    smem = pl.BlockSpec(memory_space=pltpu.SMEM)
    vmem = pl.BlockSpec(memory_space=pltpu.VMEM)
    return pl.pallas_call(
        body,
        out_shape=[jax.ShapeDtypeStruct(s, d) for s, d in outs],
        in_specs=[smem] + [vmem] * (len(args) - 1),
        out_specs=[vmem] * len(outs),
        scratch_shapes=list(scratch),
        compiler_params=pltpu.CompilerParams(vmem_limit_bytes=VMEM_LIMIT),
        cost_estimate=pl.CostEstimate(flops=flops, bytes_accessed=moved, transcendentals=0),
    )(*args)


def flip(value, axis, mask):
    size = lax.axis_size(axis)
    return lax.ppermute(value, axis, [(i, i ^ mask) for i in range(size)])


def gather_parts(shard, dim):
    if lax.axis_size("fsdp") != 8:
        return [lax.all_gather(shard, "fsdp", axis=dim, tiled=True)]
    chips = [shard] + [flip(shard, "fsdp", mask) for mask in (2, 4, 6)]
    others = [flip(part, "fsdp", 1) for part in chips]
    return [part for pair in zip(chips, others) for part in pair]


def fsdp_sum(keep, send):
    got = flip(send, "fsdp", 1)
    total = keep.astype(wide) + got.astype(wide)
    sent = [flip(total[j].astype(low), "fsdp", 2 * j) for j in (1, 2, 3)]
    return total[0] + sum(part.astype(wide) for part in sent)


def summed_on_arrival(value, dim):
    peers = lax.axis_size("fsdp")
    before, after = (value.shape[:dim], value.shape[dim + 1 :])
    blocks = jnp.moveaxis(value.reshape(*before, peers, -1, *after), dim, 0)
    blocks = lax.all_to_all(blocks, "fsdp", 0, 0, tiled=True)
    return jnp.sum(blocks.astype(wide), axis=0)


def norm_parts(values):
    row_mean = jnp.mean(values, axis=-1, keepdims=True)
    centred = values - row_mean
    row_var = jnp.mean(centred * centred, axis=-1, keepdims=True)
    inverse = lax.rsqrt(row_var + norm_eps)
    return centred * inverse, inverse


def norm_backward(grad_out, normed, inverse, gain_vec):
    scaled = grad_out * gain_vec
    return inverse * (
        scaled
        - jnp.mean(scaled, axis=-1, keepdims=True)
        - normed * jnp.mean(scaled * normed, axis=-1, keepdims=True)
    )


def place_rows(at_ref, parts, target, lead):
    if len(parts) == 1:
        target[...] = parts[0][...]
        return
    for slot, part in enumerate(parts):
        height = part.shape[lead]
        start = pl.multiple_of((at_ref[0] ^ slot) * height, 32)
        if lead == 0:
            target[pl.ds(start, height), :] = part[...]
        else:
            target[:, pl.ds(start, height), :] = part[...]


def take_rows(at_ref, source, slot, height):
    start = pl.multiple_of((at_ref[0] ^ slot) * height, 32)
    return source[pl.ds(start, height), :]


def pack_heads(value):
    half = value.shape[0] // 2
    side = value[:, 128:]
    return value[:, :128], jnp.concatenate([side[:half], side[half:]], axis=1)


def unpack_heads(packed):
    rows = packed.shape[0] * 2 // 3
    head, side = packed[:rows], packed[rows:]
    return jnp.concatenate([head, jnp.concatenate([side[:, :64], side[:, 64:]], axis=0)], axis=1)


def attend_kernel(n_parts, at_ref, x_ref, vec_ref, qv_ref, *refs):
    parts = refs[:n_parts]
    a1_ref, qkv_ref, lse_ref, o_ref, w_ref, ot_ref = refs[n_parts:]
    place_rows(at_ref, parts, w_ref, 1)
    normed, _ = norm_parts(x_ref[...].astype(wide))
    a1 = (normed * vec_ref[0:1, :] + vec_ref[1:2, :]).astype(low)
    a1_ref[...] = a1
    q = (dot(a1, w_ref[0]) + qv_ref[0:1, :]).astype(low)
    k = dot(a1, w_ref[1]).astype(low)
    v = (dot(a1, w_ref[2]) + qv_ref[1:2, :]).astype(low)
    qkv_ref[0] = q
    qkv_ref[1] = k
    qkv_ref[2] = v
    vt = v.T
    for head in range(q.shape[1] // HD):
        cols = slice(head * HD, (head + 1) * HD)
        scores = dot(k[:, cols], q[:, cols], NT) * score_scale
        top = jnp.max(scores, axis=0, keepdims=True)
        expos = jnp.exp(scores - top)
        summed = jnp.sum(expos, axis=0, keepdims=True)
        lse_ref[head : head + 1, :] = top + jnp.log(summed)
        ot_ref[cols, :] = dot(vt[cols, :], expos.astype(low)) / summed
    o = ot_ref[...].T.astype(low)
    head_part, side_part = pack_heads(o)
    rows = o.shape[0]
    o_ref[0:rows, :] = head_part
    o_ref[rows:, :] = side_part


def mlp_kernel(n_parts, at_ref, x_ref, c_ref, vec_ref, ub_ref, o_ref, *refs):
    parts = refs[:n_parts]
    (dn2_ref, a2_ref, g_ref, du_ref, own_ref, stat_ref, sums_ref, gub_ref,
     w_ref, h_ref, n_ref, s_ref) = refs[n_parts:]
    ranks = o_ref.shape[0]
    rows, width = x_ref.shape
    part_rows = rows // ranks
    hidden = ub_ref.shape[1]
    heads_width = width // ranks
    if n_parts == 1:
        w_ref[...] = parts[0][...]
    else:
        for slot, part in enumerate(parts):
            height = part.shape[1]
            start = pl.multiple_of((at_ref[0] ^ slot) * height, 32)
            w_ref[:, pl.ds(start, height), :] = part[...]
    rank = at_ref[1]
    o = jnp.concatenate([unpack_heads(o_ref[j]) for j in range(ranks)], axis=1)
    hidden_state = x_ref[...].astype(wide) + dot(o, w_ref[2], NT) + vec_ref[6:7, :]
    h_ref[...] = hidden_state
    normed, inverse = norm_parts(hidden_state)
    n_ref[...] = normed
    s_ref[...] = jnp.broadcast_to(inverse, s_ref.shape)
    a2 = (normed * vec_ref[2:3, :] + vec_ref[3:4, :]).astype(low)
    a2_ref[...] = a2
    pre = dot(a2, w_ref[0]) + ub_ref[...]
    square = pre * pre
    tangent = jnp.tanh(gelu_coef * pre * (1.0 + 0.044715 * square))
    half = 0.5 * (1.0 + tangent)
    g_ref[...] = (pre * half).astype(low)
    slope = half + 0.5 * pre * (1.0 - tangent * tangent) * gelu_coef * (1.0 + 3.0 * 0.044715 * square)
    du = (dot(c_ref[...], w_ref[1]) * slope).astype(low)
    du_ref[...] = du
    gub_ref[...] = jnp.sum(du.astype(wide), axis=0, keepdims=True)
    dn2 = dot(du, w_ref[0], NT)
    sums_ref[0:1, :] = jnp.sum(dn2 * normed, axis=0, keepdims=True)
    sums_ref[1:2, :] = jnp.sum(dn2, axis=0, keepdims=True)
    for j in range(ranks):
        dn2_ref[j ^ rank] = dn2[j * part_rows : (j + 1) * part_rows].astype(low)
    own = pl.ds(pl.multiple_of(rank * part_rows, 16), part_rows)
    own_ref[0] = h_ref[own, :]
    own_ref[1] = n_ref[own, :]
    stat_ref[...] = s_ref[own, :]
    cotan = c_ref[own, :].astype(wide)
    sums_ref[2:3, :] = jnp.sum(cotan, axis=0, keepdims=True)


def mlp_out_kernel(at_ref, g_ref, w_ref, out_ref):
    rank = at_ref[1]
    part_rows = out_ref.shape[1]
    out = dot(g_ref[...], w_ref[1], NT).astype(low)
    for j in range(4):
        out_ref[j ^ rank] = out[j * part_rows : (j + 1) * part_rows]


def mix_kernel(at_ref, own_ref, stat_ref, c_ref, vec_ref, wo_ref, *refs):
    chunks = refs[:4]
    dh_ref, dz_ref, do_ref, gbo_ref = refs[4:]
    rank = at_ref[1]
    part_rows = stat_ref.shape[0]
    grad = sum(ref[...].astype(wide) for ref in chunks)
    own = pl.ds(pl.multiple_of(rank * part_rows, 16), part_rows)
    cotan = c_ref[own, :].astype(wide)
    dh = cotan + norm_backward(grad, own_ref[1], stat_ref[:, 0:1], vec_ref[2:3, :])
    dh_ref[...] = dh
    gbo_ref[...] = jnp.sum(dh, axis=0, keepdims=True)
    dz = dh.astype(low)
    dz_ref[...] = dz
    do = dot(dz, wo_ref[2]).astype(low)
    ranks = do_ref.shape[0]
    heads_width = do.shape[1] // ranks
    for j in range(ranks):
        head_part, side_part = pack_heads(do[:, j * heads_width : (j + 1) * heads_width])
        do_ref[j ^ rank, 0:part_rows, :] = head_part
        do_ref[j ^ rank, part_rows:, :] = side_part


def attend_back_kernel(fast, at_ref, x_ref, a1_ref, qkv_ref, lse_ref, w_ref, *refs):
    chunks = refs[:4]
    if fast:
        dn1_ref, keep_ref, send_ref, sums_ref, qvsum_ref = refs[4:9]
    else:
        dn1_ref, whole_ref, sums_ref, qvsum_ref = refs[4:8]
    do_ref, dqt_ref, d_ref, g_ref = refs[-4:]
    rank = at_ref[1]
    rows, width = x_ref.shape
    part_rows = rows // 4
    for j in range(4):
        do_ref[pl.ds(pl.multiple_of((rank ^ j) * part_rows, 16), part_rows), :] = unpack_heads(chunks[j][...])
    q, k, v, do = qkv_ref[0], qkv_ref[1], qkv_ref[2], do_ref[...]
    kt = k.T
    for head in range(q.shape[1] // HD):
        cols = slice(head * HD, (head + 1) * HD)
        scores = dot(k[:, cols], q[:, cols], NT) * score_scale
        probs = jnp.exp(scores - lse_ref[head : head + 1, :])
        grad_probs = dot(v[:, cols], do[:, cols], NT)
        d_ref[2, :, cols] = dot(probs.astype(low), do[:, cols]).astype(low)
        both = probs * grad_probs
        grad_scores = (both - probs * jnp.sum(both, axis=0, keepdims=True)).astype(low)
        d_ref[1, :, cols] = (dot(grad_scores, q[:, cols]) * score_scale).astype(low)
        dqt_ref[cols, :] = dot(kt[cols, :], grad_scores) * score_scale
    d_ref[0] = dqt_ref[...].T.astype(low)
    qvsum_ref[0:1, :] = jnp.sum(d_ref[0].astype(wide), axis=0, keepdims=True)
    qvsum_ref[1:2, :] = jnp.sum(d_ref[2].astype(wide), axis=0, keepdims=True)
    dn1 = dot(d_ref[0], w_ref[0], NT) + dot(d_ref[1], w_ref[1], NT) + dot(d_ref[2], w_ref[2], NT)
    for j in range(4):
        dn1_ref[j ^ rank] = dn1[j * part_rows : (j + 1) * part_rows].astype(low)
    normed, _ = norm_parts(x_ref[...].astype(wide))
    sums_ref[0:1, :] = jnp.sum(dn1 * normed, axis=0, keepdims=True)
    sums_ref[1:2, :] = jnp.sum(dn1, axis=0, keepdims=True)
    a1t = a1_ref[...].T
    for which in range(3):
        grad = dot(a1t, d_ref[which])
        if fast:
            g_ref[...] = grad.astype(low)
            height = width // 8
            for slot in range(4):
                keep_ref[slot, which] = take_rows(at_ref, g_ref, 2 * slot, height)
                send_ref[slot, which] = take_rows(at_ref, g_ref, 2 * slot + 1, height)
        else:
            whole_ref[which] = grad.astype(low)


def weight_grad_kernel(fast, at_ref, left_ref, right_ref, *refs):
    grad = dot(left_ref[...].T, right_ref[...]).astype(low)
    if not fast:
        refs[0][...] = grad
        return
    keep_ref, send_ref, g_ref = refs
    g_ref[...] = grad
    height = grad.shape[0] // 8
    for slot in range(4):
        keep_ref[slot] = take_rows(at_ref, g_ref, 2 * slot, height)
        send_ref[slot] = take_rows(at_ref, g_ref, 2 * slot + 1, height)


def input_kernel(at_ref, x_ref, dh_ref, vec_ref, *refs):
    chunks, out_ref = refs[:4], refs[4]
    part_rows = dh_ref.shape[0]
    own = pl.ds(pl.multiple_of(at_ref[1] * part_rows, 16), part_rows)
    normed, inverse = norm_parts(x_ref[own, :].astype(wide))
    grad = sum(ref[...].astype(wide) for ref in chunks)
    out_ref[...] = dh_ref[...] + norm_backward(grad, normed, inverse, vec_ref[0:1, :])


def adamw(weight, gradient, first, second, rate, decay):
    first_new = beta_one * first + (1.0 - beta_one) * gradient
    second_new = beta_two * second + (1.0 - beta_two) * gradient * gradient
    first_hat = first_new / (1.0 - beta_one**STEP)
    second_hat = second_new / (1.0 - beta_two**STEP)
    weight_new = weight - rate * (first_hat / (jnp.sqrt(second_hat) + adam_eps) + decay * weight)
    return (weight_new, first_new, second_new)


def body(
    images,
    cotangent,
    qkv_weight,
    out_weight,
    up_weight,
    down_weight,
    vectors,
    up_bias,
    qkv_first,
    qkv_second,
    out_first,
    out_second,
    up_first,
    up_second,
    down_first,
    down_second,
    vector_first,
    vector_second,
    bias_first,
    bias_second,
):
    fsdp_size = lax.axis_size("fsdp")
    tensor_size = lax.axis_size("tensor")
    devices = fsdp_size * tensor_size
    fast = fsdp_size == 8
    rank = lax.axis_index("tensor")
    at = jnp.stack([lax.axis_index("fsdp"), rank]).astype(jnp.int32)
    _, rows, width = images.shape
    hidden = up_weight.shape[1]
    heads_width = width // tensor_size
    part_rows = rows // tensor_size
    height = width // fsdp_size
    x = images.reshape(rows, width)
    c = cotangent.reshape(rows, width)

    cols = vectors.shape[1]
    ends = up_bias.shape[0]
    mine = jnp.concatenate([vectors.reshape(-1), up_bias])
    small = lax.all_to_all(
        jnp.broadcast_to(mine[None], (devices, mine.shape[0])), ("fsdp", "tensor"), 0, 0, tiled=True
    )
    vec = small[:, : 8 * cols].reshape(devices, 8, cols).transpose(1, 0, 2).reshape(8, width)
    full_bias = small[:, 8 * cols :].reshape(1, devices * ends)
    up_local = lax.dynamic_slice_in_dim(full_bias, rank * hidden, hidden, 1)
    qv_bias = lax.dynamic_slice_in_dim(vec[4:6], rank * heads_width, heads_width, 1)

    qkv_parts = gather_parts(qkv_weight.astype(low), 1)
    out_t = out_weight.astype(low).T
    out_slots = jnp.stack([out_t] + [flip(out_t, "tensor", mask) for mask in (1, 2, 3)])
    out_rows = jnp.concatenate([lax.dynamic_index_in_dim(out_slots, rank ^ j, 0, False) for j in range(4)], axis=1)
    shard = jnp.stack([up_weight.astype(low), down_weight.astype(low).T, out_rows])
    shard, qkv_parts = lax.optimization_barrier((shard, qkv_parts))
    rest_parts = gather_parts(shard, 1)

    n = len(qkv_parts)
    a1, qkv, lse, o_mine, qkv_full = kernel_call(
        functools.partial(attend_kernel, n),
        [
            ((rows, width), low),
            ((3, rows, heads_width), low),
            ((8, rows), wide),
            ((rows * 3 // 2, 128), low),
            ((3, width, heads_width), low),
        ],
        (at, x, vec, qv_bias, *qkv_parts),
        [pltpu.VMEM((heads_width, rows), wide)],
        flops=2 * rows * width * heads_width * 3 + 4 * rows * rows * heads_width,
        moved=8 << 20,
    )
    o_all = lax.all_gather(o_mine, "tensor", axis=0)

    dn2, a2, g, du, own, stat, sums_two, gub, w_full = kernel_call(
        functools.partial(mlp_kernel, n),
        [
            ((4, part_rows, width), low),
            ((rows, width), low),
            ((rows, hidden), low),
            ((rows, hidden), low),
            ((2, part_rows, width), wide),
            ((part_rows, 128), wide),
            ((8, width), wide),
            ((1, hidden), wide),
            ((3, width, hidden), low),
        ],
        (at, x, c, vec, up_local, o_all, *rest_parts),
        [pltpu.VMEM((rows, width), wide), pltpu.VMEM((rows, width), wide), pltpu.VMEM((rows, 128), wide)],
        flops=2 * rows * width * (width + 3 * hidden),
        moved=16 << 20,
    )

    dn2_got = [dn2[0]] + [flip(dn2[j], "tensor", j) for j in (1, 2, 3)]

    def weight_grad(left, right):
        shape = (left.shape[1], right.shape[1])
        cut = (4, height, shape[1])
        outs = [(cut, low), (cut, low)] if fast else [(shape, low)]
        got = kernel_call(
            functools.partial(weight_grad_kernel, fast),
            outs,
            (at, left, right),
            [pltpu.VMEM(shape, low)] if fast else [],
            flops=2 * left.shape[0] * shape[0] * shape[1],
            moved=4 << 20,
        )
        return fsdp_sum(*got) if fast else summed_on_arrival(got[0], 0)

    up_owned = weight_grad(a2, du)
    down_owned = weight_grad(c, g).T

    (mlp,) = kernel_call(
        mlp_out_kernel,
        [((4, part_rows, width), low)],
        (at, g, w_full),
        flops=2 * rows * width * hidden,
        moved=3 << 20,
    )

    dh, dz, do, gbo = kernel_call(
        mix_kernel,
        [
            ((part_rows, width), wide),
            ((part_rows, width), low),
            ((4, part_rows * 3 // 2, 128), low),
            ((1, width), wide),
        ],
        (at, own, stat, c, vec, w_full, *dn2_got),
        flops=2 * part_rows * width * width,
        moved=4 << 20,
    )
    do_got = [do[0]] + [flip(do[j], "tensor", j) for j in (1, 2, 3)]

    cut = (4, 3, height, heads_width)
    outs = [((4, part_rows, width), low)]
    outs += [(cut, low), (cut, low)] if fast else [((3, width, heads_width), low)]
    outs += [((8, width), wide), ((8, heads_width), wide)]
    back = kernel_call(
        functools.partial(attend_back_kernel, fast),
        outs,
        (at, x, a1, qkv, lse, qkv_full, *do_got),
        [
            pltpu.VMEM((rows, heads_width), low),
            pltpu.VMEM((heads_width, rows), wide),
            pltpu.VMEM((3, rows, heads_width), low),
            pltpu.VMEM((width, heads_width), low),
        ],
        flops=10 * rows * rows * heads_width + 4 * rows * width * heads_width * 3,
        moved=8 << 20,
    )
    dn1, sums_one, qv_sums = back[0], back[-2], back[-1]
    dn1_got = [dn1[0]] + [flip(dn1[j], "tensor", j) for j in (1, 2, 3)]
    qkv_owned = fsdp_sum(back[1], back[2]) if fast else summed_on_arrival(back[1], 1)

    def place(value, total):
        return lax.dynamic_update_slice_in_dim(
            jnp.zeros((value.shape[0], total), wide), value, rank * value.shape[1], 1
        )

    vector_grad = jnp.concatenate(
        [sums_one[0:2], sums_two[0:2], place(qv_sums[0:2], width), gbo, sums_two[2:3]], axis=0
    )
    bias_grad = place(gub, hidden * tensor_size)
    blocks = jnp.concatenate(
        [
            vector_grad.reshape(8, devices, cols).transpose(1, 0, 2).reshape(devices, 8 * cols),
            bias_grad.reshape(devices, ends),
        ],
        axis=1,
    )
    owned = jnp.sum(lax.all_to_all(blocks, ("fsdp", "tensor"), 0, 0, tiled=True), axis=0)
    vector_owned = owned[: 8 * cols].reshape(8, cols)
    bias_owned = owned[8 * cols :]

    mlp_got = [mlp[0]] + [flip(mlp[j], "tensor", j) for j in (1, 2, 3)]
    output = (own[0] + sum(part.astype(wide) for part in mlp_got) + vec[7]).astype(low)
    dz_all = lax.all_gather(dz, "tensor", axis=0, tiled=True)
    o_flat = unpack_heads(o_mine)
    out_owned = weight_grad(dz_all, o_flat).T

    (input_own,) = kernel_call(
        input_kernel,
        [((part_rows, width), wide)],
        (at, x, dh, vec, *dn1_got),
        moved=3 << 20,
    )

    qkv_state = adamw(qkv_weight, qkv_owned, qkv_first, qkv_second, 0.08, 0.1)
    out_state = adamw(out_weight, out_owned, out_first, out_second, 0.3, 0.1)
    up_state = adamw(up_weight, up_owned, up_first, up_second, 0.08, 0.1)
    down_state = adamw(down_weight, down_owned, down_first, down_second, 0.045, 0.1)
    vec_state = adamw(vectors, vector_owned, vector_first, vector_second, 0.5, 0.0)
    bias_state = adamw(up_bias, bias_owned, bias_first, bias_second, 0.7, 0.0)
    return (
        output[None],
        input_own[None],
        *qkv_state,
        *out_state,
        *up_state,
        *down_state,
        *vec_state,
        *bias_state,
    )


def solution(mesh):
    weights = (P(None, "fsdp", "tensor"), P("tensor", "fsdp"), P("fsdp", "tensor"), P("tensor", "fsdp"))
    vector, bias = P(None, ("fsdp", "tensor")), P(("fsdp", "tensor"))
    twice = [spec for spec in (*weights, vector, bias) for _ in range(2)]
    thrice = [spec for spec in (*weights, vector, bias) for _ in range(3)]
    return jax.shard_map(
        body,
        mesh=mesh,
        in_specs=(P("fsdp", None, None), P("fsdp", None, None), *weights, vector, bias, *twice),
        out_specs=(P("fsdp", "tensor", None), P("fsdp", "tensor", None), *thrice),
        check_vma=False,
    )
```

```python
import functools
import math

import jax
import jax.numpy as jnp
from jax import lax
from jax.experimental import pallas as pl
from jax.experimental.pallas import tpu as pltpu
from jax.sharding import PartitionSpec as P

HD = 64
STEP = 10


norm_eps = 1e-06
beta_one = 0.9
beta_two = 0.999
adam_eps = 1e-08
gelu_coef = math.sqrt(2.0 / math.pi)
score_scale = float(HD) ** (-0.5)
low = jnp.bfloat16
wide = jnp.float32
VMEM_LIMIT = 24 * 1024 * 1024

NN = (((1,), (0,)), ((), ()))
NT = (((1,), (1,)), ((), ()))
TN = (((0,), (0,)), ((), ()))


def dot(left, right, dims=NN):
    return lax.dot_general(left, right, dims, preferred_element_type=wide)


def kernel_call(body, outs, args, scratch=()):
    smem = pl.BlockSpec(memory_space=pltpu.SMEM)
    vmem = pl.BlockSpec(memory_space=pltpu.VMEM)
    return pl.pallas_call(
        body,
        out_shape=[jax.ShapeDtypeStruct(s, d) for s, d in outs],
        in_specs=[smem] + [vmem] * (len(args) - 1),
        out_specs=[vmem] * len(outs),
        scratch_shapes=list(scratch),
        compiler_params=pltpu.CompilerParams(vmem_limit_bytes=VMEM_LIMIT),
        cost_estimate=pl.CostEstimate(flops=0, bytes_accessed=0, transcendentals=0),
    )(*args)


def flip(value, axis, mask):
    size = lax.axis_size(axis)
    return lax.ppermute(value, axis, [(i, i ^ mask) for i in range(size)])


def after(value, *others):
    return lax.optimization_barrier((value, *others))[0]


def chips_of(shard):
    return lax.optimization_barrier([shard] + [flip(shard, "fsdp", mask) for mask in (2, 4, 6)])


def cores_of(chips):
    others = [flip(part, "fsdp", 1) for part in chips]
    return [part for pair in zip(chips, others) for part in pair]


def summed_on_arrival(value, dim):
    peers = lax.axis_size("fsdp")
    before, behind = (value.shape[:dim], value.shape[dim + 1 :])
    blocks = jnp.moveaxis(value.reshape(*before, peers, -1, *behind), dim, 0)
    blocks = lax.all_to_all(blocks, "fsdp", 0, 0, tiled=True)
    return [jnp.sum(blocks.astype(wide), axis=0)]


def rank_gather(value):
    one, two = flip(value, "tensor", 1), flip(value, "tensor", 2)
    return [value, one, two, flip(two, "tensor", 1)]


def rank_sum(at, slots):
    three = flip(slots[3], "tensor", 1)
    one = flip(slots[1], "tensor", 1)
    (two,) = kernel_call(add_kernel, [(three.shape, low)], (at, slots[2], three))
    return [slots[0], one, flip(two, "tensor", 2)]


def to_ranks(slots):
    return [slots[0]] + [flip(slots[j], "tensor", j) for j in (1, 2, 3)]


def norm_parts(values):
    row_mean = jnp.mean(values, axis=-1, keepdims=True)
    centred = values - row_mean
    row_var = jnp.mean(centred * centred, axis=-1, keepdims=True)
    inverse = lax.rsqrt(row_var + norm_eps)
    return centred * inverse, inverse


def norm_backward(grad_out, normed, inverse, gain_vec):
    scaled = grad_out * gain_vec
    return inverse * (
        scaled
        - jnp.mean(scaled, axis=-1, keepdims=True)
        - normed * jnp.mean(scaled * normed, axis=-1, keepdims=True)
    )


def place_rows(at_ref, parts, target):
    if len(parts) == 1:
        target[...] = parts[0][...]
        return
    for slot, part in enumerate(parts):
        height = part.shape[1]
        start = pl.multiple_of((at_ref[0] ^ slot) * height, 32)
        target[:, pl.ds(start, height), :] = part[...]


def take_rows(at_ref, source, slot, height):
    start = pl.multiple_of((at_ref[0] ^ slot) * height, 32)
    return source[pl.ds(start, height), :]


def rank_rows(at_ref, slot, height):
    return pl.ds(pl.multiple_of((at_ref[1] ^ slot) * height, 16), height)


def pack_heads(value):
    half = value.shape[0] // 2
    side = value[:, 128:]
    return value[:, :128], jnp.concatenate([side[:half], side[half:]], axis=1)


def unpack_heads(packed):
    rows = packed.shape[0] * 2 // 3
    head, side = packed[:rows], packed[rows:]
    return jnp.concatenate([head, jnp.concatenate([side[:, :64], side[:, 64:]], axis=0)], axis=1)


def two_halves(value):
    upper = value.astype(low)
    return jnp.concatenate([upper.astype(wide), value - upper.astype(wide)], axis=0)


def small_pack_kernel(at_ref, vec_ref, bias_ref, out_ref):
    cols, ends = vec_ref.shape[1], bias_ref.shape[1]
    tile = jnp.concatenate(
        [vec_ref[...], jnp.zeros((8, 128 - cols - ends), wide), jnp.broadcast_to(bias_ref[...], (8, ends))], axis=1
    )
    for j in range(out_ref.shape[0]):
        out_ref[j] = tile


def small_unpack_kernel(cols, at_ref, small_ref, vec_ref, qv_ref, bias_ref):
    devices = small_ref.shape[0]
    ends = bias_ref.shape[1] * 4 // devices
    share = devices // 4
    vec_ref[...] = jnp.concatenate([small_ref[j, :, :cols] for j in range(devices)], axis=1)
    mine = [small_ref[at_ref[1] * share + j] for j in range(share)]
    qv_ref[...] = jnp.concatenate([tile[:, :cols] for tile in mine], axis=1)
    bias_ref[...] = jnp.concatenate([tile[0:1, 128 - ends :] for tile in mine], axis=1)


def round_kernel(turned, at_ref, in_ref, out_ref):
    value = in_ref[...]
    out_ref[...] = (value.T if turned else value).astype(low)


def add_kernel(at_ref, left_ref, right_ref, out_ref):
    out_ref[...] = (left_ref[...].astype(wide) + right_ref[...].astype(wide)).astype(out_ref.dtype)


def pair_kernel(at_ref, keep_ref, got_ref, stay_ref, go_ref):
    stay_ref[...] = keep_ref[0].astype(wide) + got_ref[0].astype(wide)
    go_ref[...] = (keep_ref[1].astype(wide) + got_ref[1].astype(wide)).astype(low)


def across_kernel(at_ref, stay_ref, got_ref, mine_ref, go_ref):
    mine_ref[...] = stay_ref[0] + got_ref[0].astype(wide)
    go_ref[...] = (stay_ref[1] + got_ref[1].astype(wide)).astype(low)


def quad_kernel(at_ref, keep_ref, got_ref, mine_ref, *go_refs):
    mine_ref[...] = keep_ref[0, 0].astype(wide) + got_ref[0, 0].astype(wide)
    for j, ref in enumerate(go_refs, 1):
        at = (j // 2, j % 2)
        ref[...] = (keep_ref[at].astype(wide) + got_ref[at].astype(wide)).astype(low)


def ranks_kernel(at_ref, left_ref, right_ref, *out_refs):
    total = left_ref[...] + right_ref[...].astype(wide)
    width = total.shape[1] // 4
    for j, ref in enumerate(out_refs):
        ref[...] = total[:, j * width : (j + 1) * width].astype(low)


def output_kernel(at_ref, own_ref, vec_ref, one_ref, two_ref, three_ref, out_ref):
    total = one_ref[...].astype(wide) + two_ref[...].astype(wide) + three_ref[...].astype(wide)
    out_ref[...] = (own_ref[0] + total + vec_ref[7:8, :]).astype(low)


def sums_pack_kernel(cols, ends, at_ref, one_ref, two_ref, qv_ref, gbo_ref, gub_ref, out_ref):
    devices = out_ref.shape[0]
    share = devices // 4
    middle = jnp.zeros((8, 128 - cols - ends), wide)
    for j in range(devices):
        span = slice(j * cols, (j + 1) * cols)
        mine = (at_ref[1] == j // share).astype(wide)
        k = j % share
        rows = [
            one_ref[0:2, span],
            two_ref[0:2, span],
            qv_ref[0:2, k * cols : (k + 1) * cols] * mine,
            gbo_ref[0:1, span],
            two_ref[2:3, span],
        ]
        bias = gub_ref[0:1, k * ends : (k + 1) * ends] * mine
        out_ref[j] = jnp.concatenate(
            [jnp.concatenate(rows, axis=0), middle, jnp.broadcast_to(bias, (8, ends))], axis=1
        )


def small_adam_kernel(at_ref, got_ref, *refs):
    (w_ref, m_ref, s_ref, b_ref, bm_ref, bs_ref), outs = refs[:6], refs[6:]
    total = jnp.sum(got_ref[...], axis=0)
    cols, ends = w_ref.shape[1], b_ref.shape[1]
    states = adamw(w_ref[...], total[:, :cols], m_ref[...], s_ref[...], 0.5, 0.0)
    states += adamw(b_ref[...], total[0:1, 128 - ends :], bm_ref[...], bs_ref[...], 0.7, 0.0)
    for ref, value in zip(outs, states):
        ref[...] = value


def adam_kernel(n_parts, turned, rate, decay, at_ref, *refs):
    parts, (w_ref, m_ref, s_ref) = refs[:n_parts], refs[n_parts : n_parts + 3]
    total = sum(ref[...].astype(wide) for ref in parts)
    if turned:
        total = total.T
    states = adamw(w_ref[...], total, m_ref[...], s_ref[...], rate, decay)
    for ref, value in zip(refs[n_parts + 3 :], states):
        ref[...] = value


def weights_kernel(at_ref, up_ref, down_ref, *refs):
    parts, out_ref = refs[:4], refs[4]
    height = up_ref.shape[0]
    out_ref[0] = up_ref[...].astype(low)
    out_ref[1] = down_ref[...].astype(low)
    out_ref[2] = jnp.concatenate([ref[...] for ref in parts], axis=1)


def attend_kernel(n_parts, at_ref, x_ref, vec_ref, qv_ref, *refs):
    parts = refs[:n_parts]
    a1_ref, qkv_ref, lse_ref, o_ref, w_ref, ot_ref = refs[n_parts:]
    if n_parts == 1:
        w_ref[...] = parts[0][...]
    else:
        height = w_ref.shape[1] // n_parts
        for slot, part in enumerate(parts):
            start = pl.multiple_of((at_ref[0] ^ slot) * height, 32)
            for j in range(3):
                w_ref[j, pl.ds(start, height), :] = part[j]
    normed, _ = norm_parts(x_ref[...].astype(wide))
    a1 = (normed * vec_ref[0:1, :] + vec_ref[1:2, :]).astype(low)
    a1_ref[...] = a1
    q = (dot(a1, w_ref[0]) + qv_ref[4:5, :]).astype(low)
    k = dot(a1, w_ref[1]).astype(low)
    v = (dot(a1, w_ref[2]) + qv_ref[5:6, :]).astype(low)
    qkv_ref[0] = q
    qkv_ref[1] = k
    qkv_ref[2] = v
    vt = v.T
    for head in range(q.shape[1] // HD):
        cols = slice(head * HD, (head + 1) * HD)
        scores = dot(k[:, cols], q[:, cols], NT) * score_scale
        top = jnp.max(scores, axis=0, keepdims=True)
        expos = jnp.exp(scores - top)
        summed = jnp.sum(expos, axis=0, keepdims=True)
        lse_ref[head : head + 1, :] = top + jnp.log(summed)
        ot_ref[cols, :] = dot(vt[cols, :], expos.astype(low)) / summed
    o = ot_ref[...].T.astype(low)
    head_part, side_part = pack_heads(o)
    rows = o.shape[0]
    o_ref[0:rows, :] = head_part
    o_ref[rows:, :] = side_part


def mlp_kernel(n_parts, at_ref, x_ref, c_ref, vec_ref, ub_ref, *refs):
    heads, parts = refs[:4], refs[4 : 4 + n_parts]
    dn2_refs = refs[4 + n_parts : 8 + n_parts]
    (a2_ref, g_ref, du_ref, own_ref, stat_ref, sums_ref, gub_ref, oo_ref,
     w_ref, h_ref, n_ref, s_ref, o_ref) = refs[8 + n_parts :]
    part_rows = dn2_refs[0].shape[0]
    place_rows(at_ref, parts, w_ref)
    o_ref[...] = jnp.concatenate([unpack_heads(ref[...]) for ref in heads], axis=1)
    hidden_state = x_ref[...].astype(wide) + dot(o_ref[...], w_ref[2], NT) + vec_ref[6:7, :]
    h_ref[...] = hidden_state
    normed, inverse = norm_parts(hidden_state)
    n_ref[...] = normed
    s_ref[...] = jnp.broadcast_to(inverse, s_ref.shape)
    a2 = (normed * vec_ref[2:3, :] + vec_ref[3:4, :]).astype(low)
    a2_ref[...] = a2
    pre = dot(a2, w_ref[0]) + ub_ref[...]
    square = pre * pre
    tangent = jnp.tanh(gelu_coef * pre * (1.0 + 0.044715 * square))
    half = 0.5 * (1.0 + tangent)
    g_ref[...] = (pre * half).astype(low)
    slope = half + 0.5 * pre * (1.0 - tangent * tangent) * gelu_coef * (1.0 + 3.0 * 0.044715 * square)
    du = (dot(c_ref[...], w_ref[1]) * slope).astype(low)
    du_ref[...] = du
    gub_ref[...] = jnp.sum(du.astype(wide), axis=0, keepdims=True)
    own = rank_rows(at_ref, 0, part_rows)
    own_ref[0] = h_ref[own, :]
    own_ref[1] = n_ref[own, :]
    stat_ref[...] = s_ref[own, :]
    oo_ref[...] = o_ref[own, :]
    dn2 = dot(du, w_ref[0], NT)
    h_ref[...] = dn2
    sums_ref[0:1, :] = jnp.sum(dn2 * normed, axis=0, keepdims=True)
    sums_ref[1:2, :] = jnp.sum(dn2, axis=0, keepdims=True)
    for j, ref in enumerate(dn2_refs):
        ref[...] = h_ref[rank_rows(at_ref, j, part_rows), :].astype(low)
    sums_ref[2:3, :] = jnp.sum(c_ref[own, :].astype(wide), axis=0, keepdims=True)


def mlp_out_kernel(at_ref, g_ref, w_ref, *refs):
    slots, out_ref = refs[:4], refs[4]
    out_ref[...] = dot(g_ref[...], w_ref[1], NT)
    for j, ref in enumerate(slots):
        ref[...] = out_ref[rank_rows(at_ref, j, ref.shape[0]), :].astype(low)


def mix_kernel(at_ref, own_ref, stat_ref, c_ref, vec_ref, w_ref, *refs):
    chunks = refs[:3]
    dh_ref, dz_ref, gbo_ref = refs[3:6]
    do_refs = refs[6:]
    part_rows = stat_ref.shape[0]
    grad = sum(ref[...].astype(wide) for ref in chunks)
    cotan = c_ref[rank_rows(at_ref, 0, part_rows), :].astype(wide)
    dh = cotan + norm_backward(grad, own_ref[1], stat_ref[:, 0:1], vec_ref[2:3, :])
    dh_ref[...] = dh
    gbo_ref[...] = jnp.sum(dh, axis=0, keepdims=True)
    dz = dh.astype(low)
    dz_ref[...] = dz
    do = dot(dz, w_ref[2]).astype(low)
    heads_width = do.shape[1] // 4
    for j, ref in enumerate(do_refs):
        head_part, side_part = pack_heads(do[:, j * heads_width : (j + 1) * heads_width])
        ref[0:part_rows, :] = head_part
        ref[part_rows:, :] = side_part


def attend_back_kernel(fast, at_ref, x_ref, a1_ref, qkv_ref, lse_ref, w_ref, *refs):
    chunks, dn1_refs = refs[:4], refs[4:8]
    if fast:
        keep_ref, send_ref, sums_ref, qvsum_ref = refs[8:12]
    else:
        whole_ref, sums_ref, qvsum_ref = refs[8:11]
    do_ref, dqt_ref, d_ref, g_ref, dn1_ref = refs[-5:]
    rows, width = x_ref.shape
    part_rows = rows // 4
    for j in range(4):
        do_ref[rank_rows(at_ref, j, part_rows), :] = unpack_heads(chunks[j][...])
    q, k, v, do = qkv_ref[0], qkv_ref[1], qkv_ref[2], do_ref[...]
    kt = k.T
    for head in range(q.shape[1] // HD):
        cols = slice(head * HD, (head + 1) * HD)
        scores = dot(k[:, cols], q[:, cols], NT) * score_scale
        probs = jnp.exp(scores - lse_ref[head : head + 1, :])
        grad_probs = dot(v[:, cols], do[:, cols], NT)
        d_ref[2, :, cols] = dot(probs.astype(low), do[:, cols]).astype(low)
        both = probs * grad_probs
        grad_scores = (both - probs * jnp.sum(both, axis=0, keepdims=True)).astype(low)
        d_ref[1, :, cols] = (dot(grad_scores, q[:, cols]) * score_scale).astype(low)
        dqt_ref[cols, :] = dot(kt[cols, :], grad_scores) * score_scale
    d_ref[0] = dqt_ref[...].T.astype(low)
    qvsum_ref[0:1, :] = jnp.sum(d_ref[0].astype(wide), axis=0, keepdims=True)
    qvsum_ref[1:2, :] = jnp.sum(d_ref[2].astype(wide), axis=0, keepdims=True)
    dn1 = dot(d_ref[0], w_ref[0], NT) + dot(d_ref[1], w_ref[1], NT) + dot(d_ref[2], w_ref[2], NT)
    dn1_ref[...] = dn1
    for j, ref in enumerate(dn1_refs):
        ref[...] = dn1_ref[rank_rows(at_ref, j, part_rows), :].astype(low)
    normed, _ = norm_parts(x_ref[...].astype(wide))
    sums_ref[0:1, :] = jnp.sum(dn1 * normed, axis=0, keepdims=True)
    sums_ref[1:2, :] = jnp.sum(dn1, axis=0, keepdims=True)
    a1t = a1_ref[...].T
    for which in range(3):
        grad = dot(a1t, d_ref[which])
        if fast:
            g_ref[...] = grad.astype(low)
            height = width // 8
            for slot in range(4):
                mask = (0, 4, 2, 6)[slot]
                keep_ref[slot // 2, slot % 2, which] = take_rows(at_ref, g_ref, mask, height)
                send_ref[slot // 2, slot % 2, which] = take_rows(at_ref, g_ref, mask ^ 1, height)
        else:
            whole_ref[which] = grad.astype(low)


def weight_grad_kernel(fast, masks, at_ref, left_ref, right_ref, *refs):
    grad = dot(left_ref[...].T, right_ref[...]).astype(low)
    if not fast:
        refs[0][...] = grad
        return
    keep_ref, send_ref, g_ref = refs
    g_ref[...] = grad
    height = grad.shape[0] // 8
    for slot, mask in enumerate(masks):
        keep_ref[slot // 2, slot % 2] = take_rows(at_ref, g_ref, mask, height)
        send_ref[slot // 2, slot % 2] = take_rows(at_ref, g_ref, mask ^ 1, height)


def input_kernel(at_ref, x_ref, dh_ref, vec_ref, *refs):
    chunks, out_ref = refs[:3], refs[3]
    part_rows = dh_ref.shape[0]
    normed, inverse = norm_parts(x_ref[rank_rows(at_ref, 0, part_rows), :].astype(wide))
    grad = sum(ref[...].astype(wide) for ref in chunks)
    out_ref[...] = dh_ref[...] + norm_backward(grad, normed, inverse, vec_ref[0:1, :])


def adamw(weight, gradient, first, second, rate, decay):
    first_new = beta_one * first + (1.0 - beta_one) * gradient
    second_new = beta_two * second + (1.0 - beta_two) * gradient * gradient
    first_hat = first_new / (1.0 - beta_one**STEP)
    second_hat = second_new / (1.0 - beta_two**STEP)
    weight_new = weight - rate * (first_hat / (jnp.sqrt(second_hat) + adam_eps) + decay * weight)
    return (weight_new, first_new, second_new)


def body(
    images,
    cotangent,
    qkv_weight,
    out_weight,
    up_weight,
    down_weight,
    vectors,
    up_bias,
    qkv_first,
    qkv_second,
    out_first,
    out_second,
    up_first,
    up_second,
    down_first,
    down_second,
    vector_first,
    vector_second,
    bias_first,
    bias_second,
):
    fsdp_size = lax.axis_size("fsdp")
    tensor_size = lax.axis_size("tensor")
    devices = fsdp_size * tensor_size
    fast = fsdp_size == 8
    at = jnp.stack([lax.axis_index("fsdp"), lax.axis_index("tensor")]).astype(jnp.int32)
    _, rows, width = images.shape
    hidden = up_weight.shape[1]
    heads_width = width // tensor_size
    part_rows = rows // tensor_size
    height = width // fsdp_size
    x = images.reshape(rows, width)
    c = cotangent.reshape(rows, width)
    cols, ends = vectors.shape[1], up_bias.shape[0]
    both_axes = ("fsdp", "tensor")

    (tiles,) = kernel_call(
        small_pack_kernel, [((devices, 8, 128), wide)], (at, vectors, up_bias[None])
    )
    small = lax.all_to_all(tiles, both_axes, 0, 0, tiled=True)
    vec, qv, up_local = kernel_call(
        functools.partial(small_unpack_kernel, cols),
        [((8, width), wide), ((8, heads_width), wide), ((1, hidden), wide)],
        (at, small),
    )

    (qkv_low,) = kernel_call(
        functools.partial(round_kernel, False), [(qkv_weight.shape, low)], (at, after(qkv_weight, tiles))
    )
    (out_t,) = kernel_call(
        functools.partial(round_kernel, True), [((height, heads_width), low)], (at, after(out_weight, qkv_low))
    )
    if fast:
        chips = chips_of(qkv_low)
        qkv_parts = cores_of(chips)
    else:
        chips = qkv_parts = [lax.all_gather(qkv_low, "fsdp", axis=1, tiled=True)]
    (shard,) = kernel_call(
        weights_kernel,
        [((3, height, width), low)],
        (at, after(up_weight, chips[-1]), down_weight.T, *to_ranks([out_t] * 4)),
    )
    if fast:
        chips = chips_of(shard)

    n = len(qkv_parts)
    a1, qkv, lse, o_mine, qkv_full = kernel_call(
        functools.partial(attend_kernel, n),
        [
            ((rows, width), low),
            ((3, rows, heads_width), low),
            ((8, rows), wide),
            ((rows * 3 // 2, 128), low),
            ((3, width, heads_width), low),
        ],
        (at, x, vec, qv, *qkv_parts),
        [pltpu.VMEM((heads_width, rows), wide)],
    )
    o_parts = rank_gather(o_mine)
    if fast:
        chips = lax.optimization_barrier((*chips, o_parts[1]))[:4]
        rest_parts = cores_of(chips)
    else:
        rest_parts = [lax.all_gather(shard, "fsdp", axis=1, tiled=True)]

    block = ((part_rows, width), low)
    *dn2, a2, g, du, own, stat, sums_two, gub, o_own, w_full = kernel_call(
        functools.partial(mlp_kernel, n),
        [
            *[block] * 4,
            ((rows, width), low),
            ((rows, hidden), low),
            ((rows, hidden), low),
            ((2, part_rows, width), wide),
            ((part_rows, 128), wide),
            ((8, width), wide),
            ((1, hidden), wide),
            block,
            ((3, width, hidden), low),
        ],
        (at, x, c, vec, up_local, *o_parts, *rest_parts),
        [
            pltpu.VMEM((rows, width), wide),
            pltpu.VMEM((rows, width), wide),
            pltpu.VMEM((rows, 128), wide),
            pltpu.VMEM((rows, width), low),
        ],
    )
    dn2_got = rank_sum(at, dn2)

    def weight_grad(left, right, masks):
        shape = (left.shape[1], right.shape[1])
        cut = (2, 2, height, shape[1])
        return kernel_call(
            functools.partial(weight_grad_kernel, fast, masks),
            [(cut, low), (cut, low)] if fast else [(shape, low)],
            (at, left, right),
            [pltpu.VMEM(shape, low)] if fast else [],
        )

    def over_cores(grads):
        keep, send = grads
        half = keep.shape[1:]
        return kernel_call(pair_kernel, [(half, wide), (half, low)], (at, keep, flip(send, "fsdp", 1)))

    def over_first(stay, go, mask):
        block = stay.shape[1:]
        return kernel_call(across_kernel, [(block, wide), (block, low)], (at, stay, flip(go, "fsdp", mask)))

    along_x, along_y = (0, 4, 2, 6), (0, 2, 4, 6)
    up_sums = weight_grad(a2, du, along_x)
    down_sums = weight_grad(c, g, along_y)
    if fast:
        up_sums, down_sums = over_cores(up_sums), over_cores(down_sums)
    mlp = kernel_call(
        mlp_out_kernel,
        [block] * 4,
        (at, g, w_full),
        [pltpu.VMEM((rows, width), wide)],
    )
    held = lax.optimization_barrier((dn2_got, up_sums, down_sums, mlp))
    dn2_got, up_sums, down_sums, mlp = held
    dh, dz, gbo, *do = kernel_call(
        mix_kernel,
        [
            ((part_rows, width), wide),
            block,
            ((1, width), wide),
            *[((part_rows * 3 // 2, 128), low)] * 4,
        ],
        (at, own, stat, c, vec, w_full, *dn2_got),
    )
    do_got = to_ranks(do)
    out_grads = weight_grad(dz, o_own, along_x)
    if fast:
        up_sums, down_sums = over_first(*up_sums, 2), over_first(*down_sums, 4)
    held = lax.optimization_barrier((do_got, mlp, out_grads, up_sums, down_sums))
    do_got, mlp, out_grads, up_sums, down_sums = held
    mlp_got = rank_sum(at, mlp)
    (output,) = kernel_call(output_kernel, [block], (at, own, vec, *mlp_got))
    if fast:
        up_sums = [up_sums[0], flip(up_sums[1], "fsdp", 4)]
        down_sums = [down_sums[0], flip(down_sums[1], "fsdp", 2)]
        out_sums = over_first(*over_cores(out_grads), 2)
        out_sums = [out_sums[0], flip(out_sums[1], "fsdp", 4)]
    else:
        up_sums = summed_on_arrival(up_sums[0], 0)
        down_sums = summed_on_arrival(down_sums[0], 0)
        out_sums = summed_on_arrival(out_grads[0], 0)
        out_sums = [out_sums[0], jnp.zeros(out_sums[0].shape, low)]
    out_sums = to_ranks(
        kernel_call(ranks_kernel, [((height, heads_width), low)] * 4, (at, *out_sums))
    )

    cut = (2, 2, 3, height, heads_width)
    outs = [block] * 4
    outs += [(cut, low), (cut, low)] if fast else [((3, width, heads_width), low)]
    outs += [((8, width), wide), ((8, heads_width), wide)]
    back = kernel_call(
        functools.partial(attend_back_kernel, fast),
        outs,
        (at, x, a1, qkv, lse, qkv_full, *do_got),
        [
            pltpu.VMEM((rows, heads_width), low),
            pltpu.VMEM((heads_width, rows), wide),
            pltpu.VMEM((3, rows, heads_width), low),
            pltpu.VMEM((width, heads_width), low),
            pltpu.VMEM((rows, width), wide),
        ],
    )
    dn1, sums_one, qv_sums = back[:4], back[-2], back[-1]
    dn1_got = rank_sum(at, dn1)
    if fast:
        got = flip(back[5], "fsdp", 1)
        blk = (3, height, heads_width)
        mine, *go = kernel_call(quad_kernel, [(blk, wide)] + [(blk, low)] * 3, (at, back[4], got))
        qkv_sums = [mine] + [flip(part, "fsdp", mask) for part, mask in zip(go, (4, 2, 6))]
    else:
        qkv_sums = summed_on_arrival(back[4], 1)

    (tiles,) = kernel_call(
        functools.partial(sums_pack_kernel, cols, ends),
        [((devices, 8, 128), wide)],
        (at, sums_one, sums_two, qv_sums, gbo, gub),
    )
    tiles = lax.all_to_all(tiles, both_axes, 0, 0, tiled=True)
    *vec_state, bias_new, bias_m, bias_s = kernel_call(
        small_adam_kernel,
        [(vectors.shape, wide)] * 3 + [((1, ends), wide)] * 3,
        (at, tiles, vectors, vector_first, vector_second, up_bias[None], bias_first[None], bias_second[None]),
    )

    def update(sums, weight, first, second, rate, decay, turned=False):
        return kernel_call(
            functools.partial(adam_kernel, len(sums), turned, rate, decay),
            [(weight.shape, wide)] * 3,
            (at, *sums, weight, first, second),
        )

    up_state = update(up_sums, up_weight, up_first, up_second, 0.08, 0.1)
    down_state = update(down_sums, down_weight.T, down_first.T, down_second.T, 0.045, 0.1)
    down_state = [value.T for value in down_state]
    out_state = update(out_sums, out_weight, out_first, out_second, 0.3, 0.1, True)
    qkv_state = update(qkv_sums, qkv_weight, qkv_first, qkv_second, 0.08, 0.1)

    (input_own,) = kernel_call(
        input_kernel,
        [((part_rows, width), wide)],
        (at, x, dh, vec, *dn1_got),
    )
    return (
        output[None],
        input_own[None],
        *qkv_state,
        *out_state,
        *up_state,
        *down_state,
        *vec_state,
        bias_new[0],
        bias_m[0],
        bias_s[0],
    )


def solution(mesh):
    weights = (P(None, "fsdp", "tensor"), P("tensor", "fsdp"), P("fsdp", "tensor"), P("tensor", "fsdp"))
    vector, bias = P(None, ("fsdp", "tensor")), P(("fsdp", "tensor"))
    twice = [spec for spec in (*weights, vector, bias) for _ in range(2)]
    thrice = [spec for spec in (*weights, vector, bias) for _ in range(3)]
    return jax.shard_map(
        body,
        mesh=mesh,
        in_specs=(P("fsdp", None, None), P("fsdp", None, None), *weights, vector, bias, *twice),
        out_specs=(P("fsdp", "tensor", None), P("fsdp", "tensor", None), *thrice),
        check_vma=False,
    )
```

```python
import functools
import math

import jax
import jax.numpy as jnp
from jax import lax
from jax.experimental import pallas as pl
from jax.experimental.pallas import tpu as pltpu
from jax.sharding import PartitionSpec as P

HD = 64
STEP = 10


norm_eps = 1e-06
beta_one = 0.9
beta_two = 0.999
adam_eps = 1e-08
gelu_coef = math.sqrt(2.0 / math.pi)
score_scale = float(HD) ** (-0.5)
low = jnp.bfloat16
wide = jnp.float32
VMEM_LIMIT = 24 * 1024 * 1024

NN = (((1,), (0,)), ((), ()))
NT = (((1,), (1,)), ((), ()))
TN = (((0,), (0,)), ((), ()))


def dot(left, right, dims=NN):
    return lax.dot_general(left, right, dims, preferred_element_type=wide)


def kernel_call(body, outs, args, scratch=(), hbm=(), free=(), hbm_outs=False):
    def spec(i):
        space = pltpu.HBM if i in hbm else pl.ANY if i in free else pltpu.VMEM
        return pl.BlockSpec(memory_space=space)

    out_space = pltpu.HBM if hbm_outs else pltpu.VMEM
    args = [pltpu.with_memory_space_constraint(arg, pltpu.HBM) if i in hbm else arg for i, arg in enumerate(args)]
    return pl.pallas_call(
        body,
        out_shape=[jax.ShapeDtypeStruct(s, d) for s, d in outs],
        in_specs=[pl.BlockSpec(memory_space=pltpu.SMEM)] + [spec(i) for i in range(1, len(args))],
        out_specs=[pl.BlockSpec(memory_space=out_space)] * len(outs),
        scratch_shapes=list(scratch),
        compiler_params=pltpu.CompilerParams(vmem_limit_bytes=VMEM_LIMIT),
        cost_estimate=pl.CostEstimate(flops=0, bytes_accessed=0, transcendentals=0),
    )(*args)


def fetch(pairs, sems):
    copies = [pltpu.make_async_copy(source, target, sems.at[i]) for i, (source, target) in enumerate(pairs)]
    for copy in copies:
        copy.start()
    return copies


def flip(value, axis, mask):
    size = lax.axis_size(axis)
    return lax.ppermute(value, axis, [(i, i ^ mask) for i in range(size)])


def after(value, *others):
    return lax.optimization_barrier((value, *others))[0]


def chips_of(shard):
    return lax.optimization_barrier([shard] + [flip(shard, "fsdp", mask) for mask in (2, 4, 6)])


def cores_of(chips):
    others = [flip(part, "fsdp", 1) for part in chips]
    return [part for pair in zip(chips, others) for part in pair]


def summed_on_arrival(value, dim):
    peers = lax.axis_size("fsdp")
    before, behind = (value.shape[:dim], value.shape[dim + 1 :])
    blocks = jnp.moveaxis(value.reshape(*before, peers, -1, *behind), dim, 0)
    blocks = lax.all_to_all(blocks, "fsdp", 0, 0, tiled=True)
    return [jnp.sum(blocks.astype(wide), axis=0)]


def rank_gather(value):
    one, two = flip(value, "tensor", 1), flip(value, "tensor", 2)
    return [value, one, two, flip(two, "tensor", 1)]


def rank_sum(at, slots, *gates):
    three = after(flip(slots[3], "tensor", 1), *gates)
    one = flip(slots[1], "tensor", 1)
    (two,) = kernel_call(add_kernel, [(three.shape, low)], (at, slots[2], three))
    return [slots[0], one, flip(two, "tensor", 2)], two


def to_ranks(slots):
    return [slots[0]] + [flip(slots[j], "tensor", j) for j in (1, 2, 3)]


def norm_parts(values):
    row_mean = jnp.mean(values, axis=-1, keepdims=True)
    centred = values - row_mean
    row_var = jnp.mean(centred * centred, axis=-1, keepdims=True)
    inverse = lax.rsqrt(row_var + norm_eps)
    return centred * inverse, inverse


def norm_backward(grad_out, normed, inverse, gain_vec):
    scaled = grad_out * gain_vec
    return inverse * (
        scaled
        - jnp.mean(scaled, axis=-1, keepdims=True)
        - normed * jnp.mean(scaled * normed, axis=-1, keepdims=True)
    )


def place_rows(at_ref, parts, target, sems):
    if len(parts) == 1:
        return fetch([(parts[0], target)], sems)
    height = parts[0].shape[1]
    spots = [pl.ds(pl.multiple_of((at_ref[0] ^ slot) * height, 32), height) for slot in range(len(parts))]
    return fetch([(part, target.at[:, spot, :]) for part, spot in zip(parts, spots)], sems)


def take_rows(at_ref, source, slot, height):
    start = pl.multiple_of((at_ref[0] ^ slot) * height, 32)
    return source[pl.ds(start, height), :]


def rank_rows(at_ref, slot, height):
    return pl.ds(pl.multiple_of((at_ref[1] ^ slot) * height, 16), height)


def pack_heads(value):
    half = value.shape[0] // 2
    side = value[:, 128:]
    return value[:, :128], jnp.concatenate([side[:half], side[half:]], axis=1)


def unpack_heads(packed):
    rows = packed.shape[0] * 2 // 3
    head, side = packed[:rows], packed[rows:]
    return jnp.concatenate([head, jnp.concatenate([side[:, :64], side[:, 64:]], axis=0)], axis=1)


def two_halves(value):
    upper = value.astype(low)
    return jnp.concatenate([upper.astype(wide), value - upper.astype(wide)], axis=0)


def first_kernel(at_ref, *refs):
    ins, (tile_ref, low_ref, turned_ref), bufs, sems = refs[:4], refs[4:7], refs[7:11], refs[11]
    copies = fetch(list(zip(ins, bufs)), sems)
    vec_buf, bias_buf, qkv_buf, out_buf = bufs
    copies[0].wait()
    copies[1].wait()
    cols, ends = vec_buf.shape[1], bias_buf.shape[1]
    tile = jnp.concatenate(
        [vec_buf[...], jnp.zeros((8, 128 - cols - ends), wide), jnp.broadcast_to(bias_buf[...], (8, ends))], axis=1
    )
    for j in range(tile_ref.shape[0]):
        tile_ref[j] = tile
    copies[2].wait()
    low_ref[...] = qkv_buf[...].astype(low)
    copies[3].wait()
    turned_ref[...] = out_buf[...].T.astype(low)


def small_unpack_kernel(cols, at_ref, small_ref, vec_ref, qv_ref, bias_ref):
    devices = small_ref.shape[0]
    ends = bias_ref.shape[1] * 4 // devices
    share = devices // 4
    vec_ref[...] = jnp.concatenate([small_ref[j, :, :cols] for j in range(devices)], axis=1)
    mine = [small_ref[at_ref[1] * share + j] for j in range(share)]
    qv_ref[...] = jnp.concatenate([tile[:, :cols] for tile in mine], axis=1)
    bias_ref[...] = jnp.concatenate([tile[0:1, 128 - ends :] for tile in mine], axis=1)


def add_kernel(at_ref, left_ref, right_ref, out_ref):
    out_ref[...] = (left_ref[...].astype(wide) + right_ref[...].astype(wide)).astype(out_ref.dtype)


def quad_kernel(at_ref, keep_ref, got_ref, *out_refs):
    for j, ref in enumerate(out_refs):
        ref[...] = (keep_ref[j].astype(wide) + got_ref[j].astype(wide)).astype(ref.dtype)


def ranks_kernel(at_ref, *refs):
    parts, out_refs = refs[:-4], refs[-4:]
    width = out_refs[0].shape[1]
    total = sum(ref[:, : 4 * width].astype(wide) for ref in parts)
    for j, ref in enumerate(out_refs):
        ref[...] = total[:, j * width : (j + 1) * width].astype(low)


def output_kernel(at_ref, own_ref, vec_ref, one_ref, two_ref, three_ref, out_ref):
    total = one_ref[...].astype(wide) + two_ref[...].astype(wide) + three_ref[...].astype(wide)
    out_ref[...] = (own_ref[0] + total + vec_ref[7:8, :]).astype(low)


def sums_pack_kernel(cols, ends, at_ref, one_ref, two_ref, qv_ref, gbo_ref, gub_ref, out_ref):
    devices = out_ref.shape[0]
    share = devices // 4
    middle = jnp.zeros((8, 128 - cols - ends), wide)
    for j in range(devices):
        span = slice(j * cols, (j + 1) * cols)
        mine = (at_ref[1] == j // share).astype(wide)
        k = j % share
        rows = [
            one_ref[0:2, span],
            two_ref[0:2, span],
            qv_ref[0:2, k * cols : (k + 1) * cols] * mine,
            gbo_ref[0:1, span],
            two_ref[2:3, span],
        ]
        bias = gub_ref[0:1, k * ends : (k + 1) * ends] * mine
        out_ref[j] = jnp.concatenate(
            [jnp.concatenate(rows, axis=0), middle, jnp.broadcast_to(bias, (8, ends))], axis=1
        )


def stored(values, bufs, refs, sems):
    for value, buf in zip(values, bufs):
        buf[...] = value
    for copy in fetch(list(zip(bufs, refs)), sems):
        copy.wait()


def small_adam_kernel(at_ref, got_ref, *refs):
    ins, outs, bufs, in_sems, out_sems = refs[:6], refs[6:12], refs[12:18], refs[18], refs[19]
    copies = fetch(list(zip(ins, bufs)), in_sems)
    total = jnp.sum(got_ref[...], axis=0)
    for copy in copies:
        copy.wait()
    cols, ends = bufs[0].shape[1], bufs[3].shape[1]
    vectors, biases = [buf[...] for buf in bufs[:3]], [buf[...] for buf in bufs[3:]]
    states = adamw(vectors[0], total[:, :cols], vectors[1], vectors[2], 0.5, 0.0)
    states += adamw(biases[0], total[0:1, 128 - ends :], biases[1], biases[2], 0.7, 0.0)
    stored(states, bufs, outs, out_sems)


def adam_kernel(n_parts, turned, rates, at_ref, *refs):
    count = len(rates)
    parts, refs = refs[: n_parts * count], refs[n_parts * count :]
    ins, outs, bufs = refs[: 3 * count], refs[3 * count : 6 * count], refs[6 * count : 9 * count]
    in_sems, out_sems = refs[9 * count :]
    copies = fetch(list(zip(ins, bufs)), in_sems)
    states = []
    for j, (rate, decay) in enumerate(rates):
        total = sum(ref[...].astype(wide) for ref in parts[j * n_parts : (j + 1) * n_parts])
        if turned:
            total = total.T
        for copy in copies[3 * j : 3 * j + 3]:
            copy.wait()
        weight, first, second = (buf[...] for buf in bufs[3 * j : 3 * j + 3])
        states += adamw(weight, total, first, second, rate, decay)
    stored(states, bufs, outs, out_sems)


def weights_kernel(at_ref, up_ref, down_ref, *refs):
    parts, (out_ref, up_buf, down_buf, sems) = refs[:4], refs[4:]
    copies = fetch([(up_ref, up_buf), (down_ref, down_buf)], sems)
    out_ref[2] = jnp.concatenate([ref[...] for ref in parts], axis=1)
    copies[0].wait()
    out_ref[0] = up_buf[...].astype(low)
    copies[1].wait()
    out_ref[1] = down_buf[...].astype(low)


def attend_kernel(n_parts, at_ref, x_ref, vec_ref, qv_ref, *refs):
    parts = refs[:n_parts]
    a1_ref, qkv_ref, lse_ref, o_ref, w_ref, ot_ref, sems = refs[n_parts:]
    copies = place_rows(at_ref, parts, w_ref, sems)
    normed, _ = norm_parts(x_ref[...].astype(wide))
    a1 = (normed * vec_ref[0:1, :] + vec_ref[1:2, :]).astype(low)
    a1_ref[...] = a1
    for copy in copies:
        copy.wait()
    q = (dot(a1, w_ref[0]) + qv_ref[4:5, :]).astype(low)
    k = dot(a1, w_ref[1]).astype(low)
    v = (dot(a1, w_ref[2]) + qv_ref[5:6, :]).astype(low)
    qkv_ref[0] = q
    qkv_ref[1] = k
    qkv_ref[2] = v
    vt = v.T
    for head in range(q.shape[1] // HD):
        cols = slice(head * HD, (head + 1) * HD)
        scores = dot(k[:, cols], q[:, cols], NT) * score_scale
        top = jnp.max(scores, axis=0, keepdims=True)
        expos = jnp.exp(scores - top)
        summed = jnp.sum(expos, axis=0, keepdims=True)
        lse_ref[head : head + 1, :] = top + jnp.log(summed)
        ot_ref[cols, :] = dot(vt[cols, :], expos.astype(low)) / summed
    o = ot_ref[...].T.astype(low)
    head_part, side_part = pack_heads(o)
    rows = o.shape[0]
    o_ref[0:rows, :] = head_part
    o_ref[rows:, :] = side_part


def mlp_kernel(n_parts, at_ref, x_ref, c_ref, vec_ref, ub_ref, *refs):
    heads, parts = refs[:4], refs[4 : 4 + n_parts]
    dn2_refs = refs[4 + n_parts : 8 + n_parts]
    (a2_ref, g_ref, du_ref, own_ref, stat_ref, sums_ref, gub_ref, oo_ref,
     w_ref, h_ref, n_ref, s_ref, o_ref, sems) = refs[8 + n_parts :]
    part_rows = dn2_refs[0].shape[0]
    copies = place_rows(at_ref, parts, w_ref, sems)
    o_ref[...] = jnp.concatenate([unpack_heads(ref[...]) for ref in heads], axis=1)
    for copy in copies:
        copy.wait()
    hidden_state = x_ref[...].astype(wide) + dot(o_ref[...], w_ref[2], NT) + vec_ref[6:7, :]
    h_ref[...] = hidden_state
    normed, inverse = norm_parts(hidden_state)
    n_ref[...] = normed
    s_ref[...] = jnp.broadcast_to(inverse, s_ref.shape)
    a2 = (normed * vec_ref[2:3, :] + vec_ref[3:4, :]).astype(low)
    a2_ref[...] = a2
    pre = dot(a2, w_ref[0]) + ub_ref[...]
    square = pre * pre
    tangent = jnp.tanh(gelu_coef * pre * (1.0 + 0.044715 * square))
    half = 0.5 * (1.0 + tangent)
    g_ref[...] = (pre * half).astype(low)
    slope = half + 0.5 * pre * (1.0 - tangent * tangent) * gelu_coef * (1.0 + 3.0 * 0.044715 * square)
    du = (dot(c_ref[...], w_ref[1]) * slope).astype(low)
    du_ref[...] = du
    gub_ref[...] = jnp.sum(du.astype(wide), axis=0, keepdims=True)
    own = rank_rows(at_ref, 0, part_rows)
    own_ref[0] = h_ref[own, :]
    own_ref[1] = n_ref[own, :]
    stat_ref[...] = s_ref[own, :]
    oo_ref[...] = o_ref[own, :]
    dn2 = dot(du, w_ref[0], NT)
    h_ref[...] = dn2
    sums_ref[0:1, :] = jnp.sum(dn2 * normed, axis=0, keepdims=True)
    sums_ref[1:2, :] = jnp.sum(dn2, axis=0, keepdims=True)
    for j, ref in enumerate(dn2_refs):
        ref[...] = h_ref[rank_rows(at_ref, j, part_rows), :].astype(low)
    sums_ref[2:3, :] = jnp.sum(c_ref[own, :].astype(wide), axis=0, keepdims=True)


def mlp_out_kernel(at_ref, g_ref, w_ref, *refs):
    slots, out_ref = refs[:4], refs[4]
    out_ref[...] = dot(g_ref[...], w_ref[1], NT)
    for j, ref in enumerate(slots):
        ref[...] = out_ref[rank_rows(at_ref, j, ref.shape[0]), :].astype(low)


def mix_kernel(at_ref, own_ref, stat_ref, c_ref, vec_ref, w_ref, *refs):
    chunks = refs[:3]
    dh_ref, dz_ref, gbo_ref = refs[3:6]
    do_refs = refs[6:]
    part_rows = stat_ref.shape[0]
    grad = sum(ref[...].astype(wide) for ref in chunks)
    cotan = c_ref[rank_rows(at_ref, 0, part_rows), :].astype(wide)
    dh = cotan + norm_backward(grad, own_ref[1], stat_ref[:, 0:1], vec_ref[2:3, :])
    dh_ref[...] = dh
    gbo_ref[...] = jnp.sum(dh, axis=0, keepdims=True)
    dz = dh.astype(low)
    dz_ref[...] = dz
    do = dot(dz, w_ref[2]).astype(low)
    heads_width = do.shape[1] // 4
    for j, ref in enumerate(do_refs):
        head_part, side_part = pack_heads(do[:, j * heads_width : (j + 1) * heads_width])
        ref[0:part_rows, :] = head_part
        ref[part_rows:, :] = side_part


def attend_back_kernel(fast, at_ref, x_ref, a1_ref, qkv_ref, lse_ref, w_ref, out_grad_ref, *refs):
    chunks, dn1_refs = refs[:4], refs[4:8]
    grad_refs, (sums_ref, qvsum_ref) = refs[8:-7], refs[-7:-5]
    do_ref, dqt_ref, d_ref, g_ref, dn1_ref = refs[-5:]
    rows, width = x_ref.shape
    part_rows = rows // 4
    for j in range(4):
        do_ref[rank_rows(at_ref, j, part_rows), :] = unpack_heads(chunks[j][...])
    q, k, v, do = qkv_ref[0], qkv_ref[1], qkv_ref[2], do_ref[...]
    kt = k.T
    heads_width = q.shape[1]
    for head in range(q.shape[1] // HD):
        cols = slice(head * HD, (head + 1) * HD)
        scores = dot(k[:, cols], q[:, cols], NT) * score_scale
        probs = jnp.exp(scores - lse_ref[head : head + 1, :])
        grad_probs = dot(v[:, cols], do[:, cols], NT)
        d_ref[:, 2 * heads_width + head * HD : 2 * heads_width + (head + 1) * HD] = dot(
            probs.astype(low), do[:, cols]
        ).astype(low)
        both = probs * grad_probs
        grad_scores = (both - probs * jnp.sum(both, axis=0, keepdims=True)).astype(low)
        d_ref[:, heads_width + head * HD : heads_width + (head + 1) * HD] = (
            dot(grad_scores, q[:, cols]) * score_scale
        ).astype(low)
        dqt_ref[cols, :] = dot(kt[cols, :], grad_scores) * score_scale
    d_ref[:, :heads_width] = dqt_ref[...].T.astype(low)
    dq, dk, dv = (d_ref[:, j * heads_width : (j + 1) * heads_width] for j in range(3))
    qvsum_ref[0:1, :] = jnp.sum(dq.astype(wide), axis=0, keepdims=True)
    qvsum_ref[1:2, :] = jnp.sum(dv.astype(wide), axis=0, keepdims=True)
    dn1 = dot(dq, w_ref[0], NT) + dot(dk, w_ref[1], NT) + dot(dv, w_ref[2], NT)
    dn1_ref[...] = dn1
    for j, ref in enumerate(dn1_refs):
        ref[...] = dn1_ref[rank_rows(at_ref, j, part_rows), :].astype(low)
    normed, _ = norm_parts(x_ref[...].astype(wide))
    sums_ref[0:1, :] = jnp.sum(dn1 * normed, axis=0, keepdims=True)
    sums_ref[1:2, :] = jnp.sum(dn1, axis=0, keepdims=True)
    grad = jnp.concatenate([out_grad_ref[...], dot(a1_ref[...].T, d_ref[...]).astype(low)], axis=1)
    if fast:
        g_ref[...] = grad
        cut_blocks(at_ref, g_ref, *grad_refs)
    else:
        grad_refs[0][...] = grad


def cut_blocks(at_ref, source, keep_refs, send_refs):
    height = source.shape[0] // 8
    for slot in range(4):
        keep_refs[slot] = take_rows(at_ref, source, 2 * slot, height)
        send_refs[slot] = take_rows(at_ref, source, 2 * slot + 1, height)


def weight_grad_kernel(at_ref, left_ref, right_ref, out_ref):
    out_ref[...] = dot(left_ref[...].T, right_ref[...]).astype(low)


def mlp_grad_kernel(at_ref, a2_ref, du_ref, c_ref, g_ref, keep_ref, send_ref, grad_ref):
    for j, (left, right) in enumerate(((a2_ref, du_ref), (c_ref, g_ref))):
        grad_ref[j] = dot(left[...].T, right[...]).astype(low)
        cut_blocks(at_ref, grad_ref.at[j], keep_ref.at[:, j], send_ref.at[:, j])


def input_kernel(at_ref, x_ref, dh_ref, vec_ref, *refs):
    chunks, out_ref = refs[:3], refs[3]
    part_rows = dh_ref.shape[0]
    normed, inverse = norm_parts(x_ref[rank_rows(at_ref, 0, part_rows), :].astype(wide))
    grad = sum(ref[...].astype(wide) for ref in chunks)
    out_ref[...] = dh_ref[...] + norm_backward(grad, normed, inverse, vec_ref[0:1, :])


def adamw(weight, gradient, first, second, rate, decay):
    first_new = beta_one * first + (1.0 - beta_one) * gradient
    second_new = beta_two * second + (1.0 - beta_two) * gradient * gradient
    first_hat = first_new / (1.0 - beta_one**STEP)
    second_hat = second_new / (1.0 - beta_two**STEP)
    weight_new = weight - rate * (first_hat / (jnp.sqrt(second_hat) + adam_eps) + decay * weight)
    return (weight_new, first_new, second_new)


def body(
    images,
    cotangent,
    qkv_weight,
    out_weight,
    up_weight,
    down_weight,
    vectors,
    up_bias,
    qkv_first,
    qkv_second,
    out_first,
    out_second,
    up_first,
    up_second,
    down_first,
    down_second,
    vector_first,
    vector_second,
    bias_first,
    bias_second,
):
    fsdp_size = lax.axis_size("fsdp")
    tensor_size = lax.axis_size("tensor")
    devices = fsdp_size * tensor_size
    fast = fsdp_size == 8
    at = jnp.stack([lax.axis_index("fsdp"), lax.axis_index("tensor")]).astype(jnp.int32)
    _, rows, width = images.shape
    hidden = up_weight.shape[1]
    heads_width = width // tensor_size
    part_rows = rows // tensor_size
    height = width // fsdp_size
    x = images.reshape(rows, width)
    c = cotangent.reshape(rows, width)
    cols, ends = vectors.shape[1], up_bias.shape[0]
    both_axes = ("fsdp", "tensor")

    tiles, qkv_low, out_t = kernel_call(
        first_kernel,
        [((devices, 8, 128), wide), (qkv_weight.shape, low), ((height, heads_width), low)],
        (at, vectors, up_bias[None], qkv_weight, out_weight),
        [
            pltpu.VMEM(vectors.shape, wide),
            pltpu.VMEM((1, ends), wide),
            pltpu.VMEM(qkv_weight.shape, wide),
            pltpu.VMEM(out_weight.shape, wide),
            pltpu.SemaphoreType.DMA((4,)),
        ],
        hbm=(1, 2, 3, 4),
    )
    small = lax.all_to_all(tiles, both_axes, 0, 0, tiled=True)
    vec, qv, up_local = kernel_call(
        functools.partial(small_unpack_kernel, cols),
        [((8, width), wide), ((8, heads_width), wide), ((1, hidden), wide)],
        (at, small),
    )

    if fast:
        chips = chips_of(qkv_low)
        qkv_parts = cores_of(chips)
    else:
        chips = qkv_parts = [lax.all_gather(qkv_low, "fsdp", axis=1, tiled=True)]
    (shard,) = kernel_call(
        weights_kernel,
        [((3, height, width), low)],
        (at, after(up_weight, chips[-1]), down_weight.T, *to_ranks([out_t] * 4)),
        [
            pltpu.VMEM(up_weight.shape, wide),
            pltpu.VMEM(up_weight.shape, wide),
            pltpu.SemaphoreType.DMA((2,)),
        ],
        hbm=(1, 2),
    )
    if fast:
        chips = chips_of(shard)

    n = len(qkv_parts)
    a1, qkv, lse, o_mine, qkv_full = kernel_call(
        functools.partial(attend_kernel, n),
        [
            ((rows, width), low),
            ((3, rows, heads_width), low),
            ((8, rows), wide),
            ((rows * 3 // 2, 128), low),
            ((3, width, heads_width), low),
        ],
        (at, x, vec, qv, *qkv_parts),
        [pltpu.VMEM((heads_width, rows), wide), pltpu.SemaphoreType.DMA((n,))],
        free=(4,), hbm=range(5, 4 + n),
    )
    o_parts = rank_gather(o_mine)
    if fast:
        chips = lax.optimization_barrier((*chips, o_parts[1]))[:4]
        rest_parts = cores_of(chips)
    else:
        rest_parts = [lax.all_gather(shard, "fsdp", axis=1, tiled=True)]

    block = ((part_rows, width), low)
    *dn2, a2, g, du, own, stat, sums_two, gub, o_own, w_full = kernel_call(
        functools.partial(mlp_kernel, n),
        [
            *[block] * 4,
            ((rows, width), low),
            ((rows, hidden), low),
            ((rows, hidden), low),
            ((2, part_rows, width), wide),
            ((part_rows, 128), wide),
            ((8, width), wide),
            ((1, hidden), wide),
            block,
            ((3, width, hidden), low),
        ],
        (at, x, c, vec, up_local, *o_parts, *rest_parts),
        [
            pltpu.VMEM((rows, width), wide),
            pltpu.VMEM((rows, width), wide),
            pltpu.VMEM((rows, 128), wide),
            pltpu.VMEM((rows, width), low),
            pltpu.SemaphoreType.DMA((n,)),
        ],
        free=range(9, 9 + n),
    )

    def over_cores(keep, send):
        cut = keep.shape[1:]
        return kernel_call(
            quad_kernel, [(cut, wide)] + [(cut, low)] * 3, (at, keep, flip(send, "fsdp", 1))
        )

    def over_chips(mine, *go):
        return [mine] + [flip(part, "fsdp", mask) for part, mask in zip(go, (2, 4, 6))]

    if fast:
        cut = (4, 2, height, hidden)
        keep, send = kernel_call(
            mlp_grad_kernel, [(cut, low)] * 2, (at, a2, du, c, g), [pltpu.VMEM((2, width, hidden), low)]
        )
        dn2_got, dn2_pair = rank_sum(at, dn2, keep, send)
        mlp_sums = over_chips(*over_cores(keep, after(send, dn2_pair)))
    else:
        (up_grad,) = kernel_call(weight_grad_kernel, [((width, hidden), low)], (at, a2, du))
        (down_grad,) = kernel_call(weight_grad_kernel, [((width, hidden), low)], (at, c, g))
        dn2_got, dn2_pair = rank_sum(at, dn2)
        mlp_sums = summed_on_arrival(jnp.stack([up_grad, down_grad]), 1)
    mlp = kernel_call(
        mlp_out_kernel,
        [block] * 4,
        (at, after(g, dn2_got[1]), w_full),
        [pltpu.VMEM((rows, width), wide)],
    )
    dn2_got = lax.optimization_barrier((dn2_got, mlp, mlp_sums))[0]
    dh, dz, gbo, *do = kernel_call(
        mix_kernel,
        [
            ((part_rows, width), wide),
            block,
            ((1, width), wide),
            *[((part_rows * 3 // 2, 128), low)] * 4,
        ],
        (at, own, stat, c, vec, w_full, *dn2_got),
    )
    do_got = to_ranks(do)
    (out_grad,) = kernel_call(weight_grad_kernel, [((width, width), low)], (at, dz, o_own))

    def update(sums, weight, first, second, rate, decay):
        return adamw(weight, sum(part.astype(wide) for part in sums), first, second, rate, decay)

    mlp_sums = lax.optimization_barrier((mlp_sums, dz))[0]
    up_state = update([part[0] for part in mlp_sums], up_weight, up_first, up_second, 0.08, 0.1)
    down_state = update(
        [part[1] for part in mlp_sums], down_weight.T, down_first.T, down_second.T, 0.045, 0.1
    )
    mlp_three, mlp_one = flip(mlp[3], "tensor", 1), flip(mlp[1], "tensor", 1)
    (mlp_two,) = kernel_call(add_kernel, [block], (at, mlp[2], mlp_three))
    do_got = lax.optimization_barrier((do_got, out_grad, mlp_one, mlp_two, up_state, down_state))[0]
    down_state = [value.T for value in down_state]

    lanes = width + 3 * heads_width
    cut = (4, height, lanes)
    grads = [(cut, low)] * 2 if fast else [((width, lanes), low)]
    *dn1, sums_one, qv_sums = kernel_call(
        functools.partial(attend_back_kernel, fast),
        [*[block] * 4, *grads, ((8, width), wide), ((8, heads_width), wide)],
        (at, x, a1, qkv, lse, qkv_full, out_grad, *do_got),
        [
            pltpu.VMEM((rows, heads_width), low),
            pltpu.VMEM((heads_width, rows), wide),
            pltpu.VMEM((rows, 3 * heads_width), low),
            pltpu.VMEM((width, lanes), low),
            pltpu.VMEM((rows, width), wide),
        ],
    )
    dn1, grads = dn1[:4], dn1[4:]

    if fast:
        sums = over_cores(*grads)
        dn1_got, dn1_pair = rank_sum(at, dn1, *sums)
        sums = over_chips(*sums)
    else:
        dn1_got, dn1_pair = rank_sum(at, dn1)
        sums = summed_on_arrival(grads[0], 0)

    sums_one, mlp_two = lax.optimization_barrier((sums_one, mlp_two, dn1_pair))[:2]
    (tiles,) = kernel_call(
        functools.partial(sums_pack_kernel, cols, ends),
        [((devices, 8, 128), wide)],
        (at, sums_one, sums_two, qv_sums, gbo, gub),
    )
    (output,) = kernel_call(output_kernel, [block], (at, own, vec, mlp[0], mlp_one, flip(mlp_two, "tensor", 2)))
    out_sums = to_ranks(kernel_call(ranks_kernel, [((height, heads_width), low)] * 4, (at, *sums)))
    tiles = lax.all_to_all(tiles, both_axes, 0, 0, tiled=True)
    small_state = (vectors, vector_first, vector_second, up_bias[None], bias_first[None], bias_second[None])
    *vec_state, bias_new, bias_m, bias_s = kernel_call(
        small_adam_kernel,
        [(value.shape, wide) for value in small_state],
        (at, tiles, *small_state),
        [pltpu.VMEM(value.shape, wide) for value in small_state] + [pltpu.SemaphoreType.DMA((6,))] * 2,
        hbm=range(2, 8),
        hbm_outs=True,
    )

    qkv_sums = [
        jnp.stack([part[:, width + j * heads_width : width + (j + 1) * heads_width] for j in range(3)]) for part in sums
    ]
    qkv_state = update(qkv_sums, qkv_weight, qkv_first, qkv_second, 0.08, 0.1)
    out_state = (out_weight, out_first, out_second)
    sems = pltpu.SemaphoreType.DMA((3,))
    out_state = kernel_call(
        functools.partial(adam_kernel, 4, True, ((0.3, 0.1),)),
        [(value.shape, wide) for value in out_state],
        (at, *out_sums, *out_state),
        [pltpu.VMEM(value.shape, wide) for value in out_state] + [sems, sems],
        hbm=range(5, 8),
        hbm_outs=True,
    )

    dn1_got = lax.optimization_barrier((dn1_got, output, qkv_state))[0]
    (input_own,) = kernel_call(
        input_kernel,
        [((part_rows, width), wide)],
        (at, x, dh, vec, *dn1_got),
    )
    return (
        output[None],
        input_own[None],
        *qkv_state,
        *out_state,
        *up_state,
        *down_state,
        *vec_state,
        bias_new[0],
        bias_m[0],
        bias_s[0],
    )


def solution(mesh):
    weights = (P(None, "fsdp", "tensor"), P("tensor", "fsdp"), P("fsdp", "tensor"), P("tensor", "fsdp"))
    vector, bias = P(None, ("fsdp", "tensor")), P(("fsdp", "tensor"))
    twice = [spec for spec in (*weights, vector, bias) for _ in range(2)]
    thrice = [spec for spec in (*weights, vector, bias) for _ in range(3)]
    return jax.shard_map(
        body,
        mesh=mesh,
        in_specs=(P("fsdp", None, None), P("fsdp", None, None), *weights, vector, bias, *twice),
        out_specs=(P("fsdp", "tensor", None), P("fsdp", "tensor", None), *thrice),
        check_vma=False,
    )
```

```python
import functools
import math

import jax
import jax.numpy as jnp
from jax import lax
from jax.experimental import pallas as pl
from jax.experimental.pallas import tpu as pltpu
from jax.sharding import PartitionSpec as P

HD = 64
STEP = 10


norm_eps = 1e-06
beta_one = 0.9
beta_two = 0.999
adam_eps = 1e-08
gelu_coef = math.sqrt(2.0 / math.pi)
score_scale = float(HD) ** (-0.5)
low = jnp.bfloat16
wide = jnp.float32
VMEM_LIMIT = 24 * 1024 * 1024

NN = (((1,), (0,)), ((), ()))
NT = (((1,), (1,)), ((), ()))
TN = (((0,), (0,)), ((), ()))


def dot(left, right, dims=NN):
    return lax.dot_general(left, right, dims, preferred_element_type=wide)


def kernel_call(body, outs, args, scratch=(), hbm=(), free=(), hbm_outs=False):
    def spec(i):
        space = pltpu.HBM if i in hbm else pl.ANY if i in free else pltpu.VMEM
        return pl.BlockSpec(memory_space=space)

    out_space = pltpu.HBM if hbm_outs else pltpu.VMEM
    args = [pltpu.with_memory_space_constraint(arg, pltpu.HBM) if i in hbm else arg for i, arg in enumerate(args)]
    return pl.pallas_call(
        body,
        out_shape=[jax.ShapeDtypeStruct(s, d) for s, d in outs],
        in_specs=[pl.BlockSpec(memory_space=pltpu.SMEM)] + [spec(i) for i in range(1, len(args))],
        out_specs=[pl.BlockSpec(memory_space=out_space)] * len(outs),
        scratch_shapes=list(scratch),
        compiler_params=pltpu.CompilerParams(vmem_limit_bytes=VMEM_LIMIT),
        cost_estimate=pl.CostEstimate(flops=0, bytes_accessed=0, transcendentals=0),
    )(*args)


def fetch(pairs, sems):
    copies = [pltpu.make_async_copy(source, target, sems.at[i]) for i, (source, target) in enumerate(pairs)]
    for copy in copies:
        copy.start()
    return copies


def flip(value, axis, mask):
    size = lax.axis_size(axis)
    return lax.ppermute(value, axis, [(i, i ^ mask) for i in range(size)])


def after(value, *others):
    return lax.optimization_barrier((value, *others))[0]


def chips_of(shard):
    return lax.optimization_barrier([shard] + [flip(shard, "fsdp", mask) for mask in (2, 4, 6)])


def cores_of(chips):
    others = [flip(part, "fsdp", 1) for part in chips]
    return [part for pair in zip(chips, others) for part in pair]


def summed_on_arrival(value, dim):
    peers = lax.axis_size("fsdp")
    before, behind = (value.shape[:dim], value.shape[dim + 1 :])
    blocks = jnp.moveaxis(value.reshape(*before, peers, -1, *behind), dim, 0)
    blocks = lax.all_to_all(blocks, "fsdp", 0, 0, tiled=True)
    return [jnp.sum(blocks.astype(wide), axis=0)]


def rank_gather(value):
    one, two = flip(value, "tensor", 1), flip(value, "tensor", 2)
    return [value, one, two, flip(two, "tensor", 1)]


def rank_sum(at, slots, *gates):
    three = after(flip(slots[3], "tensor", 1), *gates)
    one = flip(slots[1], "tensor", 1)
    (two,) = kernel_call(add_kernel, [(three.shape, low)], (at, slots[2], three))
    return [slots[0], one, flip(two, "tensor", 2)], two


def to_ranks(slots):
    return [slots[0]] + [flip(slots[j], "tensor", j) for j in (1, 2, 3)]


def norm_parts(values):
    row_mean = jnp.mean(values, axis=-1, keepdims=True)
    centred = values - row_mean
    row_var = jnp.mean(centred * centred, axis=-1, keepdims=True)
    inverse = lax.rsqrt(row_var + norm_eps)
    return centred * inverse, inverse


def norm_backward(grad_out, normed, inverse, gain_vec):
    scaled = grad_out * gain_vec
    return inverse * (
        scaled
        - jnp.mean(scaled, axis=-1, keepdims=True)
        - normed * jnp.mean(scaled * normed, axis=-1, keepdims=True)
    )


def place_rows(at_ref, parts, target, sems):
    if len(parts) == 1:
        return fetch([(parts[0], target)], sems)
    height = parts[0].shape[1]
    spots = [pl.ds(pl.multiple_of((at_ref[0] ^ slot) * height, 32), height) for slot in range(len(parts))]
    return fetch([(part, target.at[:, spot, :]) for part, spot in zip(parts, spots)], sems)


def take_rows(at_ref, source, slot, height):
    start = pl.multiple_of((at_ref[0] ^ slot) * height, 32)
    return source[pl.ds(start, height), :]


def rank_rows(at_ref, slot, height):
    return pl.ds(pl.multiple_of((at_ref[1] ^ slot) * height, 16), height)


def pack_heads(value):
    half = value.shape[0] // 2
    side = value[:, 128:]
    return value[:, :128], jnp.concatenate([side[:half], side[half:]], axis=1)


def unpack_heads(packed):
    rows = packed.shape[0] * 2 // 3
    head, side = packed[:rows], packed[rows:]
    return jnp.concatenate([head, jnp.concatenate([side[:, :64], side[:, 64:]], axis=0)], axis=1)


def two_halves(value):
    upper = value.astype(low)
    return jnp.concatenate([upper.astype(wide), value - upper.astype(wide)], axis=0)


def first_kernel(at_ref, *refs):
    ins, (tile_ref, low_ref, turned_ref), bufs, sems = refs[:4], refs[4:7], refs[7:11], refs[11]
    copies = fetch(list(zip(ins, bufs)), sems)
    vec_buf, bias_buf, qkv_buf, out_buf = bufs
    copies[0].wait()
    copies[1].wait()
    cols, ends = vec_buf.shape[1], bias_buf.shape[1]
    tile = jnp.concatenate(
        [vec_buf[...], jnp.zeros((8, 128 - cols - ends), wide), jnp.broadcast_to(bias_buf[...], (8, ends))], axis=1
    )
    for j in range(tile_ref.shape[0]):
        tile_ref[j] = tile
    copies[2].wait()
    low_ref[...] = qkv_buf[...].astype(low)
    copies[3].wait()
    turned_ref[...] = out_buf[...].T.astype(low)


def small_unpack_kernel(cols, at_ref, small_ref, vec_ref, qv_ref, bias_ref):
    devices = small_ref.shape[0]
    ends = bias_ref.shape[1] * 4 // devices
    share = devices // 4
    vec_ref[...] = jnp.concatenate([small_ref[j, :, :cols] for j in range(devices)], axis=1)
    mine = [small_ref[at_ref[1] * share + j] for j in range(share)]
    qv_ref[...] = jnp.concatenate([tile[:, :cols] for tile in mine], axis=1)
    bias_ref[...] = jnp.concatenate([tile[0:1, 128 - ends :] for tile in mine], axis=1)


def add_kernel(at_ref, left_ref, right_ref, out_ref):
    out_ref[...] = (left_ref[...].astype(wide) + right_ref[...].astype(wide)).astype(out_ref.dtype)


def quad_kernel(at_ref, keep_ref, got_ref, *out_refs):
    for j, ref in enumerate(out_refs):
        ref[...] = (keep_ref[j].astype(wide) + got_ref[j].astype(wide)).astype(ref.dtype)


def ranks_kernel(at_ref, *refs):
    parts, out_refs = refs[:-4], refs[-4:]
    width = out_refs[0].shape[1]
    total = sum(ref[...].astype(wide) for ref in parts)
    height = total.shape[0]
    for j, ref in enumerate(out_refs):
        ref[0:height, :] = total[:, j * width : (j + 1) * width].astype(low)
        if ref.shape[0] > height:
            small = total[0:16, 4 * width : 4 * width + 96]
            cols = 96 // 4
            vec = jnp.zeros((16, cols), wide)
            bias = jnp.zeros((1, 96), wide)
            for other in range(4):
                here = ((at_ref[1] ^ j) == other).astype(wide)
                vec += small[:, other * cols : (other + 1) * cols] * here
                bias += small[8 + other : 9 + other, :] * here
            ref[height:, :] = jnp.concatenate(
                [vec, jnp.zeros((16, width - cols - 96), wide), jnp.broadcast_to(bias, (16, 96))], axis=1
            ).astype(low)


def last_kernel(at_ref, *refs):
    parts, ins, outs, bufs, (in_sems, out_sems) = refs[:4], refs[4:13], refs[13:22], refs[22:31], refs[31:]
    copies = fetch(list(zip(ins, bufs)), in_sems)
    total = sum(ref[...].astype(wide) for ref in parts)
    height, cols, ends = bufs[0].shape[1], bufs[3].shape[1], bufs[6].shape[1]
    small = total[height : height + 8]
    grads = (total[0:height].T, small[:, :cols], small[0:1, total.shape[1] - ends :])
    for copy in copies:
        copy.wait()
    states = []
    for j, (rate, decay) in enumerate(((0.3, 0.1), (0.5, 0.0), (0.7, 0.0))):
        weight, first, second = (buf[...] for buf in bufs[3 * j : 3 * j + 3])
        states += adamw(weight, grads[j], first, second, rate, decay)
    stored(states, bufs, outs, out_sems)


def output_kernel(at_ref, own_ref, vec_ref, one_ref, two_ref, three_ref, out_ref):
    total = one_ref[...].astype(wide) + two_ref[...].astype(wide) + three_ref[...].astype(wide)
    out_ref[...] = (own_ref[0] + total + vec_ref[7:8, :]).astype(low)


def sums_pack_kernel(cols, ends, at_ref, one_ref, two_ref, qv_ref, gbo_ref, gub_ref, out_ref):
    devices = out_ref.shape[0]
    share = devices // 4
    middle = jnp.zeros((8, 128 - cols - ends), wide)
    for j in range(devices):
        span = slice(j * cols, (j + 1) * cols)
        mine = (at_ref[1] == j // share).astype(wide)
        k = j % share
        rows = [
            one_ref[0:2, span],
            two_ref[0:2, span],
            qv_ref[0:2, k * cols : (k + 1) * cols] * mine,
            gbo_ref[0:1, span],
            two_ref[2:3, span],
        ]
        bias = gub_ref[0:1, k * ends : (k + 1) * ends] * mine
        out_ref[j] = jnp.concatenate(
            [jnp.concatenate(rows, axis=0), middle, jnp.broadcast_to(bias, (8, ends))], axis=1
        )


def stored(values, bufs, refs, sems):
    for value, buf in zip(values, bufs):
        buf[...] = value
    for copy in fetch(list(zip(bufs, refs)), sems):
        copy.wait()


def small_adam_kernel(at_ref, got_ref, *refs):
    ins, outs, bufs, in_sems, out_sems = refs[:6], refs[6:12], refs[12:18], refs[18], refs[19]
    copies = fetch(list(zip(ins, bufs)), in_sems)
    total = jnp.sum(got_ref[...], axis=0)
    for copy in copies:
        copy.wait()
    cols, ends = bufs[0].shape[1], bufs[3].shape[1]
    vectors, biases = [buf[...] for buf in bufs[:3]], [buf[...] for buf in bufs[3:]]
    states = adamw(vectors[0], total[:, :cols], vectors[1], vectors[2], 0.5, 0.0)
    states += adamw(biases[0], total[0:1, 128 - ends :], biases[1], biases[2], 0.7, 0.0)
    stored(states, bufs, outs, out_sems)


def adam_kernel(n_parts, turned, rates, at_ref, *refs):
    count = len(rates)
    parts, refs = refs[: n_parts * count], refs[n_parts * count :]
    ins, outs, bufs = refs[: 3 * count], refs[3 * count : 6 * count], refs[6 * count : 9 * count]
    in_sems, out_sems = refs[9 * count :]
    copies = fetch(list(zip(ins, bufs)), in_sems)
    states = []
    for j, (rate, decay) in enumerate(rates):
        total = sum(ref[...].astype(wide) for ref in parts[j * n_parts : (j + 1) * n_parts])
        if turned:
            total = total.T
        for copy in copies[3 * j : 3 * j + 3]:
            copy.wait()
        weight, first, second = (buf[...] for buf in bufs[3 * j : 3 * j + 3])
        states += adamw(weight, total, first, second, rate, decay)
    stored(states, bufs, outs, out_sems)


def weights_kernel(at_ref, up_ref, down_ref, *refs):
    parts, (out_ref, up_buf, down_buf, sems) = refs[:4], refs[4:]
    copies = fetch([(up_ref, up_buf), (down_ref, down_buf)], sems)
    out_ref[2] = jnp.concatenate([ref[...] for ref in parts], axis=1)
    copies[0].wait()
    out_ref[0] = up_buf[...].astype(low)
    copies[1].wait()
    out_ref[1] = down_buf[...].astype(low)


def attend_kernel(n_parts, at_ref, x_ref, vec_ref, qv_ref, *refs):
    parts = refs[:n_parts]
    a1_ref, qkv_ref, lse_ref, o_ref, w_ref, ot_ref, sems = refs[n_parts:]
    copies = place_rows(at_ref, parts, w_ref, sems)
    normed, _ = norm_parts(x_ref[...].astype(wide))
    a1 = (normed * vec_ref[0:1, :] + vec_ref[1:2, :]).astype(low)
    a1_ref[...] = a1
    for copy in copies:
        copy.wait()
    q = (dot(a1, w_ref[0]) + qv_ref[4:5, :]).astype(low)
    k = dot(a1, w_ref[1]).astype(low)
    v = (dot(a1, w_ref[2]) + qv_ref[5:6, :]).astype(low)
    qkv_ref[0] = q
    qkv_ref[1] = k
    qkv_ref[2] = v
    vt = v.T
    for head in range(q.shape[1] // HD):
        cols = slice(head * HD, (head + 1) * HD)
        scores = dot(k[:, cols], q[:, cols], NT) * score_scale
        top = jnp.max(scores, axis=0, keepdims=True)
        expos = jnp.exp(scores - top)
        summed = jnp.sum(expos, axis=0, keepdims=True)
        lse_ref[head : head + 1, :] = top + jnp.log(summed)
        ot_ref[cols, :] = dot(vt[cols, :], expos.astype(low)) / summed
    o = ot_ref[...].T.astype(low)
    head_part, side_part = pack_heads(o)
    rows = o.shape[0]
    o_ref[0:rows, :] = head_part
    o_ref[rows:, :] = side_part


def mlp_kernel(n_parts, at_ref, x_ref, c_ref, vec_ref, ub_ref, *refs):
    heads, parts = refs[:4], refs[4 : 4 + n_parts]
    dn2_refs = refs[4 + n_parts : 8 + n_parts]
    (a2_ref, g_ref, du_ref, own_ref, stat_ref, sums_ref, gub_ref, oo_ref,
     w_ref, h_ref, n_ref, s_ref, o_ref, sems) = refs[8 + n_parts :]
    part_rows = dn2_refs[0].shape[0]
    copies = place_rows(at_ref, parts, w_ref, sems)
    o_ref[...] = jnp.concatenate([unpack_heads(ref[...]) for ref in heads], axis=1)
    for copy in copies:
        copy.wait()
    hidden_state = x_ref[...].astype(wide) + dot(o_ref[...], w_ref[2], NT) + vec_ref[6:7, :]
    h_ref[...] = hidden_state
    normed, inverse = norm_parts(hidden_state)
    n_ref[...] = normed
    s_ref[...] = jnp.broadcast_to(inverse, s_ref.shape)
    a2 = (normed * vec_ref[2:3, :] + vec_ref[3:4, :]).astype(low)
    a2_ref[...] = a2
    pre = dot(a2, w_ref[0]) + ub_ref[...]
    square = pre * pre
    tangent = jnp.tanh(gelu_coef * pre * (1.0 + 0.044715 * square))
    half = 0.5 * (1.0 + tangent)
    g_ref[...] = (pre * half).astype(low)
    slope = half + 0.5 * pre * (1.0 - tangent * tangent) * gelu_coef * (1.0 + 3.0 * 0.044715 * square)
    du = (dot(c_ref[...], w_ref[1]) * slope).astype(low)
    du_ref[...] = du
    gub_ref[...] = jnp.sum(du.astype(wide), axis=0, keepdims=True)
    own = rank_rows(at_ref, 0, part_rows)
    own_ref[0] = h_ref[own, :]
    own_ref[1] = n_ref[own, :]
    stat_ref[...] = s_ref[own, :]
    oo_ref[...] = o_ref[own, :]
    dn2 = dot(du, w_ref[0], NT)
    h_ref[...] = dn2
    sums_ref[0:1, :] = jnp.sum(dn2 * normed, axis=0, keepdims=True)
    sums_ref[1:2, :] = jnp.sum(dn2, axis=0, keepdims=True)
    for j, ref in enumerate(dn2_refs):
        ref[...] = h_ref[rank_rows(at_ref, j, part_rows), :].astype(low)
    sums_ref[2:3, :] = jnp.sum(c_ref[own, :].astype(wide), axis=0, keepdims=True)


def mlp_out_kernel(at_ref, g_ref, w_ref, *refs):
    slots, out_ref = refs[:4], refs[4]
    out_ref[...] = dot(g_ref[...], w_ref[1], NT)
    for j, ref in enumerate(slots):
        ref[...] = out_ref[rank_rows(at_ref, j, ref.shape[0]), :].astype(low)


def mix_kernel(at_ref, own_ref, stat_ref, c_ref, vec_ref, w_ref, *refs):
    chunks = refs[:3]
    dh_ref, dz_ref, gbo_ref = refs[3:6]
    do_refs = refs[6:]
    part_rows = stat_ref.shape[0]
    grad = sum(ref[...].astype(wide) for ref in chunks)
    cotan = c_ref[rank_rows(at_ref, 0, part_rows), :].astype(wide)
    dh = cotan + norm_backward(grad, own_ref[1], stat_ref[:, 0:1], vec_ref[2:3, :])
    dh_ref[...] = dh
    gbo_ref[...] = jnp.sum(dh, axis=0, keepdims=True)
    dz = dh.astype(low)
    dz_ref[...] = dz
    do = dot(dz, w_ref[2]).astype(low)
    heads_width = do.shape[1] // 4
    for j, ref in enumerate(do_refs):
        head_part, side_part = pack_heads(do[:, j * heads_width : (j + 1) * heads_width])
        ref[0:part_rows, :] = head_part
        ref[part_rows:, :] = side_part


def attend_back_kernel(fast, at_ref, x_ref, a1_ref, qkv_ref, lse_ref, w_ref, out_grad_ref, *refs):
    if fast:
        (two_ref, gbo_ref, gub_ref), refs = refs[:3], refs[3:]
    chunks, dn1_refs = refs[:4], refs[4:8]
    grad_refs, (sums_ref, qvsum_ref) = refs[8:-7], refs[-7:-5]
    do_ref, dqt_ref, d_ref, g_ref, dn1_ref = refs[-5:]
    rows, width = x_ref.shape
    part_rows = rows // 4
    for j in range(4):
        do_ref[rank_rows(at_ref, j, part_rows), :] = unpack_heads(chunks[j][...])
    q, k, v, do = qkv_ref[0], qkv_ref[1], qkv_ref[2], do_ref[...]
    kt = k.T
    heads_width = q.shape[1]
    for head in range(q.shape[1] // HD):
        cols = slice(head * HD, (head + 1) * HD)
        scores = dot(k[:, cols], q[:, cols], NT) * score_scale
        probs = jnp.exp(scores - lse_ref[head : head + 1, :])
        grad_probs = dot(v[:, cols], do[:, cols], NT)
        d_ref[:, 2 * heads_width + head * HD : 2 * heads_width + (head + 1) * HD] = dot(
            probs.astype(low), do[:, cols]
        ).astype(low)
        both = probs * grad_probs
        grad_scores = (both - probs * jnp.sum(both, axis=0, keepdims=True)).astype(low)
        d_ref[:, heads_width + head * HD : heads_width + (head + 1) * HD] = (
            dot(grad_scores, q[:, cols]) * score_scale
        ).astype(low)
        dqt_ref[cols, :] = dot(kt[cols, :], grad_scores) * score_scale
    d_ref[:, :heads_width] = dqt_ref[...].T.astype(low)
    dq, dk, dv = (d_ref[:, j * heads_width : (j + 1) * heads_width] for j in range(3))
    qvsum_ref[0:1, :] = jnp.sum(dq.astype(wide), axis=0, keepdims=True)
    qvsum_ref[1:2, :] = jnp.sum(dv.astype(wide), axis=0, keepdims=True)
    dn1 = dot(dq, w_ref[0], NT) + dot(dk, w_ref[1], NT) + dot(dv, w_ref[2], NT)
    dn1_ref[...] = dn1
    for j, ref in enumerate(dn1_refs):
        ref[...] = dn1_ref[rank_rows(at_ref, j, part_rows), :].astype(low)
    normed, _ = norm_parts(x_ref[...].astype(wide))
    sums_ref[0:1, :] = jnp.sum(dn1 * normed, axis=0, keepdims=True)
    sums_ref[1:2, :] = jnp.sum(dn1, axis=0, keepdims=True)
    g_ref[:, :width] = out_grad_ref[...]
    g_ref[:, g_ref.shape[1] - 3 * heads_width :] = dot(a1_ref[...].T, d_ref[...]).astype(low)
    if not fast:
        grad_refs[0][...] = g_ref[...]
        return
    height = width // 8
    ends = gub_ref.shape[1] // 8
    for j in range(8):
        span, half = slice(j * height, (j + 1) * height), j % 2
        here = (at_ref[1] == j // 2).astype(wide)
        rows_in = [
            sums_ref[0:2, span],
            two_ref[0:2, span],
            qvsum_ref[0:2, half * height : (half + 1) * height] * here,
            gbo_ref[0:1, span],
            two_ref[2:3, span],
        ]
        rows_in += [gub_ref[0:1, (4 * half + k) * ends : (4 * half + k + 1) * ends] * here for k in range(4)]
        rows_in += [jnp.zeros((4, height), wide)]
        small = jnp.concatenate(rows_in, axis=0)
        g_ref[j * height : j * height + 16, width : width + 128] = jnp.concatenate(
            [small, jnp.zeros((16, 128 - height), wide)], axis=1
        ).astype(low)
    cut_blocks(at_ref, g_ref, *grad_refs)


def cut_blocks(at_ref, source, keep_refs, send_refs):
    height = source.shape[0] // 8
    for slot in range(4):
        keep_refs[slot] = take_rows(at_ref, source, 2 * slot, height)
        send_refs[slot] = take_rows(at_ref, source, 2 * slot + 1, height)


def weight_grad_kernel(at_ref, left_ref, right_ref, out_ref):
    out_ref[...] = dot(left_ref[...].T, right_ref[...]).astype(low)


def mlp_grad_kernel(at_ref, a2_ref, du_ref, c_ref, g_ref, keep_ref, send_ref, grad_ref):
    for j, (left, right) in enumerate(((a2_ref, du_ref), (c_ref, g_ref))):
        grad_ref[j] = dot(left[...].T, right[...]).astype(low)
        cut_blocks(at_ref, grad_ref.at[j], keep_ref.at[:, j], send_ref.at[:, j])


def input_kernel(at_ref, x_ref, dh_ref, vec_ref, *refs):
    chunks, out_ref = refs[:3], refs[3]
    part_rows = dh_ref.shape[0]
    normed, inverse = norm_parts(x_ref[rank_rows(at_ref, 0, part_rows), :].astype(wide))
    grad = sum(ref[...].astype(wide) for ref in chunks)
    out_ref[...] = dh_ref[...] + norm_backward(grad, normed, inverse, vec_ref[0:1, :])


def adamw(weight, gradient, first, second, rate, decay):
    first_new = beta_one * first + (1.0 - beta_one) * gradient
    second_new = beta_two * second + (1.0 - beta_two) * gradient * gradient
    first_hat = first_new / (1.0 - beta_one**STEP)
    second_hat = second_new / (1.0 - beta_two**STEP)
    weight_new = weight - rate * (first_hat / (jnp.sqrt(second_hat) + adam_eps) + decay * weight)
    return (weight_new, first_new, second_new)


def body(
    images,
    cotangent,
    qkv_weight,
    out_weight,
    up_weight,
    down_weight,
    vectors,
    up_bias,
    qkv_first,
    qkv_second,
    out_first,
    out_second,
    up_first,
    up_second,
    down_first,
    down_second,
    vector_first,
    vector_second,
    bias_first,
    bias_second,
):
    fsdp_size = lax.axis_size("fsdp")
    tensor_size = lax.axis_size("tensor")
    devices = fsdp_size * tensor_size
    fast = fsdp_size == 8
    at = jnp.stack([lax.axis_index("fsdp"), lax.axis_index("tensor")]).astype(jnp.int32)
    _, rows, width = images.shape
    hidden = up_weight.shape[1]
    heads_width = width // tensor_size
    part_rows = rows // tensor_size
    height = width // fsdp_size
    x = images.reshape(rows, width)
    c = cotangent.reshape(rows, width)
    cols, ends = vectors.shape[1], up_bias.shape[0]
    both_axes = ("fsdp", "tensor")

    tiles, qkv_low, out_t = kernel_call(
        first_kernel,
        [((devices, 8, 128), wide), (qkv_weight.shape, low), ((height, heads_width), low)],
        (at, vectors, up_bias[None], qkv_weight, out_weight),
        [
            pltpu.VMEM(vectors.shape, wide),
            pltpu.VMEM((1, ends), wide),
            pltpu.VMEM(qkv_weight.shape, wide),
            pltpu.VMEM(out_weight.shape, wide),
            pltpu.SemaphoreType.DMA((4,)),
        ],
        hbm=(1, 2, 3, 4),
    )
    small = lax.all_to_all(tiles, both_axes, 0, 0, tiled=True)
    vec, qv, up_local = kernel_call(
        functools.partial(small_unpack_kernel, cols),
        [((8, width), wide), ((8, heads_width), wide), ((1, hidden), wide)],
        (at, small),
    )

    if fast:
        chips = chips_of(qkv_low)
        qkv_parts = cores_of(chips)
    else:
        chips = qkv_parts = [lax.all_gather(qkv_low, "fsdp", axis=1, tiled=True)]
    (shard,) = kernel_call(
        weights_kernel,
        [((3, height, width), low)],
        (at, after(up_weight, chips[-1]), down_weight.T, *to_ranks([out_t] * 4)),
        [
            pltpu.VMEM(up_weight.shape, wide),
            pltpu.VMEM(up_weight.shape, wide),
            pltpu.SemaphoreType.DMA((2,)),
        ],
        hbm=(1, 2),
    )
    if fast:
        chips = chips_of(shard)

    n = len(qkv_parts)
    a1, qkv, lse, o_mine, qkv_full = kernel_call(
        functools.partial(attend_kernel, n),
        [
            ((rows, width), low),
            ((3, rows, heads_width), low),
            ((8, rows), wide),
            ((rows * 3 // 2, 128), low),
            ((3, width, heads_width), low),
        ],
        (at, x, vec, qv, *qkv_parts),
        [pltpu.VMEM((heads_width, rows), wide), pltpu.SemaphoreType.DMA((n,))],
        free=(4,), hbm=range(5, 4 + n),
    )
    o_parts = rank_gather(o_mine)
    if fast:
        chips = lax.optimization_barrier((*chips, o_parts[1]))[:4]
        rest_parts = cores_of(chips)
    else:
        rest_parts = [lax.all_gather(shard, "fsdp", axis=1, tiled=True)]

    block = ((part_rows, width), low)
    *dn2, a2, g, du, own, stat, sums_two, gub, o_own, w_full = kernel_call(
        functools.partial(mlp_kernel, n),
        [
            *[block] * 4,
            ((rows, width), low),
            ((rows, hidden), low),
            ((rows, hidden), low),
            ((2, part_rows, width), wide),
            ((part_rows, 128), wide),
            ((8, width), wide),
            ((1, hidden), wide),
            block,
            ((3, width, hidden), low),
        ],
        (at, x, c, vec, up_local, *o_parts, *rest_parts),
        [
            pltpu.VMEM((rows, width), wide),
            pltpu.VMEM((rows, width), wide),
            pltpu.VMEM((rows, 128), wide),
            pltpu.VMEM((rows, width), low),
            pltpu.SemaphoreType.DMA((n,)),
        ],
        free=range(9, 9 + n),
    )

    def over_cores(keep, send):
        cut = keep.shape[1:]
        return kernel_call(
            quad_kernel, [(cut, wide)] + [(cut, low)] * 3, (at, keep, flip(send, "fsdp", 1))
        )

    def over_chips(mine, *go):
        return [mine] + [flip(part, "fsdp", mask) for part, mask in zip(go, (2, 4, 6))]

    if fast:
        cut = (4, 2, height, hidden)
        keep, send = kernel_call(
            mlp_grad_kernel, [(cut, low)] * 2, (at, a2, du, c, g), [pltpu.VMEM((2, width, hidden), low)]
        )
        dn2_got, dn2_pair = rank_sum(at, dn2, keep, send)
        mlp_sums = over_chips(*over_cores(keep, after(send, dn2_pair)))
    else:
        (up_grad,) = kernel_call(weight_grad_kernel, [((width, hidden), low)], (at, a2, du))
        (down_grad,) = kernel_call(weight_grad_kernel, [((width, hidden), low)], (at, c, g))
        dn2_got, dn2_pair = rank_sum(at, dn2)
        mlp_sums = summed_on_arrival(jnp.stack([up_grad, down_grad]), 1)
    mlp = kernel_call(
        mlp_out_kernel,
        [block] * 4,
        (at, after(g, dn2_pair), w_full),
        [pltpu.VMEM((rows, width), wide)],
    )
    dn2_got = lax.optimization_barrier((dn2_got, mlp, mlp_sums))[0]
    dh, dz, gbo, *do = kernel_call(
        mix_kernel,
        [
            ((part_rows, width), wide),
            block,
            ((1, width), wide),
            *[((part_rows * 3 // 2, 128), low)] * 4,
        ],
        (at, own, stat, c, vec, w_full, *dn2_got),
    )
    do_got = to_ranks(do)
    (out_grad,) = kernel_call(weight_grad_kernel, [((width, width), low)], (at, dz, o_own))

    def update(sums, weight, first, second, rate, decay):
        return adamw(weight, sum(part.astype(wide) for part in sums), first, second, rate, decay)

    mlp_sums = lax.optimization_barrier((mlp_sums, dz))[0]
    up_state = update([part[0] for part in mlp_sums], up_weight, up_first, up_second, 0.08, 0.1)
    down_state = update(
        [part[1] for part in mlp_sums], down_weight.T, down_first.T, down_second.T, 0.045, 0.1
    )
    mlp_three, mlp_one = flip(mlp[3], "tensor", 1), flip(mlp[1], "tensor", 1)
    (mlp_two,) = kernel_call(add_kernel, [block], (at, mlp[2], mlp_three))
    mlp_two = flip(mlp_two, "tensor", 2)
    do_got = lax.optimization_barrier((do_got, out_grad, mlp_one, mlp_two, up_state, down_state))[0]
    down_state = [value.T for value in down_state]

    lanes = width + 3 * heads_width + (128 if fast else 0)
    extra = (sums_two, gbo, gub) if fast else ()
    cut = (4, height, lanes)
    grads = [(cut, low)] * 2 if fast else [((width, lanes), low)]
    *dn1, sums_one, qv_sums = kernel_call(
        functools.partial(attend_back_kernel, fast),
        [*[block] * 4, *grads, ((8, width), wide), ((8, heads_width), wide)],
        (at, x, a1, qkv, lse, qkv_full, out_grad, *extra, *do_got),
        [
            pltpu.VMEM((rows, heads_width), low),
            pltpu.VMEM((heads_width, rows), wide),
            pltpu.VMEM((rows, 3 * heads_width), low),
            pltpu.VMEM((width, lanes), low),
            pltpu.VMEM((rows, width), wide),
        ],
    )
    dn1, grads = dn1[:4], dn1[4:]

    if fast:
        sums = over_cores(*grads)
        dn1_got, dn1_pair = rank_sum(at, dn1, *sums)
        sums = over_chips(*sums)
    else:
        dn1_got, dn1_pair = rank_sum(at, dn1)
        sums = summed_on_arrival(grads[0], 0)

    (output,) = kernel_call(output_kernel, [block], (at, own, vec, mlp[0], mlp_one, mlp_two))
    qkv_sums = [
        jnp.stack([part[:, lanes - j * heads_width : lanes - (j - 1) * heads_width] for j in (3, 2, 1)]) for part in sums
    ]
    qkv_state = update(qkv_sums, qkv_weight, qkv_first, qkv_second, 0.08, 0.1)

    tall = height + (16 if fast else 0)
    out_sums = to_ranks(kernel_call(ranks_kernel, [((tall, heads_width), low)] * 4, (at, *sums)))
    out_state = (out_weight, out_first, out_second)
    small_state = (vectors, vector_first, vector_second, up_bias[None], bias_first[None], bias_second[None])
    if fast:
        states = out_state + small_state
        *last, bias_new, bias_m, bias_s = kernel_call(
            last_kernel,
            [(value.shape, wide) for value in states],
            (at, *out_sums, *states),
            [pltpu.VMEM(value.shape, wide) for value in states] + [pltpu.SemaphoreType.DMA((9,))] * 2,
            hbm=range(5, 14),
            hbm_outs=True,
        )
        out_state, vec_state = last[:3], last[3:]
    else:
        (tiles,) = kernel_call(
            functools.partial(sums_pack_kernel, cols, ends),
            [((devices, 8, 128), wide)],
            (at, sums_one, sums_two, qv_sums, gbo, gub),
        )
        tiles = lax.all_to_all(tiles, both_axes, 0, 0, tiled=True)
        *vec_state, bias_new, bias_m, bias_s = kernel_call(
            small_adam_kernel,
            [(value.shape, wide) for value in small_state],
            (at, tiles, *small_state),
            [pltpu.VMEM(value.shape, wide) for value in small_state] + [pltpu.SemaphoreType.DMA((6,))] * 2,
            hbm=range(2, 8),
            hbm_outs=True,
        )
        out_state = kernel_call(
            functools.partial(adam_kernel, 4, True, ((0.3, 0.1),)),
            [(value.shape, wide) for value in out_state],
            (at, *out_sums, *out_state),
            [pltpu.VMEM(value.shape, wide) for value in out_state] + [pltpu.SemaphoreType.DMA((3,))] * 2,
            hbm=range(5, 8),
            hbm_outs=True,
        )

    dn1_got = lax.optimization_barrier((dn1_got, output, qkv_state))[0]
    (input_own,) = kernel_call(
        input_kernel,
        [((part_rows, width), wide)],
        (at, x, dh, vec, *dn1_got),
    )
    return (
        output[None],
        input_own[None],
        *qkv_state,
        *out_state,
        *up_state,
        *down_state,
        *vec_state,
        bias_new[0],
        bias_m[0],
        bias_s[0],
    )


def solution(mesh):
    weights = (P(None, "fsdp", "tensor"), P("tensor", "fsdp"), P("fsdp", "tensor"), P("tensor", "fsdp"))
    vector, bias = P(None, ("fsdp", "tensor")), P(("fsdp", "tensor"))
    twice = [spec for spec in (*weights, vector, bias) for _ in range(2)]
    thrice = [spec for spec in (*weights, vector, bias) for _ in range(3)]
    return jax.shard_map(
        body,
        mesh=mesh,
        in_specs=(P("fsdp", None, None), P("fsdp", None, None), *weights, vector, bias, *twice),
        out_specs=(P("fsdp", "tensor", None), P("fsdp", "tensor", None), *thrice),
        check_vma=False,
    )
```

```python
import functools
import math

import jax
import jax.numpy as jnp
from jax import lax
from jax.experimental import pallas as pl
from jax.experimental.pallas import tpu as pltpu
from jax.sharding import PartitionSpec as P

HD = 64
STEP = 10


norm_eps = 1e-06
beta_one = 0.9
beta_two = 0.999
adam_eps = 1e-08
gelu_coef = math.sqrt(2.0 / math.pi)
score_scale = float(HD) ** (-0.5)
low = jnp.bfloat16
wide = jnp.float32
VMEM_LIMIT = 24 * 1024 * 1024

NN = (((1,), (0,)), ((), ()))
NT = (((1,), (1,)), ((), ()))
TN = (((0,), (0,)), ((), ()))


def dot(left, right, dims=NN):
    return lax.dot_general(left, right, dims, preferred_element_type=wide)


def kernel_call(body, outs, args, scratch=(), hbm=(), free=(), hbm_outs=False):
    def spec(i):
        space = pltpu.HBM if i in hbm else pl.ANY if i in free else pltpu.VMEM
        return pl.BlockSpec(memory_space=space)

    out_space = pltpu.HBM if hbm_outs else pltpu.VMEM
    args = [pltpu.with_memory_space_constraint(arg, pltpu.HBM) if i in hbm else arg for i, arg in enumerate(args)]
    return pl.pallas_call(
        body,
        out_shape=[jax.ShapeDtypeStruct(s, d) for s, d in outs],
        in_specs=[pl.BlockSpec(memory_space=pltpu.SMEM)] + [spec(i) for i in range(1, len(args))],
        out_specs=[pl.BlockSpec(memory_space=out_space)] * len(outs),
        scratch_shapes=list(scratch),
        compiler_params=pltpu.CompilerParams(vmem_limit_bytes=VMEM_LIMIT),
        cost_estimate=pl.CostEstimate(flops=0, bytes_accessed=0, transcendentals=0),
    )(*args)


def fetch(pairs, sems):
    copies = [pltpu.make_async_copy(source, target, sems.at[i]) for i, (source, target) in enumerate(pairs)]
    for copy in copies:
        copy.start()
    return copies


def flip(value, axis, mask):
    size = lax.axis_size(axis)
    return lax.ppermute(value, axis, [(i, i ^ mask) for i in range(size)])


def after(value, *others):
    return lax.optimization_barrier((value, *others))[0]


def chips_of(shard):
    return lax.optimization_barrier([shard] + [flip(shard, "fsdp", mask) for mask in (2, 4, 6)])


def cores_of(chips):
    others = [flip(part, "fsdp", 1) for part in chips]
    return [part for pair in zip(chips, others) for part in pair]


def summed_on_arrival(value, dim):
    peers = lax.axis_size("fsdp")
    before, behind = (value.shape[:dim], value.shape[dim + 1 :])
    blocks = jnp.moveaxis(value.reshape(*before, peers, -1, *behind), dim, 0)
    blocks = lax.all_to_all(blocks, "fsdp", 0, 0, tiled=True)
    return [jnp.sum(blocks.astype(wide), axis=0)]


def rank_gather(value):
    one, two = flip(value, "tensor", 1), flip(value, "tensor", 2)
    return [value, one, two, flip(two, "tensor", 1)]


def rank_sum(at, slots, *gates):
    three = after(flip(slots[3], "tensor", 1), *gates)
    one = flip(slots[1], "tensor", 1)
    (two,) = kernel_call(add_kernel, [(three.shape, low)], (at, slots[2], three))
    return [slots[0], one, flip(two, "tensor", 2)], two


def to_ranks(slots):
    return [slots[0]] + [flip(slots[j], "tensor", j) for j in (1, 2, 3)]


def norm_parts(values):
    row_mean = jnp.mean(values, axis=-1, keepdims=True)
    centred = values - row_mean
    row_var = jnp.mean(centred * centred, axis=-1, keepdims=True)
    inverse = lax.rsqrt(row_var + norm_eps)
    return centred * inverse, inverse


def norm_backward(grad_out, normed, inverse, gain_vec):
    scaled = grad_out * gain_vec
    return inverse * (
        scaled
        - jnp.mean(scaled, axis=-1, keepdims=True)
        - normed * jnp.mean(scaled * normed, axis=-1, keepdims=True)
    )


def place_rows(at_ref, parts, target, sems):
    if len(parts) == 1:
        return fetch([(parts[0], target)], sems)
    height = parts[0].shape[1]
    spots = [pl.ds(pl.multiple_of((at_ref[0] ^ slot) * height, 32), height) for slot in range(len(parts))]
    return fetch([(part, target.at[:, spot, :]) for part, spot in zip(parts, spots)], sems)


def take_rows(at_ref, source, slot, height):
    start = pl.multiple_of((at_ref[0] ^ slot) * height, 32)
    return source[pl.ds(start, height), :]


def rank_rows(at_ref, slot, height):
    return pl.ds(pl.multiple_of((at_ref[1] ^ slot) * height, 16), height)


def pack_heads(value):
    half = value.shape[0] // 2
    side = value[:, 128:]
    return value[:, :128], jnp.concatenate([side[:half], side[half:]], axis=1)


def unpack_heads(packed):
    rows = packed.shape[0] * 2 // 3
    head, side = packed[:rows], packed[rows:]
    return jnp.concatenate([head, jnp.concatenate([side[:, :64], side[:, 64:]], axis=0)], axis=1)


def two_halves(value):
    upper = value.astype(low)
    return jnp.concatenate([upper.astype(wide), value - upper.astype(wide)], axis=0)


def first_kernel(at_ref, *refs):
    ins, (tile_ref, low_ref, turned_ref), bufs, sems = refs[:4], refs[4:7], refs[7:11], refs[11]
    copies = fetch(list(zip(ins, bufs)), sems)
    vec_buf, bias_buf, qkv_buf, out_buf = bufs
    copies[0].wait()
    copies[1].wait()
    cols, ends = vec_buf.shape[1], bias_buf.shape[1]
    tile = jnp.concatenate(
        [vec_buf[...], jnp.zeros((8, 128 - cols - ends), wide), jnp.broadcast_to(bias_buf[...], (8, ends))], axis=1
    )
    for j in range(tile_ref.shape[0]):
        tile_ref[j] = tile
    copies[2].wait()
    low_ref[...] = qkv_buf[...].astype(low)
    copies[3].wait()
    turned_ref[...] = out_buf[...].T.astype(low)


def small_unpack_kernel(cols, at_ref, small_ref, vec_ref, qv_ref, bias_ref):
    devices = small_ref.shape[0]
    ends = bias_ref.shape[1] * 4 // devices
    share = devices // 4
    vec_ref[...] = jnp.concatenate([small_ref[j, :, :cols] for j in range(devices)], axis=1)
    mine = [small_ref[at_ref[1] * share + j] for j in range(share)]
    qv_ref[...] = jnp.concatenate([tile[:, :cols] for tile in mine], axis=1)
    bias_ref[...] = jnp.concatenate([tile[0:1, 128 - ends :] for tile in mine], axis=1)


def add_kernel(at_ref, left_ref, right_ref, out_ref):
    out_ref[...] = (left_ref[...].astype(wide) + right_ref[...].astype(wide)).astype(out_ref.dtype)


def quad_kernel(at_ref, keep_ref, got_ref, *out_refs):
    for j, ref in enumerate(out_refs):
        ref[...] = (keep_ref[j].astype(wide) + got_ref[j].astype(wide)).astype(ref.dtype)


def ranks_kernel(at_ref, *refs):
    parts, out_refs = refs[:-4], refs[-4:]
    width = out_refs[0].shape[1]
    total = sum(ref[...].astype(wide) for ref in parts)
    height = total.shape[0]
    for j, ref in enumerate(out_refs):
        ref[0:height, :] = total[:, j * width : (j + 1) * width].astype(low)
        if ref.shape[0] > height:
            small = total[0:16, 4 * width : 4 * width + 96]
            cols = 96 // 4
            vec = jnp.zeros((16, cols), wide)
            bias = jnp.zeros((1, 96), wide)
            for other in range(4):
                here = ((at_ref[1] ^ j) == other).astype(wide)
                vec += small[:, other * cols : (other + 1) * cols] * here
                bias += small[8 + other : 9 + other, :] * here
            ref[height:, :] = jnp.concatenate(
                [vec, jnp.zeros((16, width - cols - 96), wide), jnp.broadcast_to(bias, (16, 96))], axis=1
            ).astype(low)


def last_kernel(at_ref, *refs):
    parts, ins, outs, bufs, (in_sems, out_sems) = refs[:4], refs[4:13], refs[13:22], refs[22:31], refs[31:]
    copies = fetch(list(zip(ins, bufs)), in_sems)
    total = sum(ref[...].astype(wide) for ref in parts)
    height, cols, ends = bufs[0].shape[1], bufs[3].shape[1], bufs[6].shape[1]
    small = total[height : height + 8]
    grads = (total[0:height].T, small[:, :cols], small[0:1, total.shape[1] - ends :])
    for copy in copies:
        copy.wait()
    states = []
    for j, (rate, decay) in enumerate(((0.3, 0.1), (0.5, 0.0), (0.7, 0.0))):
        weight, first, second = (buf[...] for buf in bufs[3 * j : 3 * j + 3])
        states += adamw(weight, grads[j], first, second, rate, decay)
    stored(states, bufs, outs, out_sems)


def output_kernel(at_ref, own_ref, vec_ref, one_ref, two_ref, three_ref, out_ref):
    total = one_ref[...].astype(wide) + two_ref[...].astype(wide) + three_ref[...].astype(wide)
    out_ref[...] = (own_ref[0] + total + vec_ref[7:8, :]).astype(low)


def sums_pack_kernel(cols, ends, at_ref, one_ref, two_ref, qv_ref, gbo_ref, gub_ref, out_ref):
    devices = out_ref.shape[0]
    share = devices // 4
    middle = jnp.zeros((8, 128 - cols - ends), wide)
    for j in range(devices):
        span = slice(j * cols, (j + 1) * cols)
        mine = (at_ref[1] == j // share).astype(wide)
        k = j % share
        rows = [
            one_ref[0:2, span],
            two_ref[0:2, span],
            qv_ref[0:2, k * cols : (k + 1) * cols] * mine,
            gbo_ref[0:1, span],
            two_ref[2:3, span],
        ]
        bias = gub_ref[0:1, k * ends : (k + 1) * ends] * mine
        out_ref[j] = jnp.concatenate(
            [jnp.concatenate(rows, axis=0), middle, jnp.broadcast_to(bias, (8, ends))], axis=1
        )


def stored(values, bufs, refs, sems):
    for value, buf in zip(values, bufs):
        buf[...] = value
    for copy in fetch(list(zip(bufs, refs)), sems):
        copy.wait()


def small_adam_kernel(at_ref, got_ref, *refs):
    ins, outs, bufs, in_sems, out_sems = refs[:6], refs[6:12], refs[12:18], refs[18], refs[19]
    copies = fetch(list(zip(ins, bufs)), in_sems)
    total = jnp.sum(got_ref[...], axis=0)
    for copy in copies:
        copy.wait()
    cols, ends = bufs[0].shape[1], bufs[3].shape[1]
    vectors, biases = [buf[...] for buf in bufs[:3]], [buf[...] for buf in bufs[3:]]
    states = adamw(vectors[0], total[:, :cols], vectors[1], vectors[2], 0.5, 0.0)
    states += adamw(biases[0], total[0:1, 128 - ends :], biases[1], biases[2], 0.7, 0.0)
    stored(states, bufs, outs, out_sems)


def adam_kernel(n_parts, turned, rates, at_ref, *refs):
    count = len(rates)
    parts, refs = refs[: n_parts * count], refs[n_parts * count :]
    ins, outs, bufs = refs[: 3 * count], refs[3 * count : 6 * count], refs[6 * count : 9 * count]
    in_sems, out_sems = refs[9 * count :]
    copies = fetch(list(zip(ins, bufs)), in_sems)
    states = []
    for j, (rate, decay) in enumerate(rates):
        total = sum(ref[...].astype(wide) for ref in parts[j * n_parts : (j + 1) * n_parts])
        if turned:
            total = total.T
        for copy in copies[3 * j : 3 * j + 3]:
            copy.wait()
        weight, first, second = (buf[...] for buf in bufs[3 * j : 3 * j + 3])
        states += adamw(weight, total, first, second, rate, decay)
    stored(states, bufs, outs, out_sems)


def weights_kernel(at_ref, up_ref, down_ref, *refs):
    parts, (out_ref, up_buf, down_buf, sems) = refs[:4], refs[4:]
    copies = fetch([(up_ref, up_buf), (down_ref, down_buf)], sems)
    out_ref[2] = jnp.concatenate([ref[...] for ref in parts], axis=1)
    copies[0].wait()
    out_ref[0] = up_buf[...].astype(low)
    copies[1].wait()
    out_ref[1] = down_buf[...].astype(low)


def attend_kernel(n_parts, at_ref, x_ref, vec_ref, qv_ref, *refs):
    parts = refs[:n_parts]
    a1_ref, qkv_ref, lse_ref, o_ref, w_ref, ot_ref, sems = refs[n_parts:]
    copies = place_rows(at_ref, parts, w_ref, sems)
    normed, _ = norm_parts(x_ref[...].astype(wide))
    a1 = (normed * vec_ref[0:1, :] + vec_ref[1:2, :]).astype(low)
    a1_ref[...] = a1
    for copy in copies:
        copy.wait()
    q = ((dot(a1, w_ref[0]) + qv_ref[4:5, :]) * score_scale).astype(low)
    k = dot(a1, w_ref[1]).astype(low)
    v = (dot(a1, w_ref[2]) + qv_ref[5:6, :]).astype(low)
    qkv_ref[0] = q
    qkv_ref[1] = k
    qkv_ref[2] = v
    vt = v.T
    for head in range(q.shape[1] // HD):
        cols = slice(head * HD, (head + 1) * HD)
        scores = dot(k[:, cols], q[:, cols], NT)
        top = jnp.max(scores, axis=0, keepdims=True)
        expos = jnp.exp(scores - top)
        summed = jnp.sum(expos, axis=0, keepdims=True)
        lse_ref[head : head + 1, :] = top + jnp.log(summed)
        ot_ref[cols, :] = dot(vt[cols, :], expos.astype(low)) / summed
    o = ot_ref[...].T.astype(low)
    head_part, side_part = pack_heads(o)
    rows = o.shape[0]
    o_ref[0:rows, :] = head_part
    o_ref[rows:, :] = side_part


def ready_kernel(at_ref, c_ref, *refs):
    parts, (w_ref, dg_ref, sems) = refs[:-3], refs[-3:]
    for copy in place_rows(at_ref, parts, w_ref, sems):
        copy.wait()
    dg_ref[...] = dot(c_ref[...], w_ref[1])


def mlp_kernel(at_ref, x_ref, c_ref, vec_ref, ub_ref, w_ref, dg_ref, *refs):
    heads, dn2_refs = refs[:4], refs[4:8]
    a2_ref, g_ref, du_ref, own_ref, stat_ref, sums_ref, gub_ref, oo_ref, h_ref, n_ref, s_ref, o_ref = refs[8:]
    part_rows = dn2_refs[0].shape[0]
    o_ref[...] = jnp.concatenate([unpack_heads(ref[...]) for ref in heads], axis=1)
    hidden_state = x_ref[...].astype(wide) + dot(o_ref[...], w_ref[2], NT) + vec_ref[6:7, :]
    h_ref[...] = hidden_state
    normed, inverse = norm_parts(hidden_state)
    n_ref[...] = normed
    s_ref[...] = jnp.broadcast_to(inverse, s_ref.shape)
    a2 = (normed * vec_ref[2:3, :] + vec_ref[3:4, :]).astype(low)
    a2_ref[...] = a2
    pre = dot(a2, w_ref[0]) + ub_ref[...]
    square = pre * pre
    tangent = jnp.tanh(pre * (gelu_coef + (0.044715 * gelu_coef) * square))
    half = 0.5 + 0.5 * tangent
    active = pre * half
    g_ref[...] = active.astype(low)
    slope = half + active * (1.0 - half) * (2.0 * gelu_coef + (6.0 * 0.044715 * gelu_coef) * square)
    du = (dg_ref[...] * slope).astype(low)
    du_ref[...] = du
    gub_ref[...] = jnp.sum(du.astype(wide), axis=0, keepdims=True)
    own = rank_rows(at_ref, 0, part_rows)
    own_ref[0] = h_ref[own, :]
    own_ref[1] = n_ref[own, :]
    stat_ref[...] = s_ref[own, :]
    oo_ref[...] = o_ref[own, :]
    dn2 = dot(du, w_ref[0], NT)
    h_ref[...] = dn2
    sums_ref[0:1, :] = jnp.sum(dn2 * normed, axis=0, keepdims=True)
    sums_ref[1:2, :] = jnp.sum(dn2, axis=0, keepdims=True)
    for j, ref in enumerate(dn2_refs):
        ref[...] = h_ref[rank_rows(at_ref, j, part_rows), :].astype(low)
    sums_ref[2:3, :] = jnp.sum(c_ref[own, :].astype(wide), axis=0, keepdims=True)


def mlp_out_kernel(at_ref, g_ref, w_ref, *refs):
    slots, out_ref = refs[:4], refs[4]
    out_ref[...] = dot(g_ref[...], w_ref[1], NT)
    for j, ref in enumerate(slots):
        ref[...] = out_ref[rank_rows(at_ref, j, ref.shape[0]), :].astype(low)


def mix_kernel(at_ref, own_ref, stat_ref, c_ref, vec_ref, w_ref, *refs):
    chunks = refs[:3]
    dh_ref, dz_ref, gbo_ref = refs[3:6]
    do_refs = refs[6:]
    part_rows = stat_ref.shape[0]
    grad = sum(ref[...].astype(wide) for ref in chunks)
    cotan = c_ref[rank_rows(at_ref, 0, part_rows), :].astype(wide)
    dh = cotan + norm_backward(grad, own_ref[1], stat_ref[:, 0:1], vec_ref[2:3, :])
    dh_ref[...] = dh
    gbo_ref[...] = jnp.sum(dh, axis=0, keepdims=True)
    dz = dh.astype(low)
    dz_ref[...] = dz
    do = dot(dz, w_ref[2]).astype(low)
    heads_width = do.shape[1] // 4
    for j, ref in enumerate(do_refs):
        head_part, side_part = pack_heads(do[:, j * heads_width : (j + 1) * heads_width])
        ref[0:part_rows, :] = head_part
        ref[part_rows:, :] = side_part


def attend_back_kernel(fast, at_ref, x_ref, a1_ref, qkv_ref, lse_ref, w_ref, *refs):
    if fast:
        (two_ref, gbo_ref, gub_ref), refs = refs[:3], refs[3:]
    chunks, dn1_refs = refs[:4], refs[4:8]
    grad_refs, (sums_ref, qvsum_ref) = refs[8:-7], refs[-7:-5]
    do_ref, dqt_ref, d_ref, g_ref, dn1_ref = refs[-5:]
    rows, width = x_ref.shape
    part_rows = rows // 4
    for j in range(4):
        do_ref[rank_rows(at_ref, j, part_rows), :] = unpack_heads(chunks[j][...])
    q, k, v, do = qkv_ref[0], qkv_ref[1], qkv_ref[2], do_ref[...]
    kt = k.T
    heads_width = q.shape[1]
    for head in range(q.shape[1] // HD):
        cols = slice(head * HD, (head + 1) * HD)
        scores = dot(k[:, cols], q[:, cols], NT)
        probs = jnp.exp(scores - lse_ref[head : head + 1, :])
        grad_probs = dot(v[:, cols], do[:, cols], NT)
        d_ref[:, 2 * heads_width + head * HD : 2 * heads_width + (head + 1) * HD] = dot(
            probs.astype(low), do[:, cols]
        ).astype(low)
        both = probs * grad_probs
        grad_scores = (both - probs * jnp.sum(both, axis=0, keepdims=True)).astype(low)
        d_ref[:, heads_width + head * HD : heads_width + (head + 1) * HD] = dot(
            grad_scores, q[:, cols]
        ).astype(low)
        dqt_ref[cols, :] = dot(kt[cols, :], grad_scores) * score_scale
    d_ref[:, :heads_width] = dqt_ref[...].T.astype(low)
    dq, dk, dv = (d_ref[:, j * heads_width : (j + 1) * heads_width] for j in range(3))
    qvsum_ref[0:1, :] = jnp.sum(dq.astype(wide), axis=0, keepdims=True)
    qvsum_ref[1:2, :] = jnp.sum(dv.astype(wide), axis=0, keepdims=True)
    dn1 = dot(dq, w_ref[0], NT) + dot(dk, w_ref[1], NT) + dot(dv, w_ref[2], NT)
    dn1_ref[...] = dn1
    for j, ref in enumerate(dn1_refs):
        ref[...] = dn1_ref[rank_rows(at_ref, j, part_rows), :].astype(low)
    normed, _ = norm_parts(x_ref[...].astype(wide))
    sums_ref[0:1, :] = jnp.sum(dn1 * normed, axis=0, keepdims=True)
    sums_ref[1:2, :] = jnp.sum(dn1, axis=0, keepdims=True)
    g_ref[:, g_ref.shape[1] - 3 * heads_width :] = dot(a1_ref[...].T, d_ref[...]).astype(low)
    if not fast:
        grad_refs[0][...] = g_ref[...]
        return
    height = width // 8
    ends = gub_ref.shape[1] // 8
    for j in range(8):
        span, half = slice(j * height, (j + 1) * height), j % 2
        here = (at_ref[1] == j // 2).astype(wide)
        rows_in = [
            sums_ref[0:2, span],
            two_ref[0:2, span],
            qvsum_ref[0:2, half * height : (half + 1) * height] * here,
            gbo_ref[0:1, span],
            two_ref[2:3, span],
        ]
        rows_in += [gub_ref[0:1, (4 * half + k) * ends : (4 * half + k + 1) * ends] * here for k in range(4)]
        rows_in += [jnp.zeros((4, height), wide)]
        small = jnp.concatenate(rows_in, axis=0)
        g_ref[j * height : j * height + 16, 0:128] = jnp.concatenate(
            [small, jnp.zeros((16, 128 - height), wide)], axis=1
        ).astype(low)
    cut_blocks(at_ref, g_ref, *grad_refs)


def cut_blocks(at_ref, source, keep_refs, send_refs):
    height = source.shape[0] // 8
    for slot in range(4):
        keep_refs[slot] = take_rows(at_ref, source, 2 * slot, height)
        send_refs[slot] = take_rows(at_ref, source, 2 * slot + 1, height)


def weight_grad_kernel(at_ref, left_ref, right_ref, out_ref):
    out_ref[...] = dot(left_ref[...].T, right_ref[...]).astype(low)


def out_grad_kernel(at_ref, left_ref, right_ref, keep_ref, send_ref, grad_ref):
    grad_ref[...] = dot(left_ref[...].T, right_ref[...]).astype(low)
    cut_blocks(at_ref, grad_ref, keep_ref, send_ref)


def pair_quad_kernel(at_ref, keep_ref, got_ref, more_keep_ref, more_got_ref, *out_refs):
    first = keep_ref.shape[2]
    for j, ref in enumerate(out_refs):
        ref[:, :first] = (keep_ref[j].astype(wide) + got_ref[j].astype(wide)).astype(ref.dtype)
        ref[:, first:] = (more_keep_ref[j].astype(wide) + more_got_ref[j].astype(wide)).astype(ref.dtype)


def mlp_grad_kernel(at_ref, a2_ref, du_ref, c_ref, g_ref, keep_ref, send_ref, grad_ref):
    for j, (left, right) in enumerate(((a2_ref, du_ref), (c_ref, g_ref))):
        grad_ref[j] = dot(left[...].T, right[...]).astype(low)
        cut_blocks(at_ref, grad_ref.at[j], keep_ref.at[:, j], send_ref.at[:, j])


def input_kernel(at_ref, x_ref, dh_ref, vec_ref, *refs):
    chunks, out_ref = refs[:3], refs[3]
    part_rows = dh_ref.shape[0]
    normed, inverse = norm_parts(x_ref[rank_rows(at_ref, 0, part_rows), :].astype(wide))
    grad = sum(ref[...].astype(wide) for ref in chunks)
    out_ref[...] = dh_ref[...] + norm_backward(grad, normed, inverse, vec_ref[0:1, :])


def adamw(weight, gradient, first, second, rate, decay):
    first_new = beta_one * first + (1.0 - beta_one) * gradient
    second_new = beta_two * second + (1.0 - beta_two) * gradient * gradient
    first_hat = first_new / (1.0 - beta_one**STEP)
    second_hat = second_new / (1.0 - beta_two**STEP)
    weight_new = weight - rate * (first_hat / (jnp.sqrt(second_hat) + adam_eps) + decay * weight)
    return (weight_new, first_new, second_new)


def body(
    images,
    cotangent,
    qkv_weight,
    out_weight,
    up_weight,
    down_weight,
    vectors,
    up_bias,
    qkv_first,
    qkv_second,
    out_first,
    out_second,
    up_first,
    up_second,
    down_first,
    down_second,
    vector_first,
    vector_second,
    bias_first,
    bias_second,
):
    fsdp_size = lax.axis_size("fsdp")
    tensor_size = lax.axis_size("tensor")
    devices = fsdp_size * tensor_size
    fast = fsdp_size == 8
    at = jnp.stack([lax.axis_index("fsdp"), lax.axis_index("tensor")]).astype(jnp.int32)
    _, rows, width = images.shape
    hidden = up_weight.shape[1]
    heads_width = width // tensor_size
    part_rows = rows // tensor_size
    height = width // fsdp_size
    x = images.reshape(rows, width)
    c = cotangent.reshape(rows, width)
    cols, ends = vectors.shape[1], up_bias.shape[0]
    both_axes = ("fsdp", "tensor")

    tiles, qkv_low, out_t = kernel_call(
        first_kernel,
        [((devices, 8, 128), wide), (qkv_weight.shape, low), ((height, heads_width), low)],
        (at, vectors, up_bias[None], qkv_weight, out_weight),
        [
            pltpu.VMEM(vectors.shape, wide),
            pltpu.VMEM((1, ends), wide),
            pltpu.VMEM(qkv_weight.shape, wide),
            pltpu.VMEM(out_weight.shape, wide),
            pltpu.SemaphoreType.DMA((4,)),
        ],
        hbm=(1, 2, 3, 4),
    )
    small = lax.all_to_all(tiles, both_axes, 0, 0, tiled=True)
    vec, qv, up_local = kernel_call(
        functools.partial(small_unpack_kernel, cols),
        [((8, width), wide), ((8, heads_width), wide), ((1, hidden), wide)],
        (at, small),
    )

    if fast:
        chips = chips_of(qkv_low)
        qkv_parts = cores_of(chips)
    else:
        chips = qkv_parts = [lax.all_gather(qkv_low, "fsdp", axis=1, tiled=True)]
    (shard,) = kernel_call(
        weights_kernel,
        [((3, height, width), low)],
        (at, after(up_weight, chips[-1]), down_weight.T, *to_ranks([out_t] * 4)),
        [
            pltpu.VMEM(up_weight.shape, wide),
            pltpu.VMEM(up_weight.shape, wide),
            pltpu.SemaphoreType.DMA((2,)),
        ],
        hbm=(1, 2),
    )
    if fast:
        chips = chips_of(shard)

    n = len(qkv_parts)
    a1, qkv, lse, o_mine, qkv_full = kernel_call(
        functools.partial(attend_kernel, n),
        [
            ((rows, width), low),
            ((3, rows, heads_width), low),
            ((8, rows), wide),
            ((rows * 3 // 2, 128), low),
            ((3, width, heads_width), low),
        ],
        (at, x, vec, qv, *qkv_parts),
        [pltpu.VMEM((heads_width, rows), wide), pltpu.SemaphoreType.DMA((n,))],
        free=(4,), hbm=range(5, 4 + n),
    )
    o_parts = rank_gather(o_mine)
    if fast:
        chips = lax.optimization_barrier((*chips, o_parts[1], o_parts[2]))[:4]
        rest_parts = cores_of(chips)
    else:
        rest_parts = [lax.all_gather(shard, "fsdp", axis=1, tiled=True)]

    block = ((part_rows, width), low)
    w_full, dg = kernel_call(
        ready_kernel,
        [((3, width, width), low), ((rows, hidden), wide)],
        (at, c, *rest_parts),
        [pltpu.SemaphoreType.DMA((n,))],
        free=range(2, 2 + n),
    )
    *dn2, a2, g, du, own, stat, sums_two, gub, o_own = kernel_call(
        mlp_kernel,
        [
            *[block] * 4,
            ((rows, width), low),
            ((rows, hidden), low),
            ((rows, hidden), low),
            ((2, part_rows, width), wide),
            ((part_rows, 128), wide),
            ((8, width), wide),
            ((1, hidden), wide),
            block,
        ],
        (at, x, c, vec, up_local, w_full, dg, *o_parts),
        [
            pltpu.VMEM((rows, width), wide),
            pltpu.VMEM((rows, width), wide),
            pltpu.VMEM((rows, 128), wide),
            pltpu.VMEM((rows, width), low),
        ],
    )

    def over_cores(keep, send):
        cut = keep.shape[1:]
        return kernel_call(
            quad_kernel, [(cut, wide)] + [(cut, low)] * 3, (at, keep, flip(send, "fsdp", 1))
        )

    def over_chips(mine, *go):
        return [mine] + [flip(part, "fsdp", mask) for part, mask in zip(go, (2, 4, 6))]

    if fast:
        cut = (4, 2, height, hidden)
        keep, send = kernel_call(
            mlp_grad_kernel, [(cut, low)] * 2, (at, a2, du, c, g), [pltpu.VMEM((2, width, hidden), low)]
        )
        dn2_got, dn2_pair = rank_sum(at, dn2, keep, send)
        mlp_sums = over_chips(*over_cores(keep, after(send, dn2_pair)))
    else:
        (up_grad,) = kernel_call(weight_grad_kernel, [((width, hidden), low)], (at, a2, du))
        (down_grad,) = kernel_call(weight_grad_kernel, [((width, hidden), low)], (at, c, g))
        dn2_got, dn2_pair = rank_sum(at, dn2)
        mlp_sums = summed_on_arrival(jnp.stack([up_grad, down_grad]), 1)
    mlp = kernel_call(
        mlp_out_kernel,
        [block] * 4,
        (at, after(g, dn2_pair), w_full),
        [pltpu.VMEM((rows, width), wide)],
    )
    dn2_got = lax.optimization_barrier((dn2_got, mlp, mlp_sums))[0]
    dh, dz, gbo, *do = kernel_call(
        mix_kernel,
        [
            ((part_rows, width), wide),
            block,
            ((1, width), wide),
            *[((part_rows * 3 // 2, 128), low)] * 4,
        ],
        (at, own, stat, c, vec, w_full, *dn2_got),
    )
    do_got = to_ranks(do)
    if fast:
        out_grad = kernel_call(
            out_grad_kernel, [((4, height, width), low)] * 2, (at, dz, o_own), [pltpu.VMEM((width, width), low)]
        )
    else:
        out_grad = kernel_call(weight_grad_kernel, [((width, width), low)], (at, dz, o_own))

    def update(sums, weight, first, second, rate, decay):
        return adamw(weight, sum(part.astype(wide) for part in sums), first, second, rate, decay)

    mlp_sums = lax.optimization_barrier((mlp_sums, dz))[0]
    up_state = update([part[0] for part in mlp_sums], up_weight, up_first, up_second, 0.08, 0.1)
    down_state = update(
        [part[1] for part in mlp_sums], down_weight.T, down_first.T, down_second.T, 0.045, 0.1
    )
    mlp_three, mlp_one = flip(mlp[3], "tensor", 1), flip(mlp[1], "tensor", 1)
    (mlp_two,) = kernel_call(add_kernel, [block], (at, mlp[2], mlp_three))
    mlp_two = flip(mlp_two, "tensor", 2)
    do_got = lax.optimization_barrier((do_got, out_grad, mlp_one, mlp_two, up_state, down_state))[0]
    down_state = [value.T for value in down_state]

    lanes = 3 * heads_width + (128 if fast else 0)
    extra = (sums_two, gbo, gub) if fast else ()
    cut = (4, height, lanes)
    grads = [(cut, low)] * 2 if fast else [((width, lanes), low)]
    *dn1, sums_one, qv_sums = kernel_call(
        functools.partial(attend_back_kernel, fast),
        [*[block] * 4, *grads, ((8, width), wide), ((8, heads_width), wide)],
        (at, x, a1, qkv, lse, qkv_full, *extra, *do_got),
        [
            pltpu.VMEM((rows, heads_width), low),
            pltpu.VMEM((heads_width, rows), wide),
            pltpu.VMEM((rows, 3 * heads_width), low),
            pltpu.VMEM((width, lanes), low),
            pltpu.VMEM((rows, width), wide),
        ],
    )
    dn1, grads = dn1[:4], dn1[4:]

    if fast:
        full = (height, width + lanes)
        arrived = (out_grad[0], flip(out_grad[1], "fsdp", 1), grads[0], flip(grads[1], "fsdp", 1))
        sums = kernel_call(pair_quad_kernel, [(full, wide)] + [(full, low)] * 3, (at, *arrived))
        dn1_got, dn1_pair = rank_sum(at, dn1, *sums)
        sums = over_chips(*sums)
    else:
        dn1_got, dn1_pair = rank_sum(at, dn1)
        sums = summed_on_arrival(jnp.concatenate([out_grad[0], grads[0]], axis=1), 0)

    (output,) = kernel_call(output_kernel, [block], (at, after(own, dn1_pair), vec, mlp[0], mlp_one, mlp_two))
    lanes += width
    qkv_sums = [
        jnp.stack([part[:, lanes - j * heads_width : lanes - (j - 1) * heads_width] for j in (3, 2, 1)]) for part in sums
    ]
    qkv_state = update(qkv_sums, qkv_weight, qkv_first, qkv_second, 0.08, 0.1)

    tall = height + (16 if fast else 0)
    out_sums = to_ranks(kernel_call(ranks_kernel, [((tall, heads_width), low)] * 4, (at, *sums)))
    out_state = (out_weight, out_first, out_second)
    small_state = (vectors, vector_first, vector_second, up_bias[None], bias_first[None], bias_second[None])
    if fast:
        states = out_state + small_state
        *last, bias_new, bias_m, bias_s = kernel_call(
            last_kernel,
            [(value.shape, wide) for value in states],
            (at, *out_sums, *states),
            [pltpu.VMEM(value.shape, wide) for value in states] + [pltpu.SemaphoreType.DMA((9,))] * 2,
            hbm=range(5, 14),
            hbm_outs=True,
        )
        out_state, vec_state = last[:3], last[3:]
    else:
        (tiles,) = kernel_call(
            functools.partial(sums_pack_kernel, cols, ends),
            [((devices, 8, 128), wide)],
            (at, sums_one, sums_two, qv_sums, gbo, gub),
        )
        tiles = lax.all_to_all(tiles, both_axes, 0, 0, tiled=True)
        *vec_state, bias_new, bias_m, bias_s = kernel_call(
            small_adam_kernel,
            [(value.shape, wide) for value in small_state],
            (at, tiles, *small_state),
            [pltpu.VMEM(value.shape, wide) for value in small_state] + [pltpu.SemaphoreType.DMA((6,))] * 2,
            hbm=range(2, 8),
            hbm_outs=True,
        )
        out_state = kernel_call(
            functools.partial(adam_kernel, 4, True, ((0.3, 0.1),)),
            [(value.shape, wide) for value in out_state],
            (at, *out_sums, *out_state),
            [pltpu.VMEM(value.shape, wide) for value in out_state] + [pltpu.SemaphoreType.DMA((3,))] * 2,
            hbm=range(5, 8),
            hbm_outs=True,
        )

    dn1_got = lax.optimization_barrier((dn1_got, output, qkv_state))[0]
    (input_own,) = kernel_call(
        input_kernel,
        [((part_rows, width), wide)],
        (at, x, dh, vec, *dn1_got),
    )
    return (
        output[None],
        input_own[None],
        *qkv_state,
        *out_state,
        *up_state,
        *down_state,
        *vec_state,
        bias_new[0],
        bias_m[0],
        bias_s[0],
    )


def solution(mesh):
    weights = (P(None, "fsdp", "tensor"), P("tensor", "fsdp"), P("fsdp", "tensor"), P("tensor", "fsdp"))
    vector, bias = P(None, ("fsdp", "tensor")), P(("fsdp", "tensor"))
    twice = [spec for spec in (*weights, vector, bias) for _ in range(2)]
    thrice = [spec for spec in (*weights, vector, bias) for _ in range(3)]
    return jax.shard_map(
        body,
        mesh=mesh,
        in_specs=(P("fsdp", None, None), P("fsdp", None, None), *weights, vector, bias, *twice),
        out_specs=(P("fsdp", "tensor", None), P("fsdp", "tensor", None), *thrice),
        check_vma=False,
    )
```

```python
import functools
import math

import jax
import jax.numpy as jnp
from jax import lax
from jax.experimental import pallas as pl
from jax.experimental.pallas import tpu as pltpu
from jax.sharding import PartitionSpec as P

HD = 64
STEP = 10


norm_eps = 1e-06
beta_one = 0.9
beta_two = 0.999
adam_eps = 1e-08
gelu_coef = math.sqrt(2.0 / math.pi)
score_scale = float(HD) ** (-0.5)
low = jnp.bfloat16
wide = jnp.float32
VMEM_LIMIT = 24 * 1024 * 1024

NN = (((1,), (0,)), ((), ()))
NT = (((1,), (1,)), ((), ()))
TN = (((0,), (0,)), ((), ()))


def dot(left, right, dims=NN):
    return lax.dot_general(left, right, dims, preferred_element_type=wide)


def kernel_call(body, outs, args, scratch=(), hbm=(), free=(), hbm_outs=False):
    def spec(i):
        space = pltpu.HBM if i in hbm else pl.ANY if i in free else pltpu.VMEM
        return pl.BlockSpec(memory_space=space)

    out_space = pltpu.HBM if hbm_outs else pltpu.VMEM
    args = [pltpu.with_memory_space_constraint(arg, pltpu.HBM) if i in hbm else arg for i, arg in enumerate(args)]
    return pl.pallas_call(
        body,
        out_shape=[jax.ShapeDtypeStruct(s, d) for s, d in outs],
        in_specs=[pl.BlockSpec(memory_space=pltpu.SMEM)] + [spec(i) for i in range(1, len(args))],
        out_specs=[pl.BlockSpec(memory_space=out_space)] * len(outs),
        scratch_shapes=list(scratch),
        compiler_params=pltpu.CompilerParams(vmem_limit_bytes=VMEM_LIMIT),
        cost_estimate=pl.CostEstimate(flops=0, bytes_accessed=0, transcendentals=0),
    )(*args)


def fetch(pairs, sems):
    copies = [pltpu.make_async_copy(source, target, sems.at[i]) for i, (source, target) in enumerate(pairs)]
    for copy in copies:
        copy.start()
    return copies


def flip(value, axis, mask):
    size = lax.axis_size(axis)
    return lax.ppermute(value, axis, [(i, i ^ mask) for i in range(size)])


def after(value, *others):
    return lax.optimization_barrier((value, *others))[0]


def chips_of(shard):
    return lax.optimization_barrier([shard] + [flip(shard, "fsdp", mask) for mask in (2, 4, 6)])


def cores_of(chips):
    others = [flip(part, "fsdp", 1) for part in chips]
    return [part for pair in zip(chips, others) for part in pair]


def summed_on_arrival(value, dim):
    peers = lax.axis_size("fsdp")
    before, behind = (value.shape[:dim], value.shape[dim + 1 :])
    blocks = jnp.moveaxis(value.reshape(*before, peers, -1, *behind), dim, 0)
    blocks = lax.all_to_all(blocks, "fsdp", 0, 0, tiled=True)
    return [jnp.sum(blocks.astype(wide), axis=0)]


def rank_gather(value):
    one, two = flip(value, "tensor", 1), flip(value, "tensor", 2)
    return [value, one, two, flip(two, "tensor", 1)]


def rank_sum(at, slots, *gates):
    three = after(flip(slots[3], "tensor", 1), *gates)
    one = flip(slots[1], "tensor", 1)
    (two,) = kernel_call(add_kernel, [(three.shape, low)], (at, slots[2], three))
    return [slots[0], one, flip(two, "tensor", 2)], two


def to_ranks(slots):
    return [slots[0]] + [flip(slots[j], "tensor", j) for j in (1, 2, 3)]


def norm_parts(values):
    row_mean = jnp.mean(values, axis=-1, keepdims=True)
    centred = values - row_mean
    row_var = jnp.mean(centred * centred, axis=-1, keepdims=True)
    inverse = lax.rsqrt(row_var + norm_eps)
    return centred * inverse, inverse


def norm_backward(grad_out, normed, inverse, gain_vec):
    scaled = grad_out * gain_vec
    return inverse * (
        scaled
        - jnp.mean(scaled, axis=-1, keepdims=True)
        - normed * jnp.mean(scaled * normed, axis=-1, keepdims=True)
    )


def place_rows(at_ref, parts, target, sems):
    if len(parts) == 1:
        return fetch([(parts[0], target)], sems)
    height = parts[0].shape[1]
    spots = [pl.ds(pl.multiple_of((at_ref[0] ^ slot) * height, 32), height) for slot in range(len(parts))]
    return fetch([(part, target.at[:, spot, :]) for part, spot in zip(parts, spots)], sems)


def take_rows(at_ref, source, slot, height):
    start = pl.multiple_of((at_ref[0] ^ slot) * height, 32)
    return source[pl.ds(start, height), :]


def rank_rows(at_ref, slot, height):
    return pl.ds(pl.multiple_of((at_ref[1] ^ slot) * height, 16), height)


def pack_heads(value):
    half = value.shape[0] // 2
    side = value[:, 128:]
    return value[:, :128], jnp.concatenate([side[:half], side[half:]], axis=1)


def unpack_heads(packed):
    rows = packed.shape[0] * 2 // 3
    head, side = packed[:rows], packed[rows:]
    return jnp.concatenate([head, jnp.concatenate([side[:, :64], side[:, 64:]], axis=0)], axis=1)


def two_halves(value):
    upper = value.astype(low)
    return jnp.concatenate([upper.astype(wide), value - upper.astype(wide)], axis=0)


def first_kernel(at_ref, *refs):
    ins, (tile_ref, low_ref, turned_ref), bufs, sems = refs[:4], refs[4:7], refs[7:11], refs[11]
    copies = fetch(list(zip(ins, bufs)), sems)
    vec_buf, bias_buf, qkv_buf, out_buf = bufs
    copies[0].wait()
    copies[1].wait()
    cols, ends = vec_buf.shape[1], bias_buf.shape[1]
    tile = jnp.concatenate(
        [vec_buf[...], jnp.zeros((8, 128 - cols - ends), wide), jnp.broadcast_to(bias_buf[...], (8, ends))], axis=1
    )
    for j in range(tile_ref.shape[0]):
        tile_ref[j] = tile
    copies[2].wait()
    low_ref[...] = qkv_buf[...].astype(low)
    copies[3].wait()
    turned_ref[...] = out_buf[...].T.astype(low)


def small_unpack_kernel(cols, at_ref, small_ref, vec_ref, qv_ref, bias_ref):
    devices = small_ref.shape[0]
    ends = bias_ref.shape[1] * 4 // devices
    share = devices // 4
    vec_ref[...] = jnp.concatenate([small_ref[j, :, :cols] for j in range(devices)], axis=1)
    mine = [small_ref[at_ref[1] * share + j] for j in range(share)]
    qv_ref[...] = jnp.concatenate([tile[:, :cols] for tile in mine], axis=1)
    bias_ref[...] = jnp.concatenate([tile[0:1, 128 - ends :] for tile in mine], axis=1)


def add_kernel(at_ref, left_ref, right_ref, out_ref):
    out_ref[...] = (left_ref[...].astype(wide) + right_ref[...].astype(wide)).astype(out_ref.dtype)


def quad_kernel(at_ref, keep_ref, got_ref, *out_refs):
    for j, ref in enumerate(out_refs):
        ref[...] = (keep_ref[j].astype(wide) + got_ref[j].astype(wide)).astype(ref.dtype)


def ranks_kernel(at_ref, *refs):
    parts, out_refs = refs[:-4], refs[-4:]
    width = out_refs[0].shape[1]
    total = sum(ref[...].astype(wide) for ref in parts)
    height = total.shape[0]
    for j, ref in enumerate(out_refs):
        ref[0:height, :] = total[:, j * width : (j + 1) * width].astype(low)
        if ref.shape[0] > height:
            small = total[0:16, 4 * width : 4 * width + 96]
            cols = 96 // 4
            vec = jnp.zeros((16, cols), wide)
            bias = jnp.zeros((1, 96), wide)
            for other in range(4):
                here = ((at_ref[1] ^ j) == other).astype(wide)
                vec += small[:, other * cols : (other + 1) * cols] * here
                bias += small[8 + other : 9 + other, :] * here
            ref[height:, :] = jnp.concatenate(
                [vec, jnp.zeros((16, width - cols - 96), wide), jnp.broadcast_to(bias, (16, 96))], axis=1
            ).astype(low)


def last_kernel(at_ref, *refs):
    parts, ins, outs, bufs, out_sems = refs[:4], refs[4:13], refs[13:22], refs[22:31], refs[31]
    total = sum(ref[...].astype(wide) for ref in parts)
    height, cols, ends = bufs[0].shape[1], bufs[3].shape[1], bufs[6].shape[1]
    small = total[height : height + 8]
    grads = (total[0:height].T, small[:, :cols], small[0:1, total.shape[1] - ends :])
    states = []
    for j, (rate, decay) in enumerate(((0.3, 0.1), (0.5, 0.0), (0.7, 0.0))):
        weight, first, second = (ref[...] for ref in ins[3 * j : 3 * j + 3])
        states += adamw(weight, grads[j], first, second, rate, decay)
    stored(states, bufs, outs, out_sems)


def output_kernel(at_ref, own_ref, vec_ref, one_ref, two_ref, three_ref, out_ref):
    total = one_ref[...].astype(wide) + two_ref[...].astype(wide) + three_ref[...].astype(wide)
    out_ref[...] = (own_ref[0] + total + vec_ref[7:8, :]).astype(low)


def sums_pack_kernel(cols, ends, at_ref, one_ref, two_ref, qv_ref, gbo_ref, gub_ref, out_ref):
    devices = out_ref.shape[0]
    share = devices // 4
    middle = jnp.zeros((8, 128 - cols - ends), wide)
    for j in range(devices):
        span = slice(j * cols, (j + 1) * cols)
        mine = (at_ref[1] == j // share).astype(wide)
        k = j % share
        rows = [
            one_ref[0:2, span],
            two_ref[0:2, span],
            qv_ref[0:2, k * cols : (k + 1) * cols] * mine,
            gbo_ref[0:1, span],
            two_ref[2:3, span],
        ]
        bias = gub_ref[0:1, k * ends : (k + 1) * ends] * mine
        out_ref[j] = jnp.concatenate(
            [jnp.concatenate(rows, axis=0), middle, jnp.broadcast_to(bias, (8, ends))], axis=1
        )


def stored(values, bufs, refs, sems):
    for value, buf in zip(values, bufs):
        buf[...] = value
    for copy in fetch(list(zip(bufs, refs)), sems):
        copy.wait()


def small_adam_kernel(at_ref, got_ref, *refs):
    ins, outs, bufs, in_sems, out_sems = refs[:6], refs[6:12], refs[12:18], refs[18], refs[19]
    copies = fetch(list(zip(ins, bufs)), in_sems)
    total = jnp.sum(got_ref[...], axis=0)
    for copy in copies:
        copy.wait()
    cols, ends = bufs[0].shape[1], bufs[3].shape[1]
    vectors, biases = [buf[...] for buf in bufs[:3]], [buf[...] for buf in bufs[3:]]
    states = adamw(vectors[0], total[:, :cols], vectors[1], vectors[2], 0.5, 0.0)
    states += adamw(biases[0], total[0:1, 128 - ends :], biases[1], biases[2], 0.7, 0.0)
    stored(states, bufs, outs, out_sems)


def adam_kernel(n_parts, turned, rates, at_ref, *refs):
    count = len(rates)
    parts, refs = refs[: n_parts * count], refs[n_parts * count :]
    ins, outs, bufs = refs[: 3 * count], refs[3 * count : 6 * count], refs[6 * count : 9 * count]
    in_sems, out_sems = refs[9 * count :]
    copies = fetch(list(zip(ins, bufs)), in_sems)
    states = []
    for j, (rate, decay) in enumerate(rates):
        total = sum(ref[...].astype(wide) for ref in parts[j * n_parts : (j + 1) * n_parts])
        if turned:
            total = total.T
        for copy in copies[3 * j : 3 * j + 3]:
            copy.wait()
        weight, first, second = (buf[...] for buf in bufs[3 * j : 3 * j + 3])
        states += adamw(weight, total, first, second, rate, decay)
    stored(states, bufs, outs, out_sems)


def weights_kernel(at_ref, up_ref, down_ref, *refs):
    parts, (out_ref, up_buf, down_buf, sems) = refs[:4], refs[4:]
    copies = fetch([(up_ref, up_buf), (down_ref, down_buf)], sems)
    out_ref[2] = jnp.concatenate([ref[...] for ref in parts], axis=1)
    copies[0].wait()
    out_ref[0] = up_buf[...].astype(low)
    copies[1].wait()
    out_ref[1] = down_buf[...].astype(low)


def attend_kernel(n_parts, at_ref, x_ref, vec_ref, qv_ref, *refs):
    parts = refs[:n_parts]
    a1_ref, qkv_ref, lse_ref, o_ref, w_ref, ot_ref, sems = refs[n_parts:]
    copies = place_rows(at_ref, parts, w_ref, sems)
    normed, _ = norm_parts(x_ref[...].astype(wide))
    a1 = (normed * vec_ref[0:1, :] + vec_ref[1:2, :]).astype(low)
    a1_ref[...] = a1
    for copy in copies:
        copy.wait()
    q = ((dot(a1, w_ref[0]) + qv_ref[4:5, :]) * score_scale).astype(low)
    k = dot(a1, w_ref[1]).astype(low)
    v = (dot(a1, w_ref[2]) + qv_ref[5:6, :]).astype(low)
    qkv_ref[0] = q
    qkv_ref[1] = k
    qkv_ref[2] = v
    vt = v.T
    for head in range(q.shape[1] // HD):
        cols = slice(head * HD, (head + 1) * HD)
        scores = dot(k[:, cols], q[:, cols], NT)
        top = jnp.max(scores, axis=0, keepdims=True)
        expos = jnp.exp(scores - top)
        summed = jnp.sum(expos, axis=0, keepdims=True)
        lse_ref[head : head + 1, :] = top + jnp.log(summed)
        ot_ref[cols, :] = dot(vt[cols, :], expos.astype(low)) / summed
    o = ot_ref[...].T.astype(low)
    head_part, side_part = pack_heads(o)
    rows = o.shape[0]
    o_ref[0:rows, :] = head_part
    o_ref[rows:, :] = side_part


def ready_kernel(at_ref, c_ref, *refs):
    parts, (w_ref, dg_ref, sems) = refs[:-3], refs[-3:]
    for copy in place_rows(at_ref, parts, w_ref, sems):
        copy.wait()
    dg_ref[...] = dot(c_ref[...], w_ref[1])


def mlp_kernel(at_ref, x_ref, c_ref, vec_ref, ub_ref, w_ref, dg_ref, *refs):
    heads, dn2_refs = refs[:4], refs[4:8]
    a2_ref, g_ref, du_ref, own_ref, stat_ref, sums_ref, gub_ref, oo_ref, h_ref, n_ref, s_ref, o_ref = refs[8:]
    part_rows = dn2_refs[0].shape[0]
    o_ref[...] = jnp.concatenate([unpack_heads(ref[...]) for ref in heads], axis=1)
    hidden_state = x_ref[...].astype(wide) + dot(o_ref[...], w_ref[2], NT) + vec_ref[6:7, :]
    h_ref[...] = hidden_state
    normed, inverse = norm_parts(hidden_state)
    n_ref[...] = normed
    s_ref[...] = jnp.broadcast_to(inverse, s_ref.shape)
    a2 = (normed * vec_ref[2:3, :] + vec_ref[3:4, :]).astype(low)
    a2_ref[...] = a2
    pre = dot(a2, w_ref[0]) + ub_ref[...]
    square = pre * pre
    tangent = jnp.tanh(pre * (gelu_coef + (0.044715 * gelu_coef) * square))
    half = 0.5 + 0.5 * tangent
    active = pre * half
    g_ref[...] = active.astype(low)
    slope = half + active * (1.0 - half) * (2.0 * gelu_coef + (6.0 * 0.044715 * gelu_coef) * square)
    du = (dg_ref[...] * slope).astype(low)
    du_ref[...] = du
    gub_ref[...] = jnp.sum(du.astype(wide), axis=0, keepdims=True)
    own = rank_rows(at_ref, 0, part_rows)
    own_ref[0] = h_ref[own, :]
    own_ref[1] = n_ref[own, :]
    stat_ref[...] = s_ref[own, :]
    oo_ref[...] = o_ref[own, :]
    dn2 = dot(du, w_ref[0], NT)
    h_ref[...] = dn2
    sums_ref[0:1, :] = jnp.sum(dn2 * normed, axis=0, keepdims=True)
    sums_ref[1:2, :] = jnp.sum(dn2, axis=0, keepdims=True)
    for j, ref in enumerate(dn2_refs):
        ref[...] = h_ref[rank_rows(at_ref, j, part_rows), :].astype(low)
    sums_ref[2:3, :] = jnp.sum(c_ref[own, :].astype(wide), axis=0, keepdims=True)


def mlp_out_kernel(at_ref, g_ref, w_ref, *refs):
    slots, out_ref = refs[:4], refs[4]
    out_ref[...] = dot(g_ref[...], w_ref[1], NT)
    for j, ref in enumerate(slots):
        ref[...] = out_ref[rank_rows(at_ref, j, ref.shape[0]), :].astype(low)


def mix_kernel(at_ref, own_ref, stat_ref, c_ref, vec_ref, w_ref, *refs):
    chunks = refs[:3]
    dh_ref, dz_ref, gbo_ref = refs[3:6]
    do_refs = refs[6:]
    part_rows = stat_ref.shape[0]
    grad = sum(ref[...].astype(wide) for ref in chunks)
    cotan = c_ref[rank_rows(at_ref, 0, part_rows), :].astype(wide)
    dh = cotan + norm_backward(grad, own_ref[1], stat_ref[:, 0:1], vec_ref[2:3, :])
    dh_ref[...] = dh
    gbo_ref[...] = jnp.sum(dh, axis=0, keepdims=True)
    dz = dh.astype(low)
    dz_ref[...] = dz
    do = dot(dz, w_ref[2]).astype(low)
    heads_width = do.shape[1] // 4
    for j, ref in enumerate(do_refs):
        head_part, side_part = pack_heads(do[:, j * heads_width : (j + 1) * heads_width])
        ref[0:part_rows, :] = head_part
        ref[part_rows:, :] = side_part


def attend_back_kernel(fast, at_ref, x_ref, a1_ref, qkv_ref, lse_ref, w_ref, *refs):
    if fast:
        (two_ref, gbo_ref, gub_ref), refs = refs[:3], refs[3:]
    chunks, dn1_refs = refs[:4], refs[4:8]
    grad_refs, (sums_ref, qvsum_ref) = refs[8:-7], refs[-7:-5]
    do_ref, dqt_ref, d_ref, g_ref, dn1_ref = refs[-5:]
    rows, width = x_ref.shape
    part_rows = rows // 4
    for j in range(4):
        do_ref[rank_rows(at_ref, j, part_rows), :] = unpack_heads(chunks[j][...])
    q, k, v, do = qkv_ref[0], qkv_ref[1], qkv_ref[2], do_ref[...]
    kt = k.T
    heads_width = q.shape[1]
    for head in range(q.shape[1] // HD):
        cols = slice(head * HD, (head + 1) * HD)
        scores = dot(k[:, cols], q[:, cols], NT)
        probs = jnp.exp(scores - lse_ref[head : head + 1, :])
        grad_probs = dot(v[:, cols], do[:, cols], NT)
        d_ref[:, 2 * heads_width + head * HD : 2 * heads_width + (head + 1) * HD] = dot(
            probs.astype(low), do[:, cols]
        ).astype(low)
        both = probs * grad_probs
        grad_scores = (both - probs * jnp.sum(both, axis=0, keepdims=True)).astype(low)
        d_ref[:, heads_width + head * HD : heads_width + (head + 1) * HD] = dot(
            grad_scores, q[:, cols]
        ).astype(low)
        dqt_ref[cols, :] = dot(kt[cols, :], grad_scores) * score_scale
    d_ref[:, :heads_width] = dqt_ref[...].T.astype(low)
    dq, dk, dv = (d_ref[:, j * heads_width : (j + 1) * heads_width] for j in range(3))
    qvsum_ref[0:1, :] = jnp.sum(dq.astype(wide), axis=0, keepdims=True)
    qvsum_ref[1:2, :] = jnp.sum(dv.astype(wide), axis=0, keepdims=True)
    dn1 = dot(dq, w_ref[0], NT) + dot(dk, w_ref[1], NT) + dot(dv, w_ref[2], NT)
    dn1_ref[...] = dn1
    for j, ref in enumerate(dn1_refs):
        ref[...] = dn1_ref[rank_rows(at_ref, j, part_rows), :].astype(low)
    normed, _ = norm_parts(x_ref[...].astype(wide))
    sums_ref[0:1, :] = jnp.sum(dn1 * normed, axis=0, keepdims=True)
    sums_ref[1:2, :] = jnp.sum(dn1, axis=0, keepdims=True)
    g_ref[:, g_ref.shape[1] - 3 * heads_width :] = dot(a1_ref[...].T, d_ref[...]).astype(low)
    if not fast:
        grad_refs[0][...] = g_ref[...]
        return
    height = width // 8
    ends = gub_ref.shape[1] // 8
    for j in range(8):
        span, half = slice(j * height, (j + 1) * height), j % 2
        here = (at_ref[1] == j // 2).astype(wide)
        rows_in = [
            sums_ref[0:2, span],
            two_ref[0:2, span],
            qvsum_ref[0:2, half * height : (half + 1) * height] * here,
            gbo_ref[0:1, span],
            two_ref[2:3, span],
        ]
        rows_in += [gub_ref[0:1, (4 * half + k) * ends : (4 * half + k + 1) * ends] * here for k in range(4)]
        rows_in += [jnp.zeros((4, height), wide)]
        small = jnp.concatenate(rows_in, axis=0)
        g_ref[j * height : j * height + 16, 0:128] = jnp.concatenate(
            [small, jnp.zeros((16, 128 - height), wide)], axis=1
        ).astype(low)
    cut_blocks(at_ref, g_ref, *grad_refs)


def cut_blocks(at_ref, source, keep_refs, send_refs):
    height = source.shape[0] // 8
    for slot in range(4):
        keep_refs[slot] = take_rows(at_ref, source, 2 * slot, height)
        send_refs[slot] = take_rows(at_ref, source, 2 * slot + 1, height)


def weight_grad_kernel(at_ref, left_ref, right_ref, out_ref):
    out_ref[...] = dot(left_ref[...].T, right_ref[...]).astype(low)


def out_grad_kernel(at_ref, left_ref, right_ref, keep_ref, send_ref, grad_ref):
    grad_ref[...] = dot(left_ref[...].T, right_ref[...]).astype(low)
    cut_blocks(at_ref, grad_ref, keep_ref, send_ref)


def pair_quad_kernel(at_ref, keep_ref, got_ref, more_keep_ref, more_got_ref, *out_refs):
    first = keep_ref.shape[2]
    for j, ref in enumerate(out_refs):
        ref[:, :first] = (keep_ref[j].astype(wide) + got_ref[j].astype(wide)).astype(ref.dtype)
        ref[:, first:] = (more_keep_ref[j].astype(wide) + more_got_ref[j].astype(wide)).astype(ref.dtype)


def mlp_grad_kernel(at_ref, a2_ref, du_ref, c_ref, g_ref, keep_ref, send_ref, grad_ref):
    for j, (left, right) in enumerate(((a2_ref, du_ref), (c_ref, g_ref))):
        grad_ref[j] = dot(left[...].T, right[...]).astype(low)
        cut_blocks(at_ref, grad_ref.at[j], keep_ref.at[:, j], send_ref.at[:, j])


def input_kernel(at_ref, x_ref, dh_ref, vec_ref, *refs):
    count = (len(refs) - 4) // 2 if len(refs) > 4 else 0
    chunks, ins, out_ref, outs = refs[:3], refs[3 : 3 + count], refs[3 + count], refs[4 + count : 4 + 2 * count]
    copies = fetch(list(zip(ins, outs)), refs[-1]) if count else []
    part_rows = dh_ref.shape[0]
    normed, inverse = norm_parts(x_ref[rank_rows(at_ref, 0, part_rows), :].astype(wide))
    grad = sum(ref[...].astype(wide) for ref in chunks)
    out_ref[...] = dh_ref[...] + norm_backward(grad, normed, inverse, vec_ref[0:1, :])
    for copy in copies:
        copy.wait()


def adamw(weight, gradient, first, second, rate, decay):
    first_new = beta_one * first + (1.0 - beta_one) * gradient
    second_new = beta_two * second + (1.0 - beta_two) * gradient * gradient
    first_hat = first_new / (1.0 - beta_one**STEP)
    second_hat = second_new / (1.0 - beta_two**STEP)
    weight_new = weight - rate * (first_hat / (jnp.sqrt(second_hat) + adam_eps) + decay * weight)
    return (weight_new, first_new, second_new)


def body(
    images,
    cotangent,
    qkv_weight,
    out_weight,
    up_weight,
    down_weight,
    vectors,
    up_bias,
    qkv_first,
    qkv_second,
    out_first,
    out_second,
    up_first,
    up_second,
    down_first,
    down_second,
    vector_first,
    vector_second,
    bias_first,
    bias_second,
):
    fsdp_size = lax.axis_size("fsdp")
    tensor_size = lax.axis_size("tensor")
    devices = fsdp_size * tensor_size
    fast = fsdp_size == 8
    at = jnp.stack([lax.axis_index("fsdp"), lax.axis_index("tensor")]).astype(jnp.int32)
    _, rows, width = images.shape
    hidden = up_weight.shape[1]
    heads_width = width // tensor_size
    part_rows = rows // tensor_size
    height = width // fsdp_size
    x = images.reshape(rows, width)
    c = cotangent.reshape(rows, width)
    cols, ends = vectors.shape[1], up_bias.shape[0]
    both_axes = ("fsdp", "tensor")

    tiles, qkv_low, out_t = kernel_call(
        first_kernel,
        [((devices, 8, 128), wide), (qkv_weight.shape, low), ((height, heads_width), low)],
        (at, vectors, up_bias[None], qkv_weight, out_weight),
        [
            pltpu.VMEM(vectors.shape, wide),
            pltpu.VMEM((1, ends), wide),
            pltpu.VMEM(qkv_weight.shape, wide),
            pltpu.VMEM(out_weight.shape, wide),
            pltpu.SemaphoreType.DMA((4,)),
        ],
        hbm=(1, 2, 3, 4),
    )
    small = lax.all_to_all(tiles, both_axes, 0, 0, tiled=True)
    vec, qv, up_local = kernel_call(
        functools.partial(small_unpack_kernel, cols),
        [((8, width), wide), ((8, heads_width), wide), ((1, hidden), wide)],
        (at, small),
    )

    if fast:
        chips = chips_of(qkv_low)
        qkv_parts = cores_of(chips)
    else:
        chips = qkv_parts = [lax.all_gather(qkv_low, "fsdp", axis=1, tiled=True)]
    (shard,) = kernel_call(
        weights_kernel,
        [((3, height, width), low)],
        (at, after(up_weight, chips[-1]), down_weight.T, *to_ranks([out_t] * 4)),
        [
            pltpu.VMEM(up_weight.shape, wide),
            pltpu.VMEM(up_weight.shape, wide),
            pltpu.SemaphoreType.DMA((2,)),
        ],
        hbm=(1, 2),
    )
    if fast:
        chips = chips_of(shard)

    n = len(qkv_parts)
    a1, qkv, lse, o_mine, qkv_full = kernel_call(
        functools.partial(attend_kernel, n),
        [
            ((rows, width), low),
            ((3, rows, heads_width), low),
            ((8, rows), wide),
            ((rows * 3 // 2, 128), low),
            ((3, width, heads_width), low),
        ],
        (at, x, vec, qv, *qkv_parts),
        [pltpu.VMEM((heads_width, rows), wide), pltpu.SemaphoreType.DMA((n,))],
        free=(4,), hbm=range(5, 4 + n),
    )
    o_parts = rank_gather(o_mine)
    if fast:
        chips = lax.optimization_barrier((*chips, o_parts[1], o_parts[2]))[:4]
        rest_parts = cores_of(chips)
    else:
        rest_parts = [lax.all_gather(shard, "fsdp", axis=1, tiled=True)]

    block = ((part_rows, width), low)
    w_full, dg = kernel_call(
        ready_kernel,
        [((3, width, width), low), ((rows, hidden), wide)],
        (at, c, *rest_parts),
        [pltpu.SemaphoreType.DMA((n,))],
        free=range(2, 2 + n),
    )
    *dn2, a2, g, du, own, stat, sums_two, gub, o_own = kernel_call(
        mlp_kernel,
        [
            *[block] * 4,
            ((rows, width), low),
            ((rows, hidden), low),
            ((rows, hidden), low),
            ((2, part_rows, width), wide),
            ((part_rows, 128), wide),
            ((8, width), wide),
            ((1, hidden), wide),
            block,
        ],
        (at, x, c, vec, up_local, w_full, dg, *o_parts),
        [
            pltpu.VMEM((rows, width), wide),
            pltpu.VMEM((rows, width), wide),
            pltpu.VMEM((rows, 128), wide),
            pltpu.VMEM((rows, width), low),
        ],
    )

    def over_cores(keep, send):
        cut = keep.shape[1:]
        return kernel_call(
            quad_kernel, [(cut, wide)] + [(cut, low)] * 3, (at, keep, flip(send, "fsdp", 1))
        )

    def over_chips(mine, *go):
        return [mine] + [flip(part, "fsdp", mask) for part, mask in zip(go, (2, 4, 6))]

    if fast:
        cut = (4, 2, height, hidden)
        keep, send = kernel_call(
            mlp_grad_kernel, [(cut, low)] * 2, (at, a2, du, c, g), [pltpu.VMEM((2, width, hidden), low)]
        )
        dn2_got, dn2_pair = rank_sum(at, dn2, keep, send)
        mlp_sums = over_chips(*over_cores(keep, after(send, dn2_pair)))
    else:
        (up_grad,) = kernel_call(weight_grad_kernel, [((width, hidden), low)], (at, a2, du))
        (down_grad,) = kernel_call(weight_grad_kernel, [((width, hidden), low)], (at, c, g))
        dn2_got, dn2_pair = rank_sum(at, dn2)
        mlp_sums = summed_on_arrival(jnp.stack([up_grad, down_grad]), 1)
    mlp = kernel_call(
        mlp_out_kernel,
        [block] * 4,
        (at, after(g, dn2_pair), w_full),
        [pltpu.VMEM((rows, width), wide)],
    )
    dn2_got = lax.optimization_barrier((dn2_got, mlp, mlp_sums))[0]
    dh, dz, gbo, *do = kernel_call(
        mix_kernel,
        [
            ((part_rows, width), wide),
            block,
            ((1, width), wide),
            *[((part_rows * 3 // 2, 128), low)] * 4,
        ],
        (at, own, stat, c, vec, w_full, *dn2_got),
    )
    do_got = to_ranks(do)
    if fast:
        out_grad = kernel_call(
            out_grad_kernel, [((4, height, width), low)] * 2, (at, dz, o_own), [pltpu.VMEM((width, width), low)]
        )
    else:
        out_grad = kernel_call(weight_grad_kernel, [((width, width), low)], (at, dz, o_own))

    def update(sums, weight, first, second, rate, decay):
        return adamw(weight, sum(part.astype(wide) for part in sums), first, second, rate, decay)

    mlp_sums = lax.optimization_barrier((mlp_sums, dz))[0]
    up_state = update([part[0] for part in mlp_sums], up_weight, up_first, up_second, 0.08, 0.1)
    down_state = update(
        [part[1] for part in mlp_sums], down_weight.T, down_first.T, down_second.T, 0.045, 0.1
    )
    mlp_three, mlp_one = flip(mlp[3], "tensor", 1), flip(mlp[1], "tensor", 1)
    (mlp_two,) = kernel_call(add_kernel, [block], (at, mlp[2], mlp_three))
    mlp_two = flip(mlp_two, "tensor", 2)
    do_got = lax.optimization_barrier((do_got, out_grad, mlp_one, mlp_two, up_state, down_state))[0]
    down_state = [value.T for value in down_state]

    lanes = 3 * heads_width + (128 if fast else 0)
    extra = (sums_two, gbo, gub) if fast else ()
    cut = (4, height, lanes)
    grads = [(cut, low)] * 2 if fast else [((width, lanes), low)]
    *dn1, sums_one, qv_sums = kernel_call(
        functools.partial(attend_back_kernel, fast),
        [*[block] * 4, *grads, ((8, width), wide), ((8, heads_width), wide)],
        (at, x, a1, qkv, lse, qkv_full, *extra, *do_got),
        [
            pltpu.VMEM((rows, heads_width), low),
            pltpu.VMEM((heads_width, rows), wide),
            pltpu.VMEM((rows, 3 * heads_width), low),
            pltpu.VMEM((width, lanes), low),
            pltpu.VMEM((rows, width), wide),
        ],
    )
    dn1, grads = dn1[:4], dn1[4:]

    if fast:
        full = (height, width + lanes)
        arrived = (out_grad[0], flip(out_grad[1], "fsdp", 1), grads[0], flip(grads[1], "fsdp", 1))
        sums = kernel_call(pair_quad_kernel, [(full, wide)] + [(full, low)] * 3, (at, *arrived))
        dn1_got, dn1_pair = rank_sum(at, dn1, *sums)
        sums = over_chips(*sums)
    else:
        dn1_got, dn1_pair = rank_sum(at, dn1)
        sums = summed_on_arrival(jnp.concatenate([out_grad[0], grads[0]], axis=1), 0)

    (output,) = kernel_call(output_kernel, [block], (at, after(own, dn1_pair), vec, mlp[0], mlp_one, mlp_two))
    lanes += width
    qkv_sums = [
        jnp.stack([part[:, lanes - j * heads_width : lanes - (j - 1) * heads_width] for j in (3, 2, 1)]) for part in sums
    ]
    qkv_state = update(qkv_sums, qkv_weight, qkv_first, qkv_second, 0.08, 0.1)

    tall = height + (16 if fast else 0)
    out_sums = to_ranks(kernel_call(ranks_kernel, [((tall, heads_width), low)] * 4, (at, *sums)))
    out_state = (out_weight, out_first, out_second)
    small_state = (vectors, vector_first, vector_second, up_bias[None], bias_first[None], bias_second[None])
    dn1_got = lax.optimization_barrier((dn1_got, output, qkv_state))[0]
    states = out_state + small_state if fast else ()
    input_own, *brought = kernel_call(
        input_kernel,
        [((part_rows, width), wide)] + [(value.shape, wide) for value in states],
        (at, x, dh, vec, *dn1_got, *states),
        [pltpu.SemaphoreType.DMA((9,))] if fast else [],
        hbm=range(7, 7 + len(states)),
    )
    if fast:
        *last, bias_new, bias_m, bias_s = kernel_call(
            last_kernel,
            [(value.shape, wide) for value in states],
            (at, *out_sums, *brought),
            [pltpu.VMEM(value.shape, wide) for value in states] + [pltpu.SemaphoreType.DMA((9,))],
            hbm_outs=True,
        )
        out_state, vec_state = last[:3], last[3:]
    else:
        (tiles,) = kernel_call(
            functools.partial(sums_pack_kernel, cols, ends),
            [((devices, 8, 128), wide)],
            (at, sums_one, sums_two, qv_sums, gbo, gub),
        )
        tiles = lax.all_to_all(tiles, both_axes, 0, 0, tiled=True)
        *vec_state, bias_new, bias_m, bias_s = kernel_call(
            small_adam_kernel,
            [(value.shape, wide) for value in small_state],
            (at, tiles, *small_state),
            [pltpu.VMEM(value.shape, wide) for value in small_state] + [pltpu.SemaphoreType.DMA((6,))] * 2,
            hbm=range(2, 8),
            hbm_outs=True,
        )
        out_state = kernel_call(
            functools.partial(adam_kernel, 4, True, ((0.3, 0.1),)),
            [(value.shape, wide) for value in out_state],
            (at, *out_sums, *out_state),
            [pltpu.VMEM(value.shape, wide) for value in out_state] + [pltpu.SemaphoreType.DMA((3,))] * 2,
            hbm=range(5, 8),
            hbm_outs=True,
        )

    return (
        output[None],
        input_own[None],
        *qkv_state,
        *out_state,
        *up_state,
        *down_state,
        *vec_state,
        bias_new[0],
        bias_m[0],
        bias_s[0],
    )


def solution(mesh):
    weights = (P(None, "fsdp", "tensor"), P("tensor", "fsdp"), P("fsdp", "tensor"), P("tensor", "fsdp"))
    vector, bias = P(None, ("fsdp", "tensor")), P(("fsdp", "tensor"))
    twice = [spec for spec in (*weights, vector, bias) for _ in range(2)]
    thrice = [spec for spec in (*weights, vector, bias) for _ in range(3)]
    return jax.shard_map(
        body,
        mesh=mesh,
        in_specs=(P("fsdp", None, None), P("fsdp", None, None), *weights, vector, bias, *twice),
        out_specs=(P("fsdp", "tensor", None), P("fsdp", "tensor", None), *thrice),
        check_vma=False,
    )
```
